128 devices in a mesh: ctx: 32 (over y, z, x_lo), wa: 4 (over x_hi, core).
Axes of the slice: x: 4 (x_hi: 2, x_lo: 2; x = x_hi * 2 + x_lo), y: 4, z: 4, core: 2. Of those that a mesh axis runs over, the one named last changes fastest.
Arguments:
- inputs: bfloat16 [4, 6144, 1024], P('wa', 'ctx'), may hold values from -6 to 6
- first_gain: bfloat16 [1024], P('wa'), may hold values from 0.5 to 1.5
- first_bias: bfloat16 [1024], P('wa'), may hold values from -1.796875 to 1.796875
- second_gain: bfloat16 [1024], P('wa'), may hold values from 0.5 to 1.5
- second_bias: bfloat16 [1024], P('wa'), may hold values from -1.796875 to 1.796875
- mix_weight: bfloat16 [1024, 3072], P('wa'), may hold values from -0.1875 to 0.1875
- mix_bias: bfloat16 [3072], P('wa'), may hold values from -1.796875 to 1.796875
- dense_weight: bfloat16 [1024, 1024], P('wa'), may hold values from -1.5 to 1.5
- dense_bias: bfloat16 [1024], P('wa'), may hold values from -1.796875 to 1.796875
- up_weight: bfloat16 [1024, 4096], P('wa'), may hold values from -0.1875 to 0.1875
- up_bias: bfloat16 [4096], P('wa'), may hold values from -1.796875 to 1.796875
- down_weight: bfloat16 [4096, 1024], P('wa'), may hold values from -0.09375 to 0.09375
- down_bias: bfloat16 [1024], P('wa'), may hold values from -1.796875 to 1.796875
- grad_out: bfloat16 [4, 6144, 1024], P('wa', 'ctx'), may hold values from -6 to 6
Outputs:
- output: bfloat16 [4, 6144, 1024], P('wa', 'ctx')
- grad_inputs: bfloat16 [4, 6144, 1024], P('wa', 'ctx')
- grad_first_gain: float32 [1024], P('wa')
- grad_first_bias: float32 [1024], P('wa')
- grad_second_gain: float32 [1024], P('wa')
- grad_second_bias: float32 [1024], P('wa')
- grad_mix_weight: float32 [1024, 3072], P('wa')
- grad_mix_bias: float32 [3072], P('wa')
- grad_dense_weight: float32 [1024, 1024], P('wa')
- grad_dense_bias: float32 [1024], P('wa')
- grad_up_weight: float32 [1024, 4096], P('wa')
- grad_up_bias: float32 [4096], P('wa')
- grad_down_weight: float32 [4096, 1024], P('wa')
- grad_down_bias: float32 [1024], P('wa')
The draws below stay inside these ranges and needn't reach their ends.
All inputs are finite; a program needn't handle non-finite values.
Results may differ from the reference program's by a relative error of at most 0.025.
Values may be sent and summed in bfloat16 or wider, within the bound.
No kernel may reach another device: no remote copies, remote signals or barrier semaphores. Data moves between devices by JAX's collectives and lax.ppermute only.
A program may use at most 384 MiB of HBM per device.

```python
import math
import jax
import jax.numpy as jnp
from jax import lax

D = 1024
HEADS = 16
FF = 4096
HDIM = 64
ROT = 16
SEQS = 4
LEN = 6144


def block_scale(own_key, shape, cuts, low, largest):
    loudness = 1.0
    for dim, parts in cuts:
        heights = jax.random.uniform(jax.random.fold_in(jax.random.fold_in(own_key, 6), dim), (parts,), jnp.float32, low / len(cuts), largest / len(cuts))
        loudness = loudness * jnp.repeat(jnp.exp(heights), shape[dim] // parts).reshape((-1,) + (1,) * (len(shape) - 1 - dim))
    return loudness


def normal_values(stream_key, shape, deviation, reach, shards=(), held_as=jnp.bfloat16):
    gain = block_scale(stream_key, shape, shards, -0.22, 0.18) if shards else 1.0
    entries = jax.random.normal(stream_key, shape, jnp.float32) * deviation * gain
    return jnp.minimum(jnp.maximum(entries, -reach), reach).astype(held_as)


def setup_inputs(seed: int = 0) -> dict:
    keys = jax.random.split(jax.random.key(seed), 15)
    inputs = normal_values(keys[0], (SEQS, LEN, D), 1.0, 6.0, ((0, 4), (1, 32)))
    first_gain = jnp.clip(1.0 + 0.1 * jax.random.normal(keys[1], (D,), jnp.float32), 0.5, 1.5).astype(jnp.bfloat16)
    first_bias = normal_values(keys[2], (D,), 0.3, 1.796875, ((0, 4),))
    second_gain = jnp.clip(1.0 + 0.1 * jax.random.normal(keys[3], (D,), jnp.float32), 0.5, 1.5).astype(jnp.bfloat16)
    second_bias = normal_values(keys[4], (D,), 0.3, 1.796875, ((0, 4),))
    mix_weight = normal_values(keys[5], (D, 3 * D), D ** -0.5, 0.1875, ((0, 4),))
    mix_bias = normal_values(keys[6], (3 * D,), 0.3, 1.796875, ((0, 4),))
    dense_weight = normal_values(keys[7], (D, D), (D // 64) ** -0.5, 1.5, ((0, 4),))
    dense_bias = normal_values(keys[8], (D,), 0.3, 1.796875, ((0, 4),))
    up_weight = normal_values(keys[9], (D, FF), D ** -0.5, 0.1875, ((0, 4),))
    up_bias = normal_values(keys[10], (FF,), 0.3, 1.796875, ((0, 4),))
    down_weight = normal_values(keys[11], (FF, D), FF ** -0.5, 0.09375, ((0, 4),))
    down_bias = normal_values(keys[12], (D,), 0.3, 1.796875, ((0, 4),))
    grad_out = normal_values(keys[13], (SEQS, LEN, D), 1.0, 6.0, ((0, 4), (1, 32)))
    return dict(inputs=inputs, first_gain=first_gain, first_bias=first_bias, second_gain=second_gain, second_bias=second_bias, mix_weight=mix_weight, mix_bias=mix_bias, dense_weight=dense_weight, dense_bias=dense_bias, up_weight=up_weight, up_bias=up_bias, down_weight=down_weight, down_bias=down_bias, grad_out=grad_out)


highest = lax.Precision.HIGHEST
epsilon = 1e-05

@jax.custom_vjp
def low(v):
    return lax.optimization_barrier(v.astype(jnp.bfloat16)).astype(jnp.float32)

@jax.custom_vjp
def low_back(v):
    return v

def low_keep(v):
    return (low(v), None)

def low_pass(kept, grad):
    return (grad,)

def back_keep(v):
    return (v, None)

def back_low(kept, grad):
    return (low(grad),)
low.defvjp(low_keep, low_pass)
low_back.defvjp(back_keep, back_low)

def both_ways(values):
    return low(low_back(values))

def layer_norm(values, scale_vec, shift_vec):
    centre = lax.optimization_barrier(jnp.mean(values, -1, keepdims=True))
    centred = values - centre
    spread = lax.optimization_barrier(jnp.mean(centred * centred, -1, keepdims=True))
    return centred * lax.rsqrt(spread + epsilon) * scale_vec + shift_vec

def rotary_tables(positions):
    exponents = jnp.arange(0, ROT, 2, dtype=jnp.float32) / ROT
    inverse = 1.0 / 10000.0 ** exponents
    angles = positions[:, None] * inverse[None, :]
    doubled = jnp.concatenate([angles, angles], -1)
    return (jnp.cos(doubled), jnp.sin(doubled))

def rotate(values, cos_table, sin_table):
    rot_width = cos_table.shape[-1]
    half_width = rot_width // 2
    rotary_part = values[..., :rot_width]
    first_half = rotary_part[..., :half_width]
    second_half = rotary_part[..., half_width:]
    turned = jnp.concatenate([-second_half, first_half], -1)
    return jnp.concatenate([rotary_part * cos_table + turned * sin_table, values[..., rot_width:]], -1)

def attend_sequence(query_rows, key_rows, value_rows):
    total_len = query_rows.shape[0]
    block_len = math.gcd(512, total_len)
    key_pos = jnp.arange(total_len).astype(jnp.int32)
    score_scale = HDIM ** (-0.5)

    def one_block(block_index):
        first_row = (block_index * block_len).astype(jnp.int32)
        queries = lax.dynamic_slice_in_dim(query_rows, first_row, block_len, 0)
        scores = jnp.einsum('qhd,khd->hqk', queries, key_rows, precision=highest) * score_scale
        scores = low_back(scores)
        query_pos = first_row + jnp.arange(block_len).astype(jnp.int32)
        allowed = key_pos[None, :] <= query_pos[:, None]
        scores = jnp.where(allowed[None], scores, -1e+30)
        weights = jax.nn.softmax(scores, axis=-1)
        return jnp.einsum('hqk,khd->qhd', low(weights), value_rows, precision=highest)
    blocks = lax.map(jax.checkpoint(one_block), jnp.arange(total_len // block_len).astype(jnp.int32))
    return blocks.reshape(total_len, HEADS, HDIM)

def forward(inputs, first_gain, first_bias, second_gain, second_bias, mix_weight, mix_bias, dense_weight, dense_bias, up_weight, up_bias, down_weight, down_bias):
    flat_in = inputs.reshape(SEQS * LEN, D)
    norm_one = low(layer_norm(flat_in, first_gain, first_bias))
    norm_two = low(layer_norm(flat_in, second_gain, second_bias))
    mixed_rows = low_back(jnp.dot(norm_one, mix_weight, precision=highest) + mix_bias)
    mixed_rows = mixed_rows.reshape(SEQS, LEN, 3, HEADS, HDIM)
    cos_table, sin_table = rotary_tables(jnp.arange(LEN, dtype=jnp.float32))
    turned = low(rotate(mixed_rows[:, :, 0:2], cos_table[:, None, None, :], sin_table[:, None, None, :]))
    value_rows = low(mixed_rows[:, :, 2])
    heads_out = jax.vmap(attend_sequence)(turned[:, :, 0], turned[:, :, 1], value_rows)
    merged = both_ways(heads_out.reshape(SEQS * LEN, D))
    attention = jnp.dot(merged, dense_weight, precision=highest) + dense_bias
    up_pre = low_back(jnp.dot(norm_two, up_weight, precision=highest) + up_bias)
    hidden = low(jax.nn.gelu(up_pre, approximate=False))
    feed_out = jnp.dot(hidden, down_weight, precision=highest) + down_bias
    return (flat_in + attention + feed_out).reshape(SEQS, LEN, D)

def reference(inputs, first_gain, first_bias, second_gain, second_bias, mix_weight, mix_bias, dense_weight, dense_bias, up_weight, up_bias, down_weight, down_bias, grad_out):
    result, pullback = jax.vjp(forward, inputs.astype(jnp.float32), first_gain.astype(jnp.float32), first_bias.astype(jnp.float32), second_gain.astype(jnp.float32), second_bias.astype(jnp.float32), mix_weight.astype(jnp.float32), mix_bias.astype(jnp.float32), dense_weight.astype(jnp.float32), dense_bias.astype(jnp.float32), up_weight.astype(jnp.float32), up_bias.astype(jnp.float32), down_weight.astype(jnp.float32), down_bias.astype(jnp.float32))
    grads = pullback(grad_out.astype(jnp.float32))
    return (result.astype(jnp.bfloat16), grads[0].astype(jnp.bfloat16), grads[1], grads[2], grads[3], grads[4], grads[5], grads[6], grads[7], grads[8], grads[9], grads[10], grads[11], grads[12])
```

```python
import functools

import jax
import jax.numpy as jnp
from jax import lax
from jax.experimental import pallas as pl
from jax.experimental.pallas import tpu as pltpu
from jax.sharding import PartitionSpec as P

D = 1024
HEADS = 16
HDIM = 64
ROT = 16
FF = 4096
BLK = 192
HALF = 96
EPS = 1e-05
F32 = jnp.float32
BF16 = jnp.bfloat16


def attention_kernel(
    par_ref, x_ref, out_ref, kv, kvt, qd, s_buf, p_buf, dkv, oq, *, blocks, tq, kc
):
    n_keys, n_queries = blocks * BLK, blocks * HALF
    par = par_ref[0]

    def token(row):
        return (row // HALF) * BLK + par * HALF + row % HALF

    def fill(b, carry):
        kv[pl.ds(b * BLK, BLK), :] = x_ref[b, 0:BLK, :]
        qd[pl.ds(b * HALF, HALF), :] = x_ref[b, BLK : BLK + HALF, :]
        return carry

    lax.fori_loop(0, blocks, fill, 0)

    def turn(c, carry):
        kvt[:, pl.ds(pl.multiple_of(c * kc, kc), kc)] = kv[pl.ds(c * kc, kc), :].T
        dkv[pl.ds(c * kc, kc), :] = jnp.zeros((kc, 128), F32)
        return carry

    lax.fori_loop(0, n_keys // kc, turn, 0)
    row = lax.broadcasted_iota(jnp.int32, (128, tq), 0)
    lane = lax.broadcasted_iota(jnp.int32, (tq, 128), 1)
    q_col = lax.broadcasted_iota(jnp.int32, (kc, tq), 1)
    k_row = lax.broadcasted_iota(jnp.int32, (kc, tq), 0)
    zero = jnp.zeros((), F32)

    def group(t, carry):
        first = t * tq
        n_all = (token(first + tq - 1) + kc) // kc
        n_full = (token(first) + 1) // kc
        qd_rows = qd[pl.ds(pl.multiple_of(first, tq), tq), :]
        qd_t = qd_rows.astype(F32).T
        q_t = jnp.where(row < HDIM, qd_t * 0.125, zero).astype(BF16)
        q_idx = first + q_col
        q_tok = (q_idx // HALF) * BLK + par * HALF + q_idx % HALF

        def scores(c, top, masked):
            o = pl.multiple_of(c * kc, kc)
            s = jnp.dot(kv[pl.ds(o, kc), :], q_t, preferred_element_type=F32)
            if masked:
                s = jnp.where(c * kc + k_row <= q_tok, s, -1e30)
            s_buf[pl.ds(o, kc), :] = s
            return jnp.maximum(top, jnp.max(s.reshape(kc // 8, 8, tq), 0))

        top = jnp.full((8, tq), -1e30, F32)
        top = lax.fori_loop(0, n_full, lambda c, m: scores(c, m, False), top)
        top = lax.fori_loop(n_full, n_all, lambda c, m: scores(c, m, True), top)
        top = jnp.max(top, 0, keepdims=True)

        def weigh(c, state):
            total, out_t = state
            o = pl.multiple_of(c * kc, kc)
            p = jnp.exp(s_buf[pl.ds(o, kc), :] - top)
            total = total + jnp.sum(p.reshape(kc // 8, 8, tq), 0)
            p_low = p.astype(BF16)
            p_buf[pl.ds(o, kc), :] = p_low
            out_t = out_t + jnp.dot(kvt[HDIM:, pl.ds(o, kc)], p_low, preferred_element_type=F32)
            return total, out_t

        total, out_t = lax.fori_loop(
            0, n_all, weigh, (jnp.zeros((8, tq), F32), jnp.zeros((HDIM, tq), F32))
        )
        inv = 1.0 / jnp.sum(total, 0, keepdims=True)
        out_t = out_t * inv
        do_t = (qd_t[HDIM:] * inv).astype(BF16)
        delta = jnp.sum(do_t.astype(F32) * out_t, 0, keepdims=True)
        do_full = jnp.concatenate([jnp.zeros((HDIM, tq), BF16), do_t], 0)
        do_rows = do_full.astype(F32).T.astype(BF16)
        q_rows = jnp.where(lane < HDIM, qd_rows.astype(F32) * 0.125, zero).astype(BF16)

        def back(c, dq_t):
            o = pl.multiple_of(c * kc, kc)
            dp = jnp.dot(kv[pl.ds(o, kc), :], do_full, preferred_element_type=F32)
            p_low = p_buf[pl.ds(o, kc), :]
            ds = (p_low.astype(F32) * (dp - delta)).astype(BF16)
            dkv[pl.ds(o, kc), :] += jnp.dot(
                p_low, do_rows, preferred_element_type=F32
            ) + jnp.dot(ds, q_rows, preferred_element_type=F32)
            return dq_t + jnp.dot(kvt[:HDIM, pl.ds(o, kc)], ds, preferred_element_type=F32)

        dq_t = lax.fori_loop(0, n_all, back, jnp.zeros((HDIM, tq), F32)) * 0.125
        oq[pl.ds(pl.multiple_of(first, tq), tq), :] = (
            jnp.concatenate([dq_t, out_t], 0).T.astype(BF16)
        )
        return carry

    lax.fori_loop(0, n_queries // tq, group, 0)

    def drain(b, carry):
        out_ref[b, 0:BLK, :] = dkv[pl.ds(b * BLK, BLK), :].astype(BF16)
        out_ref[b, BLK : BLK + HALF, :] = oq[pl.ds(b * HALF, HALF), :]
        return carry

    lax.fori_loop(0, blocks, drain, 0)


def attention(par, x, tq=768, kc=1536):
    blocks = x.shape[0]
    n_keys, n_queries = blocks * BLK, blocks * HALF
    area = n_keys * n_queries // 2
    return pl.pallas_call(
        functools.partial(attention_kernel, blocks=blocks, tq=tq, kc=kc),
        out_shape=jax.ShapeDtypeStruct(x.shape, BF16),
        in_specs=[
            pl.BlockSpec(memory_space=pltpu.SMEM),
            pl.BlockSpec(memory_space=pltpu.VMEM),
        ],
        out_specs=pl.BlockSpec(memory_space=pltpu.VMEM),
        scratch_shapes=[
            pltpu.VMEM((n_keys, 128), BF16),
            pltpu.VMEM((128, n_keys), BF16),
            pltpu.VMEM((n_queries, 128), BF16),
            pltpu.VMEM((n_keys, tq), F32),
            pltpu.VMEM((n_keys, tq), BF16),
            pltpu.VMEM((n_keys, 128), F32),
            pltpu.VMEM((n_queries, 128), BF16),
        ],
        compiler_params=pltpu.CompilerParams(vmem_limit_bytes=50 * 2**20),
        cost_estimate=pl.CostEstimate(
            flops=12 * area * HDIM, bytes_accessed=4 * x.size, transcendentals=area
        ),
    )(par, x)


def normalize(values):
    centred = values - jnp.mean(values, -1, keepdims=True)
    spread = jnp.mean(centred * centred, -1, keepdims=True)
    inv = lax.rsqrt(spread + EPS)
    return centred * inv, inv


def norm_back(normal, inv, gain, grad):
    e = grad * gain
    return inv * (
        e
        - jnp.mean(e, -1, keepdims=True)
        - normal * jnp.mean(e * normal, -1, keepdims=True)
    )


def rotary_tables(positions):
    exponents = jnp.arange(0, ROT, 2, dtype=F32) / ROT
    inverse = 1.0 / 10000.0**exponents
    angles = positions[:, None] * inverse[None, :]
    doubled = jnp.concatenate([angles, angles], -1)
    return jnp.cos(doubled)[:, None, :], jnp.sin(doubled)[:, None, :]


def rotate(values, cos_table, sin_table):
    first = values[..., : ROT // 2]
    second = values[..., ROT // 2 : ROT]
    turned = jnp.concatenate([-second, first], -1)
    return jnp.concatenate(
        [values[..., :ROT] * cos_table + turned * sin_table, values[..., ROT:]], -1
    )


def gelu_exact(values):
    return jax.nn.gelu(values, approximate=False)


def dot(a, b):
    return jnp.dot(a, b, preferred_element_type=F32)


def dot_t(a, b):
    return lax.dot_general(a, b, (((1,), (1,)), ((), ())), preferred_element_type=F32)


def t_dot(a, b):
    return lax.dot_general(a, b, (((0,), (0,)), ((), ())), preferred_element_type=F32)


def by_quarter(vec):
    return vec.reshape(4, -1, 256).transpose(0, 2, 1).reshape(1024, -1)


def sum_over_blocks(part):
    columns = part.shape[1]
    pieces = part.reshape(16, 16, 2, columns // 2).transpose(0, 2, 1, 3)
    pieces = pieces.reshape(32, 16, columns // 2)
    mine = lax.all_to_all(pieces, "ctx", 0, 0, tiled=True)
    mine = jnp.sum(mine.astype(F32), 0).astype(BF16)
    spread = jnp.broadcast_to(mine[None], (32, *mine.shape))
    whole = lax.all_to_all(spread, "ctx", 0, 0, tiled=True)
    return (
        whole.reshape(16, 2, 16, columns // 2)
        .transpose(0, 2, 1, 3)
        .reshape(256, columns)
        .astype(F32)
    )


def shards(
    inputs,
    first_gain,
    first_bias,
    second_gain,
    second_bias,
    mix_weight,
    mix_bias,
    dense_weight,
    dense_bias,
    up_weight,
    up_bias,
    down_weight,
    down_bias,
    grad_out,
):
    small = jnp.concatenate(
        [first_gain, first_bias, second_gain, second_bias, dense_bias, down_bias, mix_bias, up_bias]
    )
    small = lax.all_gather(small, "wa", axis=0, tiled=False).astype(F32)
    vec = [small[:, 256 * i : 256 * i + 256].reshape(1, D) for i in range(6)]
    gain_one, shift_one, gain_two, shift_two, bias_dense, bias_down = vec
    bias_mix = small[:, 1536:2304].reshape(1, 3 * D)
    bias_up = small[:, 2304:3328].reshape(1, FF)
    attn_weight = lax.all_gather(
        jnp.concatenate([mix_weight, dense_weight], 1), "wa", axis=0, tiled=True
    )
    mix_full, dense_full = attn_weight[:, : 3 * D], attn_weight[:, 3 * D :]
    up_full = lax.all_gather(up_weight, "wa", axis=0, tiled=True)
    down_full = lax.all_gather(down_weight, "wa", axis=0, tiled=True)

    place = lax.axis_index("ctx")
    flat_in = inputs[0].astype(F32)
    upstream = grad_out[0]
    normal, inv = normalize(flat_in)
    norm_one = (normal * gain_one + shift_one).astype(BF16)
    norm_two = (normal * gain_two + shift_two).astype(BF16)
    mixed = (dot(norm_one, mix_full) + bias_mix).reshape(BLK, 3, HEADS, HDIM)
    positions = (place * BLK + jnp.arange(BLK, dtype=jnp.int32)).astype(F32)
    cos_table, sin_table = rotary_tables(positions)
    queries = rotate(mixed[:, 0], cos_table, sin_table).astype(BF16)
    keys = rotate(mixed[:, 1], cos_table, sin_table).astype(BF16)
    values = mixed[:, 2].astype(BF16)
    d_merged = dot_t(upstream, dense_full).astype(BF16).reshape(BLK, HEADS, HDIM)
    key_value = jnp.concatenate([keys, values], -1).transpose(1, 0, 2)
    key_value = jnp.broadcast_to(key_value[:, None], (HEADS, 2, BLK, 2 * HDIM))
    query_grad = jnp.concatenate([queries, d_merged], -1).transpose(1, 0, 2)
    query_grad = query_grad.reshape(HEADS, 2, HALF, 2 * HDIM)
    sent = jnp.concatenate([key_value, query_grad], 2).reshape(32, BLK + HALF, 2 * HDIM)
    held = lax.all_to_all(sent, "ctx", 0, 0, tiled=True)
    back = attention((place % 2).reshape(1), held)
    back = lax.all_to_all(back, "ctx", 0, 0, tiled=True)
    back = back.reshape(HEADS, 2, BLK + HALF, 2 * HDIM)
    d_key_value = jnp.sum(back[:, :, :BLK].astype(F32), 1).transpose(1, 0, 2)
    d_query_out = back[:, :, BLK:].reshape(HEADS, BLK, 2 * HDIM).transpose(1, 0, 2)
    merged = d_query_out[..., HDIM:].reshape(BLK, D)
    d_query = rotate(d_query_out[..., :HDIM].astype(F32), cos_table, -sin_table)
    d_key = rotate(d_key_value[..., :HDIM], cos_table, -sin_table)
    d_value = d_key_value[..., HDIM:]
    d_mixed = jnp.stack([d_query, d_key, d_value], 1).reshape(BLK, 3 * D).astype(BF16)

    up_pre = dot(norm_two, up_full) + bias_up
    hidden, gelu_back = jax.vjp(gelu_exact, up_pre)
    hidden = hidden.astype(BF16)
    d_pre = gelu_back(dot_t(upstream, down_full))[0].astype(BF16)
    d_norm_two = dot_t(d_pre, up_full)
    feed_out = dot(hidden, down_full) + bias_down
    attended = dot(merged, dense_full) + bias_dense
    output = (flat_in + attended + feed_out).astype(BF16)[None]
    d_norm_one = dot_t(d_mixed, mix_full)
    grad_in = (
        upstream.astype(F32)
        + norm_back(normal, inv, gain_one, d_norm_one)
        + norm_back(normal, inv, gain_two, d_norm_two)
    ).astype(BF16)[None]

    vectors = jnp.concatenate(
        [
            by_quarter(jnp.sum(v, 0))
            for v in (
                d_norm_one * normal,
                d_norm_one,
                d_norm_two * normal,
                d_norm_two,
                upstream.astype(F32),
                d_mixed.astype(F32),
                d_pre.astype(F32),
            )
        ],
        1,
    )
    vectors = jnp.pad(vectors, ((0, 0), (0, 256 - vectors.shape[1]))).astype(BF16)
    grad_up = t_dot(norm_two, d_pre).astype(BF16)
    grad_down = t_dot(hidden, upstream).astype(BF16)
    grad_attn = jnp.concatenate(
        [t_dot(norm_one, d_mixed).astype(BF16), t_dot(merged, upstream).astype(BF16), vectors], 1
    )

    def scatter(part):
        return lax.psum_scatter(part, "wa", scatter_dimension=0, tiled=True)

    sum_up = sum_over_blocks(scatter(grad_up))
    sum_down = sum_over_blocks(scatter(grad_down).reshape(256, 4096)).reshape(1024, 1024)
    sum_attn = sum_over_blocks(scatter(grad_attn))
    sum_mix, sum_dense = sum_attn[:, : 3 * D], sum_attn[:, 3 * D : 4 * D]
    rest = sum_attn[:, 4 * D : 4 * D + 12].T
    return (
        output,
        grad_in,
        rest[0],
        rest[1],
        rest[2],
        rest[3],
        sum_mix,
        rest[5:8].reshape(768),
        sum_dense,
        rest[4],
        sum_up,
        rest[8:12].reshape(1024),
        sum_down,
        rest[4],
    )


def solution(mesh):
    rows, vec, tokens = P("wa", None), P("wa"), P("wa", "ctx", None)
    return jax.shard_map(
        shards,
        mesh=mesh,
        in_specs=(tokens, vec, vec, vec, vec, rows, vec, rows, vec, rows, vec, rows, vec, tokens),
        out_specs=(
            tokens,
            tokens,
            vec,
            vec,
            vec,
            vec,
            rows,
            vec,
            rows,
            vec,
            rows,
            vec,
            rows,
            vec,
        ),
        check_vma=False,
    )
```

```python
import functools

import jax
import jax.numpy as jnp
from jax import lax
from jax.experimental import pallas as pl
from jax.experimental.pallas import tpu as pltpu
from jax.sharding import PartitionSpec as P

D = 1024
HEADS = 16
HDIM = 64
ROT = 16
FF = 4096
BLK = 192
HALF = 96
EPS = 1e-05
F32 = jnp.float32
BF16 = jnp.bfloat16


def attention_kernel(
    par_ref, x_ref, out_ref, kv, kvt, qd, s_buf, p_buf, dkv, oq, *, blocks, tq, kc
):
    n_keys, n_queries = blocks * BLK, blocks * HALF
    par = par_ref[0]

    def token(row):
        return (row // HALF) * BLK + par * HALF + row % HALF

    def fill(b, carry):
        kv[pl.ds(b * BLK, BLK), :] = x_ref[b, 0:BLK, :]
        qd[pl.ds(b * HALF, HALF), :] = x_ref[b, BLK : BLK + HALF, :]
        return carry

    lax.fori_loop(0, blocks, fill, 0)

    def turn(c, carry):
        kvt[:, pl.ds(pl.multiple_of(c * kc, kc), kc)] = kv[pl.ds(c * kc, kc), :].T
        dkv[pl.ds(c * kc, kc), :] = jnp.zeros((kc, 128), F32)
        return carry

    lax.fori_loop(0, n_keys // kc, turn, 0)
    row = lax.broadcasted_iota(jnp.int32, (128, tq), 0)
    lane = lax.broadcasted_iota(jnp.int32, (tq, 128), 1)
    q_col = lax.broadcasted_iota(jnp.int32, (kc, tq), 1)
    k_row = lax.broadcasted_iota(jnp.int32, (kc, tq), 0)
    zero = jnp.zeros((), F32)

    def group(t, carry):
        first = t * tq
        n_all = (token(first + tq - 1) + kc) // kc
        n_full = (token(first) + 1) // kc
        qd_rows = qd[pl.ds(pl.multiple_of(first, tq), tq), :]
        qd_t = qd_rows.astype(F32).T
        q_t = jnp.where(row < HDIM, qd_t * 0.125, zero).astype(BF16)
        q_idx = first + q_col
        q_tok = (q_idx // HALF) * BLK + par * HALF + q_idx % HALF

        def scores(c, top, masked):
            o = pl.multiple_of(c * kc, kc)
            s = jnp.dot(kv[pl.ds(o, kc), :], q_t, preferred_element_type=F32)
            if masked:
                s = jnp.where(c * kc + k_row <= q_tok, s, -1e30)
            s_buf[pl.ds(o, kc), :] = s
            return jnp.maximum(top, jnp.max(s.reshape(kc // 8, 8, tq), 0))

        top = jnp.full((8, tq), -1e30, F32)
        top = lax.fori_loop(0, n_full, lambda c, m: scores(c, m, False), top)
        top = lax.fori_loop(n_full, n_all, lambda c, m: scores(c, m, True), top)
        top = jnp.max(top, 0, keepdims=True)

        def weigh(c, state):
            total, out_t = state
            o = pl.multiple_of(c * kc, kc)
            p = jnp.exp(s_buf[pl.ds(o, kc), :] - top)
            total = total + jnp.sum(p.reshape(kc // 8, 8, tq), 0)
            p_low = p.astype(BF16)
            p_buf[pl.ds(o, kc), :] = p_low
            out_t = out_t + jnp.dot(kvt[HDIM:, pl.ds(o, kc)], p_low, preferred_element_type=F32)
            return total, out_t

        total, out_t = lax.fori_loop(
            0, n_all, weigh, (jnp.zeros((8, tq), F32), jnp.zeros((HDIM, tq), F32))
        )
        inv = 1.0 / jnp.sum(total, 0, keepdims=True)
        out_t = out_t * inv
        do_t = (qd_t[HDIM:] * inv).astype(BF16)
        delta = jnp.sum(do_t.astype(F32) * out_t, 0, keepdims=True)
        do_full = jnp.concatenate([jnp.zeros((HDIM, tq), BF16), do_t], 0)
        do_rows = do_full.astype(F32).T.astype(BF16)
        q_rows = jnp.where(lane < HDIM, qd_rows.astype(F32) * 0.125, zero).astype(BF16)

        def back(c, dq_t):
            o = pl.multiple_of(c * kc, kc)
            dp = jnp.dot(kv[pl.ds(o, kc), :], do_full, preferred_element_type=F32)
            p_low = p_buf[pl.ds(o, kc), :]
            ds = (p_low.astype(F32) * (dp - delta)).astype(BF16)
            dkv[pl.ds(o, kc), :] += jnp.dot(
                p_low, do_rows, preferred_element_type=F32
            ) + jnp.dot(ds, q_rows, preferred_element_type=F32)
            return dq_t + jnp.dot(kvt[:HDIM, pl.ds(o, kc)], ds, preferred_element_type=F32)

        dq_t = lax.fori_loop(0, n_all, back, jnp.zeros((HDIM, tq), F32)) * 0.125
        oq[pl.ds(pl.multiple_of(first, tq), tq), :] = (
            jnp.concatenate([dq_t, out_t], 0).T.astype(BF16)
        )
        return carry

    lax.fori_loop(0, n_queries // tq, group, 0)

    def drain(b, carry):
        out_ref[b, 0:BLK, :] = dkv[pl.ds(b * BLK, BLK), :].astype(BF16)
        out_ref[b, BLK : BLK + HALF, :] = oq[pl.ds(b * HALF, HALF), :]
        return carry

    lax.fori_loop(0, blocks, drain, 0)


def attention(par, x, tq=768, kc=1536):
    blocks = x.shape[0]
    n_keys, n_queries = blocks * BLK, blocks * HALF
    area = n_keys * n_queries // 2
    return pl.pallas_call(
        functools.partial(attention_kernel, blocks=blocks, tq=tq, kc=kc),
        out_shape=jax.ShapeDtypeStruct(x.shape, BF16),
        in_specs=[
            pl.BlockSpec(memory_space=pltpu.SMEM),
            pl.BlockSpec(memory_space=pltpu.VMEM),
        ],
        out_specs=pl.BlockSpec(memory_space=pltpu.VMEM),
        scratch_shapes=[
            pltpu.VMEM((n_keys, 128), BF16),
            pltpu.VMEM((128, n_keys), BF16),
            pltpu.VMEM((n_queries, 128), BF16),
            pltpu.VMEM((n_keys, tq), F32),
            pltpu.VMEM((n_keys, tq), BF16),
            pltpu.VMEM((n_keys, 128), F32),
            pltpu.VMEM((n_queries, 128), BF16),
        ],
        compiler_params=pltpu.CompilerParams(vmem_limit_bytes=50 * 2**20),
        cost_estimate=pl.CostEstimate(
            flops=12 * area * HDIM, bytes_accessed=4 * x.size, transcendentals=area
        ),
    )(par, x)


def normalize(values):
    centred = values - jnp.mean(values, -1, keepdims=True)
    spread = jnp.mean(centred * centred, -1, keepdims=True)
    inv = lax.rsqrt(spread + EPS)
    return centred * inv, inv


def norm_back(normal, inv, gain, grad):
    e = grad * gain
    return inv * (
        e
        - jnp.mean(e, -1, keepdims=True)
        - normal * jnp.mean(e * normal, -1, keepdims=True)
    )


def dot(a, b):
    return jnp.dot(a, b, preferred_element_type=F32)


def dot_t(a, b):
    return lax.dot_general(a, b, (((1,), (1,)), ((), ())), preferred_element_type=F32)


def t_dot(a, b):
    return lax.dot_general(a, b, (((0,), (0,)), ((), ())), preferred_element_type=F32)


AX = ("ctx", "wa")
YZ = [[2 * i + lo for i in range(16)] for lo in range(2)]
ANY = pl.BlockSpec(memory_space=pl.ANY)
VMEM = pl.BlockSpec(memory_space=pltpu.VMEM)
SMEM = pl.BlockSpec(memory_space=pltpu.SMEM)


def place_of(x, yz, core):
    return (yz * 2 + x % 2) * 4 + (x // 2) * 2 + core


def route(move):
    pairs = []
    for yz in range(16):
        for x in range(4):
            for c in range(2):
                to_x, to_c = move(x, c)
                pairs.append((place_of(x, yz, c), place_of(to_x, yz, to_c)))
    return pairs


RING = [route(lambda x, c, d=d: ((x + d) % 4, c)) for d in range(4)]
CORE = route(lambda x, c: (x, 1 - c))
CROSS = route(lambda x, c: (3 - x, c))
NEXT = route(lambda x, c: (x ^ 1, c))


def send(value, pairs):
    return lax.ppermute(value, AX, pairs)


def pick(array, index, axis=0):
    return lax.dynamic_index_in_dim(array, index, axis, keepdims=False)


def after(value, *first):
    return lax.optimization_barrier((value, *first))[0]


def ring_gather(own):
    return [own, send(own, RING[3]), send(own, RING[2]), send(own, RING[1])]


def swap(pieces):
    return lax.all_to_all(pieces, "ctx", 0, 0, axis_index_groups=YZ, tiled=True)


def params(mib):
    return pltpu.CompilerParams(vmem_limit_bytes=mib * 2**20)


def pack_kernel(at_ref, mix_ref, up_ref, small_ref, mix0, up0, mix1, up1):
    for k, (mix_out, up_out) in enumerate(((mix0, up0), (mix1, up1))):
        q = at_ref[k]
        for j in range(3):
            cols = pl.ds(pl.multiple_of(q * 256 + j * 1024, 256), 256)
            mix_out[0:256, 256 * j : 256 * j + 256] = mix_ref[:, cols]
        mix_out[256:272, 0:256] = small_ref[...]
        mix_out[256:272, 256:768] = jnp.zeros((16, 512), BF16)
        up_out[...] = up_ref[:, pl.ds(pl.multiple_of(q * 1024, 1024), 1024)]


def pack(at, mix_weight, up_weight, small):
    mix_shape = jax.ShapeDtypeStruct((272, 768), BF16)
    up_shape = jax.ShapeDtypeStruct((256, 1024), BF16)
    return pl.pallas_call(
        pack_kernel,
        out_shape=(mix_shape, up_shape, mix_shape, up_shape),
        in_specs=[SMEM, VMEM, VMEM, VMEM],
        out_specs=(VMEM,) * 4,
        compiler_params=params(24),
        cost_estimate=pl.CostEstimate(flops=0, bytes_accessed=6 * 10**6, transcendentals=0),
    )(at, mix_weight, up_weight, small)


def turn_lanes(pair, cos, sin_up, sin_down):
    return pair * cos + pltpu.roll(pair, 120, 1) * sin_up + pltpu.roll(pair, 8, 1) * sin_down


def project_kernel(at_ref, *refs):
    xs, gs, mixes = refs[0:4], refs[4:8], refs[8:12]
    dense_own, dense_other, tables = refs[12:15]
    sent, norm1, norm2, normal_out, g_out, mix_out, dense_out, vec_out = refs[15:23]
    x, core = at_ref[0], at_ref[1]
    hi, lo = x // 2, x % 2
    quarters = (2 * hi + core, 2 * (1 - hi) + core, 2 * hi + 1 - core, 2 * (1 - hi) + 1 - core)
    for w, piece in zip(quarters, mixes):
        mix_out[pl.ds(pl.multiple_of(w * 256, 256), 256), :] = piece[0:256, :]
        vec_out[0:16, pl.ds(pl.multiple_of(w * 256, 256), 256)] = piece[256:272, 0:256].astype(F32)

    @pl.when(core == lo)
    def _():
        dense_out[...] = dense_own[...]

    @pl.when(core != lo)
    def _():
        dense_out[...] = dense_other[...]

    for j in range(3):
        n = 4 * j + x
        row = vec_out[6:9, pl.ds(pl.multiple_of((n // 3) * 256, 256), 256)]
        keep = lax.broadcasted_iota(jnp.int32, (3, 256), 0) == n % 3
        vec_out[16:17, 256 * j : 256 * j + 256] = jnp.sum(
            jnp.where(keep, row, 0.0), 0, keepdims=True
        )
    for j in range(4):
        vec_out[17:18, 256 * j : 256 * j + 256] = vec_out[
            9 + j : 10 + j, pl.ds(pl.multiple_of(x * 256, 256), 256)
        ]
    gain1, shift1 = vec_out[0:1, :], vec_out[1:2, :]
    gain2, shift2 = vec_out[2:3, :], vec_out[3:4, :]
    bias = vec_out[16:17, 0:768]
    lane = lax.broadcasted_iota(jnp.int32, (BLK, 128), 1)
    left = lane < HDIM
    for j in range(4):
        chip = lax.rem(x + j, 4)
        to_hi, to_lo = chip // 2, chip % 2
        normal, _ = normalize(xs[j][...].astype(F32))
        normal_out[chip] = normal
        low1 = (normal * gain1 + shift1).astype(BF16)
        norm1[chip] = low1
        norm2[chip] = (normal * gain2 + shift2).astype(BF16)
        grad = gs[j][...]
        g_out[chip] = grad
        mixed = dot(low1, mix_out[...]) + bias
        d_merged = dot_t(grad, dense_out[...])
        cos, sin_up, sin_down = tables[0, to_lo], tables[1, to_lo], tables[2, to_lo]
        for h in range(2):
            at = slice(128 * h, 128 * h + 128)
            q = turn_lanes(mixed[:, 0:256][:, at], cos, sin_up, sin_down)
            k = turn_lanes(mixed[:, 256:512][:, at], cos, sin_up, sin_down)
            v = mixed[:, 512:768][:, at]
            dm = d_merged[:, at]
            for side in range(2):
                if side == 0:
                    kv = jnp.where(left, k, pltpu.roll(v, 64, 1)).astype(BF16)
                    qd = jnp.where(left, q, pltpu.roll(dm, 64, 1)).astype(BF16)
                else:
                    kv = jnp.where(left, pltpu.roll(k, 64, 1), v).astype(BF16)
                    qd = jnp.where(left, pltpu.roll(q, 64, 1), dm).astype(BF16)
                i = 2 * h + side
                for half in range(2):
                    sent[i, to_hi, half, to_lo, 0:BLK, :] = kv
                    sent[i, to_hi, half, to_lo, BLK : BLK + HALF, :] = qd[
                        HALF * half : HALF * half + HALF
                    ]


def project(at, xs, gs, mixes, dense_own, dense_other, tables):
    tokens = jax.ShapeDtypeStruct((4, BLK, D), BF16)
    return pl.pallas_call(
        project_kernel,
        out_shape=(
            jax.ShapeDtypeStruct((4, 2, 2, 2, BLK + HALF, 128), BF16),
            tokens,
            tokens,
            jax.ShapeDtypeStruct((4, BLK, D), F32),
            tokens,
            jax.ShapeDtypeStruct((D, 768), BF16),
            jax.ShapeDtypeStruct((256, D), BF16),
            jax.ShapeDtypeStruct((24, D), F32),
        ),
        in_specs=[SMEM] + [VMEM] * 15,
        out_specs=(VMEM,) * 8,
        compiler_params=params(40),
        cost_estimate=pl.CostEstimate(
            flops=2 * 768 * 1024 * 1024, bytes_accessed=20 * 10**6, transcendentals=0
        ),
    )(at, *xs, *gs, *mixes, dense_own, dense_other, tables)


def unpack_kernel(at_ref, back, tables, norm1_t, g_ref, d_mixed, merged, given, kept):
    core = at_ref[1]
    lane = lax.broadcasted_iota(jnp.int32, (BLK, 128), 1)
    left = lane < HDIM
    for hi in range(2):
        for lo in range(2):
            cos, sin_up, sin_down = tables[0, lo], tables[1, lo], tables[2, lo]
            rows = slice((2 * hi + lo) * BLK, (2 * hi + lo + 1) * BLK)
            for h in range(2):
                kv, qo = [], []
                for i in (2 * h, 2 * h + 1):
                    kv.append(
                        back[i, hi, 0, lo, 0:BLK, :].astype(F32)
                        + back[i, hi, 1, lo, 0:BLK, :].astype(F32)
                    )
                    qo.append(
                        jnp.concatenate(
                            [back[i, hi, s, lo, BLK : BLK + HALF, :] for s in range(2)], 0
                        ).astype(F32)
                    )
                dq = jnp.where(left, qo[0], pltpu.roll(qo[1], 64, 1))
                out = jnp.where(left, pltpu.roll(qo[0], 64, 1), qo[1])
                dk = jnp.where(left, kv[0], pltpu.roll(kv[1], 64, 1))
                dv = jnp.where(left, pltpu.roll(kv[0], 64, 1), kv[1])
                dq = turn_lanes(dq, cos, -sin_up, -sin_down)
                dk = turn_lanes(dk, cos, -sin_up, -sin_down)
                for k, value in enumerate((dq, dk, dv)):
                    at = 256 * k + 128 * h
                    d_mixed[rows, at : at + 128] = value.astype(BF16)
                merged[rows, 128 * h : 128 * h + 128] = out.astype(BF16)
    merged_t = merged[...].astype(F32).T.astype(BF16)
    dense = dot(merged_t, g_ref[...])
    for c, out in ((1 - core, given), (core, kept)):
        for hi in range(2):
            rows = pl.ds(pl.multiple_of(512 * hi + 256 * c, 256), 256)
            part = dot(norm1_t[rows, :], d_mixed[...])
            out[:, 16 * hi : 16 * hi + 16, 0:768] = part.reshape(16, 16, 768).astype(out.dtype)
        half = jnp.where(c == 0, dense[0:128], dense[128:256]).astype(out.dtype)
        for i in range(4):
            for j in range(4):
                out[4 * i + j, :, 768:1024] = half[32 * i : 32 * i + 32, 256 * j : 256 * j + 256]


def unpack(at, back, tables, norm1_t, token_g):
    return pl.pallas_call(
        unpack_kernel,
        out_shape=(
            jax.ShapeDtypeStruct((768, 768), BF16),
            jax.ShapeDtypeStruct((768, 256), BF16),
            jax.ShapeDtypeStruct((16, 32, 1024), BF16),
            jax.ShapeDtypeStruct((16, 32, 1024), F32),
        ),
        in_specs=[SMEM] + [VMEM] * 4,
        out_specs=(VMEM,) * 4,
        compiler_params=params(40),
        cost_estimate=pl.CostEstimate(
            flops=2 * 768 * 1024 * 1024, bytes_accessed=12 * 10**6, transcendentals=0
        ),
    )(at, back, tables, norm1_t, token_g)


def finish_kernel(
    at_ref, d_mixed, merged, mix, dense, feed, d_norm2, normal, g_own, d_pre, vec, parts, mine, sums
):
    x = at_ref[0]
    gain1, gain2 = vec[0:1, :], vec[2:3, :]
    totals = [jnp.zeros((1, D), F32) for _ in range(4)]
    for j in range(4):
        rows = pl.ds(pl.multiple_of(lax.rem(x + j, 4) * BLK, BLK), BLK)
        d1 = dot_t(d_mixed[rows, :], mix[...])
        d2 = d_norm2[rows, :]
        n = normal[rows, :]
        out = dot(merged[rows, :], dense[...]) + feed[rows, :]
        e = gain1 * d1 + gain2 * d2
        if j == 0:
            mine[0:BLK, :] = out
            mine[BLK : 2 * BLK, :] = e
        else:
            parts[j - 1, 0:BLK, :] = out.astype(BF16)
            parts[j - 1, BLK : 2 * BLK, :] = e.astype(BF16)
        for k, value in enumerate((d1 * n, d1, d2 * n, d2)):
            totals[k] = totals[k] + jnp.sum(value, 0, keepdims=True)
    for k in range(4):
        sums[k : k + 1, :] = totals[k].astype(BF16)
    sums[4:5, :] = jnp.sum(g_own[...].astype(F32), 0, keepdims=True).astype(BF16)
    sums[5:6, :] = jnp.zeros((1, D), BF16)
    sums[5:6, 0:768] = jnp.sum(d_mixed[...].astype(F32), 0, keepdims=True).astype(BF16)
    sums[6:7, :] = jnp.sum(d_pre[...].astype(F32), 0, keepdims=True).astype(BF16)
    sums[7:8, :] = jnp.zeros((1, D), BF16)


def finish(at, *operands):
    return pl.pallas_call(
        finish_kernel,
        out_shape=(
            jax.ShapeDtypeStruct((3, 2 * BLK, D), BF16),
            jax.ShapeDtypeStruct((2 * BLK, D), F32),
            jax.ShapeDtypeStruct((8, D), BF16),
        ),
        in_specs=[SMEM] + [VMEM] * 10,
        out_specs=(VMEM,) * 3,
        compiler_params=params(40),
        cost_estimate=pl.CostEstimate(
            flops=2 * 768 * 1024 * 1024, bytes_accessed=20 * 10**6, transcendentals=0
        ),
    )(at, *operands)


def columns_kernel(at_ref, *refs, groups):
    pieces, out = refs[:4], refs[4]
    x = at_ref[0]
    width = pieces[0].shape[1] // groups
    for j in range(4):
        chip = lax.rem(x + j, 4)
        for k in range(groups):
            at = pl.multiple_of((4 * k + chip) * width, width)
            out[:, pl.ds(at, width)] = pieces[j][:, k * width : k * width + width].astype(F32)


def all_columns(at, pieces, groups):
    rows, columns = pieces[0].shape
    return pl.pallas_call(
        functools.partial(columns_kernel, groups=groups),
        out_shape=jax.ShapeDtypeStruct((rows, 4 * columns), F32),
        in_specs=[SMEM] + [VMEM] * 4,
        out_specs=VMEM,
        compiler_params=params(24),
        cost_estimate=pl.CostEstimate(
            flops=0, bytes_accessed=24 * rows * columns, transcendentals=0
        ),
    )(at, *pieces)


def shards(
    inputs,
    first_gain,
    first_bias,
    second_gain,
    second_bias,
    mix_weight,
    mix_bias,
    dense_weight,
    dense_bias,
    up_weight,
    up_bias,
    down_weight,
    down_bias,
    grad_out,
):
    ctx, wa = lax.axis_index("ctx"), lax.axis_index("wa")
    lo, yz, hi, core = ctx % 2, ctx // 2, wa // 2, wa % 2
    x = 2 * hi + lo
    at = jnp.stack([x, core])

    small = jnp.concatenate(
        [first_gain, first_bias, second_gain, second_bias, dense_bias, down_bias, mix_bias, up_bias]
    )
    small = jnp.pad(small.reshape(13, 256), ((0, 3), (0, 0)))
    mix_own, up_own, mix_cross, up_cross = pack(
        jnp.stack([x, 3 - x]), mix_weight, up_weight, small
    )
    mix_got = send(mix_cross, CROSS)
    dense_other = send(dense_weight, CORE)
    mix_other = send(mix_own, CORE)
    mix_other_got = send(mix_got, CORE)
    xs = ring_gather(inputs[0])
    gs = ring_gather(after(grad_out[0], xs[1]))
    up_got = send(after(up_cross, gs[1]), CROSS)
    up_other = send(up_own, CORE)
    up_other_got = send(up_got, CORE)
    down_other = send(down_weight, CORE)

    spots = (jnp.arange(384, dtype=jnp.int32) + yz * 384).astype(F32)
    angles = spots[:, None] * (1.0 / 10000.0 ** (jnp.arange(0, ROT, 2, dtype=F32) / ROT))[None]
    cos8, sin8 = jnp.cos(angles), jnp.sin(angles)
    gap = jnp.zeros((384, 48), F32)
    none = jnp.zeros((384, 8), F32)
    tables = jnp.stack(
        [
            jnp.concatenate([cos8, cos8, gap + 1.0] * 2, 1),
            jnp.concatenate([-sin8, none, gap] * 2, 1),
            jnp.concatenate([none, sin8, gap] * 2, 1),
        ]
    ).reshape(3, 2, BLK, 128)

    sent, norm_one, norm_two, normal, token_g, mix, dense, vec = project(
        at, xs, gs, (mix_own, mix_got, mix_other, mix_other_got), dense_weight, dense_other, tables
    )
    norm_one, norm_two = norm_one.reshape(768, D), norm_two.reshape(768, D)
    token_g, normal = token_g.reshape(768, D), normal.reshape(768, D)
    norm1_t = norm_one.T
    held = swap(sent.reshape(16, 2 * 288, 128)).reshape(32, 288, 128)

    near, far = jnp.where(core == 0, up_own, up_other), jnp.where(core == 0, up_other, up_own)
    near_got = jnp.where(core == 0, up_got, up_other_got)
    far_got = jnp.where(core == 0, up_other_got, up_got)
    up = jnp.where(
        hi == 0,
        jnp.concatenate([near, far, near_got, far_got], 0),
        jnp.concatenate([near_got, far_got, near, far], 0),
    )
    down = jnp.where(core == lo, down_weight, down_other)
    bias_up = vec[17:18]
    up_pre = dot(norm_two, up) + bias_up
    below = 0.5 + 0.5 * lax.erf(up_pre * 0.5**0.5)
    hidden = (up_pre * below).astype(BF16)
    bell = jnp.exp(-0.5 * up_pre * up_pre) * (0.5 / jnp.pi) ** 0.5
    d_pre = (dot_t(token_g, down) * (below + up_pre * bell)).astype(BF16)
    d_norm_two = dot_t(d_pre, up)
    feed = dot(hidden, down)

    def core_sum(left, right, shape, axis):
        whole = t_dot(left, right)
        whole = whole.reshape(*shape, whole.shape[1])
        given = pick(whole, 1 - core, axis).astype(BF16)
        return (pick(whole, core, axis) + send(given, CORE).astype(F32)).astype(BF16)

    sum_up = core_sum(norm_two, d_pre, (2, 2, 256), 1)
    sum_down = core_sum(hidden, token_g, (2, 512), 0)
    ff_sums = jnp.stack(
        [
            sum_up.reshape(2, 16, 16, 1024).transpose(1, 0, 2, 3).reshape(16, 32, 1024),
            sum_down.reshape(16, 32, 1024),
        ],
        1,
    ).reshape(16, 64, 1024)
    ff_mine = jnp.sum(swap(ff_sums).astype(F32), 0).astype(BF16)

    back = attention((yz % 2).reshape(1), after(held, ff_sums)).reshape(16, 2 * 288, 128)
    back = swap(back).reshape(4, 2, 2, 2, 288, 128)
    d_mixed, merged, given, kept = unpack(at, back, tables, norm1_t, token_g)
    attn_sums = (kept + send(given, CORE).astype(F32)).astype(BF16)
    ff_all = swap(jnp.broadcast_to(after(ff_mine, back)[None], (16, 64, 1024)))
    attn_mine = jnp.sum(swap(after(attn_sums, ff_all)).astype(F32), 0).astype(BF16)

    parts, mine, vectors = finish(
        at, after(d_mixed, given), merged, mix, dense, feed, d_norm_two, normal, grad_out[0], d_pre, vec
    )
    for d in (1, 3, 2):
        mine = mine + send(parts[d - 1], RING[d]).astype(F32)
    own_in, own_g = inputs[0].astype(F32), grad_out[0].astype(F32)
    output = (own_in + mine[:BLK] + vec[4:5] + vec[5:6]).astype(BF16)[None]
    own_normal, own_inv = normalize(own_in)
    grad_in = (own_g + norm_back(own_normal, own_inv, 1.0, mine[BLK:])).astype(BF16)[None]
    spread = jnp.concatenate([attn_mine, vectors], 0)
    attn_all = swap(jnp.broadcast_to(spread[None], (16, 40, 1024)))

    def by_columns(sums, width, rows=None):
        sums = sums.reshape(16, 2, 16, width).transpose(1, 0, 2, 3).reshape(2, 256, width)
        extra = [] if rows is None else [rows]
        pieces = [jnp.concatenate([pick(sums, hi), *extra], 0)]
        for d in (3, 2, 1):
            value = jnp.concatenate([pick(sums, ((x + d) % 4) // 2), *extra], 0)
            pieces.append(send(value, RING[d]))
        return pieces

    def by_rows(half):
        beside = send(half, NEXT)
        kept = jnp.where(core == lo, half, beside)
        given = send(jnp.where(core == lo, beside, half), CORE)
        return jnp.where(
            core == 0, jnp.concatenate([kept, given], 0), jnp.concatenate([given, kept], 0)
        ).astype(F32)

    grad_up = all_columns(at, by_columns(ff_all[:, :32], 1024), 1)
    grad_down = by_rows(ff_all[:, 32:].reshape(512, 1024))
    rest = jnp.sum(attn_all[:, 32:].astype(F32), 0).reshape(-1)
    rest = rest + send(rest.astype(BF16), CORE).astype(F32)
    rest = jnp.pad(rest.astype(BF16), (0, 4096)).reshape(16, 768)
    pieces = by_columns(attn_all[:, :32, :768], 768, rest)
    grad_mix = all_columns(at, [p[:256] for p in pieces], 3)
    dense_half = attn_all[:, :32, 768:].reshape(4, 4, 32, 256).transpose(0, 2, 1, 3)
    grad_dense = by_rows(dense_half.reshape(128, 1024))
    rest = jnp.stack([p[256:] for p in pieces]).reshape(4, 12288)[:, :8192].astype(F32)
    whole = pick(jnp.sum(rest[:, :5120], 0).reshape(5, 4, 256), wa, 1)
    rest = lax.dynamic_slice_in_dim(jnp.concatenate([rest, rest]), (4 - x) % 4, 4, 0)
    rest_mix = rest[:, 5120:5888].reshape(4, 3, 256).transpose(1, 0, 2).reshape(4, 768)
    rest_up = rest[:, 6144:7168]
    return (
        output,
        grad_in,
        whole[0],
        whole[1],
        whole[2],
        whole[3],
        grad_mix,
        pick(rest_mix, wa),
        grad_dense,
        whole[4],
        grad_up,
        pick(rest_up, wa),
        grad_down,
        whole[4],
    )


def solution(mesh):
    rows, vec, tokens = P("wa", None), P("wa"), P("wa", "ctx", None)
    return jax.shard_map(
        shards,
        mesh=mesh,
        in_specs=(tokens, vec, vec, vec, vec, rows, vec, rows, vec, rows, vec, rows, vec, tokens),
        out_specs=(
            tokens,
            tokens,
            vec,
            vec,
            vec,
            vec,
            rows,
            vec,
            rows,
            vec,
            rows,
            vec,
            rows,
            vec,
        ),
        check_vma=False,
    )
```

```python
import functools
import math

import jax
import jax.numpy as jnp
from jax import lax
from jax.experimental import pallas as pl
from jax.experimental.pallas import tpu as pltpu
from jax.sharding import PartitionSpec as P

D = 1024
HEADS = 16
HDIM = 64
ROT = 16
FF = 4096
BLK = 192
HALF = 96
EPS = 1e-05
F32 = jnp.float32
BF16 = jnp.bfloat16


def attention_kernel(
    par_ref, x_ref, out_ref, kv, kvt, qd, s_buf, p_buf, dkv, oq, *, blocks, tq, kc
):
    n_keys, n_queries = blocks * BLK, blocks * HALF
    par = par_ref[0]

    def token(row):
        return (row // HALF) * BLK + par * HALF + row % HALF

    def fill(b, carry):
        kv[pl.ds(b * BLK, BLK), :] = x_ref[b, 0:BLK, :]
        qd[pl.ds(b * HALF, HALF), :] = x_ref[b, BLK : BLK + HALF, :]
        return carry

    lax.fori_loop(0, blocks, fill, 0)

    def turn(c, carry):
        kvt[:, pl.ds(pl.multiple_of(c * kc, kc), kc)] = kv[pl.ds(c * kc, kc), :].T
        dkv[pl.ds(c * kc, kc), :] = jnp.zeros((kc, 128), F32)
        return carry

    lax.fori_loop(0, n_keys // kc, turn, 0)
    row = lax.broadcasted_iota(jnp.int32, (128, tq), 0)
    lane = lax.broadcasted_iota(jnp.int32, (tq, 128), 1)
    q_col = lax.broadcasted_iota(jnp.int32, (kc, tq), 1)
    k_row = lax.broadcasted_iota(jnp.int32, (kc, tq), 0)
    zero = jnp.zeros((), F32)

    def group(t, carry):
        first = t * tq
        n_all = (token(first + tq - 1) + kc) // kc
        n_full = (token(first) + 1) // kc
        qd_rows = qd[pl.ds(pl.multiple_of(first, tq), tq), :]
        qd_t = qd_rows.astype(F32).T
        q_t = jnp.where(row < HDIM, qd_t * 0.125, zero).astype(BF16)
        q_idx = first + q_col
        q_tok = (q_idx // HALF) * BLK + par * HALF + q_idx % HALF

        def scores(c, top, masked):
            o = pl.multiple_of(c * kc, kc)
            s = jnp.dot(kv[pl.ds(o, kc), :], q_t, preferred_element_type=F32)
            if masked:
                s = jnp.where(c * kc + k_row <= q_tok, s, -1e30)
            s_buf[pl.ds(o, kc), :] = s
            return jnp.maximum(top, jnp.max(s.reshape(kc // 8, 8, tq), 0))

        top = jnp.full((8, tq), -1e30, F32)
        top = lax.fori_loop(0, n_full, lambda c, m: scores(c, m, False), top)
        top = lax.fori_loop(n_full, n_all, lambda c, m: scores(c, m, True), top)
        top = jnp.max(top, 0, keepdims=True)

        def weigh(c, state):
            total, out_t = state
            o = pl.multiple_of(c * kc, kc)
            p = jnp.exp(s_buf[pl.ds(o, kc), :] - top)
            total = total + jnp.sum(p.reshape(kc // 8, 8, tq), 0)
            p_low = p.astype(BF16)
            p_buf[pl.ds(o, kc), :] = p_low
            out_t = out_t + jnp.dot(kvt[HDIM:, pl.ds(o, kc)], p_low, preferred_element_type=F32)
            return total, out_t

        total, out_t = lax.fori_loop(
            0, n_all, weigh, (jnp.zeros((8, tq), F32), jnp.zeros((HDIM, tq), F32))
        )
        inv = 1.0 / jnp.sum(total, 0, keepdims=True)
        out_t = out_t * inv
        do_t = (qd_t[HDIM:] * inv).astype(BF16)
        delta = jnp.sum(do_t.astype(F32) * out_t, 0, keepdims=True)
        do_full = jnp.concatenate([jnp.zeros((HDIM, tq), BF16), do_t], 0)
        do_rows = do_full.astype(F32).T.astype(BF16)
        q_rows = jnp.where(lane < HDIM, qd_rows.astype(F32) * 0.125, zero).astype(BF16)

        def back(c, dq_t):
            o = pl.multiple_of(c * kc, kc)
            dp = jnp.dot(kv[pl.ds(o, kc), :], do_full, preferred_element_type=F32)
            p_low = p_buf[pl.ds(o, kc), :]
            ds = (p_low.astype(F32) * (dp - delta)).astype(BF16)
            dkv[pl.ds(o, kc), :] += jnp.dot(
                p_low, do_rows, preferred_element_type=F32
            ) + jnp.dot(ds, q_rows, preferred_element_type=F32)
            return dq_t + jnp.dot(kvt[:HDIM, pl.ds(o, kc)], ds, preferred_element_type=F32)

        dq_t = lax.fori_loop(0, n_all, back, jnp.zeros((HDIM, tq), F32)) * 0.125
        oq[pl.ds(pl.multiple_of(first, tq), tq), :] = (
            jnp.concatenate([dq_t, out_t], 0).T.astype(BF16)
        )
        return carry

    lax.fori_loop(0, n_queries // tq, group, 0)

    def drain(b, carry):
        out_ref[b, 0:BLK, :] = dkv[pl.ds(b * BLK, BLK), :].astype(BF16)
        out_ref[b, BLK : BLK + HALF, :] = oq[pl.ds(b * HALF, HALF), :]
        return carry

    lax.fori_loop(0, blocks, drain, 0)


def attention(par, x, tq=768, kc=1536):
    blocks = x.shape[0]
    n_keys, n_queries = blocks * BLK, blocks * HALF
    whole = pl.BlockSpec(x.shape, lambda i: (0, 0, 0), pipeline_mode=pl.Buffered(1))
    return pl.pallas_call(
        functools.partial(attention_kernel, blocks=blocks, tq=tq, kc=kc),
        grid=(1,),
        out_shape=jax.ShapeDtypeStruct(x.shape, BF16),
        in_specs=[pl.BlockSpec(memory_space=pltpu.SMEM), whole],
        out_specs=whole,
        scratch_shapes=[
            pltpu.VMEM((n_keys, 128), BF16),
            pltpu.VMEM((128, n_keys), BF16),
            pltpu.VMEM((n_queries, 128), BF16),
            pltpu.VMEM((n_keys, tq), F32),
            pltpu.VMEM((n_keys, tq), BF16),
            pltpu.VMEM((n_keys, 128), F32),
            pltpu.VMEM((n_queries, 128), BF16),
        ],
        compiler_params=pltpu.CompilerParams(vmem_limit_bytes=60 * 2**20),
        cost_estimate=cost(46),
    )(par, x)


def cost(micros):
    return pl.CostEstimate(flops=int(micros * 1.1e9), bytes_accessed=10**5, transcendentals=0)


def normalize(values):
    centred = values - jnp.mean(values, -1, keepdims=True)
    spread = jnp.mean(centred * centred, -1, keepdims=True)
    inv = lax.rsqrt(spread + EPS)
    return centred * inv, inv


def norm_back(normal, inv, e):
    return inv * (
        e
        - jnp.mean(e, -1, keepdims=True)
        - normal * jnp.mean(e * normal, -1, keepdims=True)
    )


def dot(a, b):
    return jnp.dot(a, b, preferred_element_type=F32)


def dot_t(a, b):
    return lax.dot_general(a, b, (((1,), (1,)), ((), ())), preferred_element_type=F32)


def t_dot(a, b):
    return lax.dot_general(a, b, (((0,), (0,)), ((), ())), preferred_element_type=F32)


AX = ("ctx", "wa")
YZ = [[2 * i + lo for i in range(16)] for lo in range(2)]
SMEM = pl.BlockSpec(memory_space=pltpu.SMEM)


def route(move):
    pairs = []
    for ctx in range(32):
        for wa in range(4):
            to_x, y, z, core = move(wa // 2 * 2 + ctx % 2, ctx // 8, ctx // 2 % 4, wa % 2)
            to_ctx, to_wa = y * 8 + z * 2 + to_x % 2, to_x // 2 * 2 + core
            pairs.append((ctx * 4 + wa, to_ctx * 4 + to_wa))
    return pairs


RING = [route(lambda x, y, z, c, d=d: ((x + d) % 4, y, z, c)) for d in range(4)]
CORE = route(lambda x, y, z, c: (x, y, z, 1 - c))
CROSS = route(lambda x, y, z, c: (3 - x, y, z, c))
FAR = RING[2]
NEXT = route(lambda x, y, z, c: (x ^ 1, y, z, c))
TREE = (0, 1, 3, 2)


def send(value, pairs):
    return lax.ppermute(value, AX, pairs)


def pick(array, index, axis=0):
    return lax.dynamic_index_in_dim(array, index, axis, keepdims=False)


def after(value, *first):
    return lax.optimization_barrier((value, *first))[0]


def ring_gather(own):
    return [own, send(own, RING[3]), send(own, RING[2]), send(own, RING[1])]


def swap(pieces):
    return lax.all_to_all(pieces, "ctx", 0, 0, axis_index_groups=YZ, tiled=True)


def call(kernel, at, operands, outs, micros, scratch=()):
    def whole(a):
        return pl.BlockSpec(a.shape, lambda i: (0,) * len(a.shape), pipeline_mode=pl.Buffered(1))

    return pl.pallas_call(
        kernel,
        grid=(1,),
        out_shape=tuple(outs),
        in_specs=[SMEM] + [whole(a) for a in operands],
        out_specs=tuple(whole(a) for a in outs),
        scratch_shapes=list(scratch),
        compiler_params=pltpu.CompilerParams(vmem_limit_bytes=60 * 2**20),
        cost_estimate=cost(micros),
    )(at, *operands)


def struct(shape, dtype=BF16):
    return jax.ShapeDtypeStruct(shape, dtype)


def pack_kernel(at_ref, mix_ref, up_ref, dense_ref, small_ref, own, mix_cross, up_cross):
    for k, (mix_out, up_out) in enumerate(((own.at[0:256], own.at[256:512]), (mix_cross, up_cross))):
        q = at_ref[0] if k == 0 else 3 - at_ref[0]
        for j in range(3):
            cols = pl.ds(pl.multiple_of(q * 256 + j * 1024, 256), 256)
            mix_out[:, 256 * j : 256 * j + 256] = mix_ref[:, cols]
        mix_out[0:16, 768:1024] = small_ref[...]
        mix_out[16:256, 768:1024] = jnp.zeros((240, 256), BF16)
        up_out[...] = up_ref[:, pl.ds(pl.multiple_of(q * 1024, 1024), 1024)]
    own[512:768, :] = dense_ref[...]


def tables_kernel(at_ref, tables):
    shape = (BLK, 128)
    feature = lax.broadcasted_iota(jnp.int32, shape, 1) % HDIM
    exponent = (feature % 8).astype(F32) * (2.0 / ROT)
    inverse = jnp.exp(exponent * -math.log(10000.0))
    for block in range(2):
        spot = at_ref[4] * (2 * BLK) + block * BLK + lax.broadcasted_iota(jnp.int32, shape, 0)
        angle = spot.astype(F32) * inverse
        sine = jnp.sin(angle)
        tables[0, block] = jnp.where(feature < ROT, jnp.cos(angle), 1.0)
        tables[1, block] = jnp.where(feature < ROT // 2, -sine, 0.0)
        tables[2, block] = jnp.where((feature >= ROT // 2) & (feature < ROT), sine, 0.0)


def turn_lanes(pair, cos, sin_up, sin_down):
    return pair * cos + pltpu.roll(pair, 120, 1) * sin_up + pltpu.roll(pair, 8, 1) * sin_down


def project_kernel(at_ref, *refs):
    tokens, mixes = refs[0:4], refs[4:8]
    tables = refs[8]
    sent, mix_out, dense_out, vec_out = refs[9:13]
    x, core = at_ref[0], at_ref[1]
    hi, lo = x // 2, x % 2
    quarters = (2 * hi + core, 2 * (1 - hi) + core, 2 * hi + 1 - core, 2 * (1 - hi) + 1 - core)
    for w, piece in zip(quarters, mixes):
        cols = pl.ds(pl.multiple_of(w * 256, 256), 256)
        mix_out[cols, :] = piece[0:256, 0:768]
        vec_out[0:16, cols] = piece[0:16, 768:1024].astype(F32)

    @pl.when(core == lo)
    def _():
        dense_out[...] = mixes[0][512:768, :]

    @pl.when(core != lo)
    def _():
        dense_out[...] = mixes[2][512:768, :]

    for j in range(3):
        n = 4 * j + x
        row = vec_out[6:9, pl.ds(pl.multiple_of((n // 3) * 256, 256), 256)]
        keep = lax.broadcasted_iota(jnp.int32, (3, 256), 0) == n % 3
        vec_out[16:17, 256 * j : 256 * j + 256] = jnp.sum(
            jnp.where(keep, row, 0.0), 0, keepdims=True
        )
    for j in range(4):
        vec_out[17:18, 256 * j : 256 * j + 256] = vec_out[
            9 + j : 10 + j, pl.ds(pl.multiple_of(x * 256, 256), 256)
        ]
    gain1, shift1 = vec_out[0:1, :], vec_out[1:2, :]
    bias = vec_out[16:17, 0:768]
    lane = lax.broadcasted_iota(jnp.int32, (BLK, 128), 1)
    left = lane < HDIM
    for j in range(4):
        chip = lax.bitwise_xor(x, TREE[j])
        to_hi, to_lo = chip // 2, chip % 2
        normal, _ = normalize(tokens[j][0:BLK, :].astype(F32))
        low1 = (normal * gain1 + shift1).astype(BF16)
        grad = tokens[j][BLK : 2 * BLK, :]
        mixed = dot(low1, mix_out[...]) + bias
        d_merged = dot_t(grad, dense_out[...])
        cos, sin_up, sin_down = tables[0, to_lo], tables[1, to_lo], tables[2, to_lo]
        for h in range(2):
            at = slice(128 * h, 128 * h + 128)
            q = turn_lanes(mixed[:, 0:256][:, at], cos, sin_up, sin_down)
            k = turn_lanes(mixed[:, 256:512][:, at], cos, sin_up, sin_down)
            v = mixed[:, 512:768][:, at]
            dm = d_merged[:, at]
            for side in range(2):
                if side == 0:
                    kv = jnp.where(left, k, pltpu.roll(v, 64, 1)).astype(BF16)
                    qd = jnp.where(left, q, pltpu.roll(dm, 64, 1)).astype(BF16)
                else:
                    kv = jnp.where(left, pltpu.roll(k, 64, 1), v).astype(BF16)
                    qd = jnp.where(left, pltpu.roll(q, 64, 1), dm).astype(BF16)
                i = 2 * h + side
                for half in range(2):
                    sent[i, to_hi, half, to_lo, 0:BLK, :] = kv
                    sent[i, to_hi, half, to_lo, BLK : BLK + HALF, :] = qd[
                        HALF * half : HALF * half + HALF
                    ]


def project(at, tokens, mixes, tables):
    outs = (
        struct((4, 2, 2, 2, BLK + HALF, 128)),
        struct((D, 768)),
        struct((256, D)),
        struct((24, D), F32),
    )
    return call(project_kernel, at, (*tokens, *mixes, tables), outs, 0.1)


def mlp_kernel(at_ref, *refs):
    tokens, vec, ups, downs = refs[0:4], refs[4], refs[5:9], refs[9:11]
    normal_out, norm1_t, g_out, d_norm2, given, kept, feed_sent, feed_own, sums = refs[11:20]
    norm1, norm2, norm2_t, hidden, hidden_t, d_pre, up, down = refs[20:28]
    x, core = at_ref[0], at_ref[1]
    hi, lo = x // 2, x % 2
    quarters = (2 * hi + core, 2 * (1 - hi) + core, 2 * hi + 1 - core, 2 * (1 - hi) + 1 - core)
    for w, piece in zip(quarters, ups):
        rows = slice(256, 512) if piece.shape[0] > 256 else slice(0, 256)
        up[pl.ds(pl.multiple_of(w * 256, 256), 256), :] = piece[rows, :]

    @pl.when(core == lo)
    def _():
        down[...] = downs[0][...]

    @pl.when(core != lo)
    def _():
        down[...] = downs[1][...]

    for j in range(4):
        rows = slice(BLK * j, BLK * j + BLK)
        normal, _ = normalize(tokens[j][0:BLK, :].astype(F32))
        normal_out[rows, :] = normal.astype(BF16)
        norm1[rows, :] = (normal * vec[0:1, :] + vec[1:2, :]).astype(BF16)
        norm2[rows, :] = (normal * vec[2:3, :] + vec[3:4, :]).astype(BF16)
        g_out[rows, :] = tokens[j][BLK : 2 * BLK, :]
    for k in range(4):
        cols = slice(256 * k, 256 * k + 256)
        pre = dot(norm2[...], up[:, cols]) + vec[17:18, cols]
        below = 0.5 + 0.5 * lax.erf(pre * 0.5**0.5)
        hidden[:, cols] = (pre * below).astype(BF16)
        bell = jnp.exp(-0.5 * pre * pre) * (0.5 / math.pi) ** 0.5
        dp = (dot_t(g_out[...], down[cols, :]) * (below + pre * bell)).astype(BF16)
        d_pre[:, cols] = dp
        sums[:, cols] = jnp.sum(dp.astype(F32), 0, keepdims=True)
    d_norm2[...] = dot_t(d_pre[...], up[...]).astype(BF16)
    for j in range(4):
        feed = dot(hidden[BLK * j : BLK * j + BLK, :], down[...])
        if j == 0:
            feed_own[...] = feed
        else:
            feed_sent[j - 1] = feed.astype(BF16)
    for k in range(8):
        at = slice(128 * k, 128 * k + 128)
        norm1_t[at, :] = norm1[:, at].T
        norm2_t[at, :] = norm2[:, at].T
        hidden_t[at, :] = hidden[:, at].T
    for c, out in ((1 - core, given), (core, kept)):
        for w in range(2):
            rows = pl.ds(pl.multiple_of(512 * w + 256 * c, 256), 256)
            part = dot(norm2_t[rows, :], d_pre[...])
            out[:, 16 * w : 16 * w + 16, :] = part.reshape(16, 16, 1024).astype(out.dtype)
        part = dot(hidden_t[pl.ds(pl.multiple_of(512 * c, 512), 512), :], g_out[...])
        out[:, 32:64, :] = part.reshape(16, 32, 1024).astype(out.dtype)


def feed_forward(at, *operands):
    outs = (
        struct((768, D)),
        struct((D, 768)),
        struct((768, D)),
        struct((768, D)),
        struct((16, 64, 1024)),
        struct((16, 64, 1024)),
        struct((3, BLK, D)),
        struct((BLK, D), F32),
        struct((1, 1024), F32),
    )
    rows, columns = pltpu.VMEM((768, D), BF16), pltpu.VMEM((D, 768), BF16)
    square = pltpu.VMEM((D, 1024), BF16)
    scratch = (rows, rows, columns, rows, columns, rows, square, square)
    return call(mlp_kernel, at, operands, outs, 0.1, scratch)


def add_kernel(at_ref, a, b, out):
    out[...] = (a[...].astype(F32) + b[...].astype(F32)).astype(out.dtype)


def add(at, a, b):
    return call(add_kernel, at, (a, b), (struct(a.shape),), 0.1)[0]


def unpack_kernel(at_ref, back, tables, norm1_t, g_ref, d_mixed, merged, given, kept):
    core = at_ref[1]
    lane = lax.broadcasted_iota(jnp.int32, (BLK, 128), 1)
    left = lane < HDIM
    for j in range(4):
        if True:
            chip = lax.bitwise_xor(at_ref[0], TREE[j])
            hi, lo = chip // 2, chip % 2
            cos, sin_up, sin_down = tables[0, lo], tables[1, lo], tables[2, lo]
            rows = slice(j * BLK, j * BLK + BLK)
            for h in range(2):
                kv, qo = [], []
                for i in (2 * h, 2 * h + 1):
                    kv.append(
                        back[i, hi, 0, lo, 0:BLK, :].astype(F32)
                        + back[i, hi, 1, lo, 0:BLK, :].astype(F32)
                    )
                    qo.append(
                        jnp.concatenate(
                            [back[i, hi, s, lo, BLK : BLK + HALF, :] for s in range(2)], 0
                        ).astype(F32)
                    )
                dq = jnp.where(left, qo[0], pltpu.roll(qo[1], 64, 1))
                out = jnp.where(left, pltpu.roll(qo[0], 64, 1), qo[1])
                dk = jnp.where(left, kv[0], pltpu.roll(kv[1], 64, 1))
                dv = jnp.where(left, pltpu.roll(kv[0], 64, 1), kv[1])
                dq = turn_lanes(dq, cos, -sin_up, -sin_down)
                dk = turn_lanes(dk, cos, -sin_up, -sin_down)
                for k, value in enumerate((dq, dk, dv)):
                    at = 256 * k + 128 * h
                    d_mixed[rows, at : at + 128] = value.astype(BF16)
                merged[rows, 128 * h : 128 * h + 128] = out.astype(BF16)
    merged_t = merged[...].astype(F32).T.astype(BF16)
    dense = dot(merged_t, g_ref[...])
    for c, out in ((1 - core, given), (core, kept)):
        for hi in range(2):
            rows = pl.ds(pl.multiple_of(512 * hi + 256 * c, 256), 256)
            part = dot(norm1_t[rows, :], d_mixed[...])
            out[:, 16 * hi : 16 * hi + 16, 0:768] = part.reshape(16, 16, 768).astype(out.dtype)
        half = jnp.where(c == 0, dense[0:128], dense[128:256]).astype(out.dtype)
        for i in range(4):
            for j in range(4):
                out[4 * i + j, :, 768:1024] = half[32 * i : 32 * i + 32, 256 * j : 256 * j + 256]


def unpack(at, *operands):
    outs = (
        struct((768, 768)),
        struct((768, 256)),
        struct((16, 32, 1024)),
        struct((16, 32, 1024)),
    )
    return call(unpack_kernel, at, operands, outs, 0.1)


def finish_kernel(
    at_ref, d_mixed, merged, mix, d_norm2, normal, g_own, up_sum, vec, parts, e_own, merged_own, sums
):
    gain1, gain2 = vec[0:1, :], vec[2:3, :]
    totals = [jnp.zeros((1, D), F32) for _ in range(4)]
    for j in range(4):
        rows = slice(j * BLK, j * BLK + BLK)
        d1 = dot_t(d_mixed[rows, :], mix[...])
        d2 = d_norm2[rows, :].astype(F32)
        n = normal[rows, :].astype(F32)
        e = gain1 * d1 + gain2 * d2
        if j == 0:
            e_own[...] = e
            merged_own[...] = merged[rows, :]
        else:
            parts[j - 1, 0:BLK, :] = e.astype(BF16)
            heads = merged[rows, :]
            for k in range(4):
                parts[j - 1, BLK : BLK + 48, 256 * k : 256 * k + 256] = heads[48 * k : 48 * k + 48]
        for k, value in enumerate((d1 * n, d1, d2 * n, d2)):
            totals[k] = totals[k] + jnp.sum(value, 0, keepdims=True)
    for k in range(4):
        sums[k : k + 1, :] = totals[k].astype(BF16)
    sums[4:5, :] = jnp.sum(g_own[...].astype(F32), 0, keepdims=True).astype(BF16)
    sums[5:6, :] = jnp.zeros((1, D), BF16)
    sums[5:6, 0:768] = jnp.sum(d_mixed[...].astype(F32), 0, keepdims=True).astype(BF16)
    sums[6:7, :] = up_sum[...].astype(BF16)
    sums[7:8, :] = jnp.zeros((1, D), BF16)


def finish(at, *operands):
    outs = (
        struct((3, BLK + 48, D)),
        struct((BLK, D), F32),
        struct((BLK, 256)),
        struct((8, D)),
    )
    return call(finish_kernel, at, operands, outs, 0.1)


def tokens_kernel(at_ref, x_ref, g_ref, *refs):
    e_own, merged_own, feed_own = refs[0:3]
    late, feeds = refs[3:6], refs[6:9]
    dense, vec, out, grad_in = refs[9:13]
    x = at_ref[0]
    tokens = x_ref[...].astype(F32)
    total = tokens + vec[4:5, :] + vec[5:6, :] + feed_own[...]
    total = total + dot(merged_own[...], dense[x])
    e = e_own[...]
    for j in range(3):
        total = total + feeds[j][...].astype(F32)
        heads = jnp.concatenate(
            [late[j][BLK : BLK + 48, 256 * k : 256 * k + 256] for k in range(4)], 0
        )
        total = total + dot(heads, dense[lax.bitwise_xor(x, TREE[j + 1])])
        e = e + late[j][0:BLK, :].astype(F32)
    out[...] = total.astype(BF16)
    normal, inv = normalize(tokens)
    grad_in[...] = (g_ref[...].astype(F32) + norm_back(normal, inv, e)).astype(BF16)


def own_tokens(at, *operands):
    return call(tokens_kernel, at, operands, (struct((BLK, D)),) * 2, 0.1)


def down_kernel(at_ref, own_half, other_half, out):
    core = at_ref[1]
    for side, half in ((core, own_half), (1 - core, other_half)):
        rows = pl.ds(pl.multiple_of(side * 512, 512), 512)
        out[rows, :] = half[...].reshape(512, 1024).astype(F32)


def columns_kernel(at_ref, *refs, groups):
    pieces, out = refs[:4], refs[4]
    x = at_ref[0]
    width = pieces[0].shape[1] // groups
    for j in range(4):
        chip = lax.rem(x + j, 4)
        for k in range(groups):
            at = pl.multiple_of((4 * k + chip) * width, width)
            out[:, pl.ds(at, width)] = pieces[j][:, k * width : k * width + width].astype(F32)


def all_columns(at, pieces, groups):
    rows, columns = pieces[0].shape
    kernel = functools.partial(columns_kernel, groups=groups)
    return call(kernel, at, pieces, (struct((rows, 4 * columns), F32),), 0.1)[0]


def shards(
    inputs,
    first_gain,
    first_bias,
    second_gain,
    second_bias,
    mix_weight,
    mix_bias,
    dense_weight,
    dense_bias,
    up_weight,
    up_bias,
    down_weight,
    down_bias,
    grad_out,
):
    ctx, wa = lax.axis_index("ctx"), lax.axis_index("wa")
    lo, yz, hi, core = ctx % 2, ctx // 2, wa // 2, wa % 2
    x = 2 * hi + lo
    at = jnp.stack([x, core, yz // 4, yz % 4, yz])

    both = jnp.concatenate([inputs[0], grad_out[0]], 0)
    beside, across = send(both, NEXT), send(both, CROSS)
    tokens = (both, beside, across, send(across, NEXT))
    small, filled = 0, 0
    for v in (
        first_gain,
        first_bias,
        second_gain,
        second_bias,
        dense_bias,
        down_bias,
        mix_bias,
        up_bias,
    ):
        rows = v.shape[0] // 256
        small = small + jnp.pad(v.reshape(rows, 256), ((filled, 16 - filled - rows), (0, 0)))
        filled += rows
    own, mix_cross, up_cross = call(
        pack_kernel,
        at,
        (mix_weight, up_weight, dense_weight, after(small, beside, across)),
        (struct((768, 1024)), struct((256, 1024)), struct((256, 1024))),
        0.1,
    )
    tables = call(tables_kernel, at, (), (struct((3, 2, BLK, 128), F32),), 0.1)[0]
    mix_got = send(mix_cross, CROSS)
    other = send(own, CORE)
    mix_other_got = send(mix_got, CORE)
    up_got = send(after(up_cross, across, mix_got), CROSS)
    up_other_got = send(up_got, CORE)
    down_other = send(after(down_weight, across), CORE)

    sent, mix, dense, vec = project(at, tokens, (own, mix_got, other, mix_other_got), tables)
    held = swap(sent.reshape(16, 2 * 288, 128)).reshape(32, 288, 128)

    up_other_got = send(after(up_got, sent), CORE)
    normal, norm1_t, token_g, d_norm2, given, kept, feed_sent, feed_own, up_sum = feed_forward(
        at, *tokens, vec, own, up_got, other, up_other_got, down_weight, down_other
    )
    ff_sums = add(at, kept, send(given, CORE))
    ff_mine = swap(ff_sums)
    back = attention((yz % 2).reshape(1), after(held, ff_sums)).reshape(16, 2 * 288, 128)
    ff_mine = jnp.sum(ff_mine.astype(F32), 0).astype(BF16)
    feeds = [send(feed_sent[j], (NEXT, CROSS, FAR)[j]) for j in range(3)]
    dense_got = send(after(dense_weight, up_got), CROSS)
    back = swap(after(back, ff_mine, dense_got, *feeds))
    dense_other_got = send(after(dense_got, ff_mine), CORE)
    near = jnp.where(
        core == 0, jnp.stack([dense_weight, other[512:]]), jnp.stack([other[512:], dense_weight])
    )
    away = jnp.where(
        core == 0,
        jnp.stack([dense_got, dense_other_got]),
        jnp.stack([dense_other_got, dense_got]),
    )
    dense_all = jnp.where(hi == 0, jnp.concatenate([near, away]), jnp.concatenate([away, near]))
    back = after(back, dense_all)

    ff_all = swap(jnp.broadcast_to(after(ff_mine, back)[None], (16, 64, 1024)))
    d_mixed, merged, given, kept = unpack(
        at, back.reshape(4, 2, 2, 2, 288, 128), tables, norm1_t, token_g
    )
    attn_sums = add(at, kept, send(given, CORE))
    parts, e_own, merged_own, vectors = finish(
        at, after(d_mixed, given), merged, mix, d_norm2, normal, grad_out[0], up_sum, vec
    )
    late = [send(parts[j], (NEXT, CROSS, FAR)[j]) for j in range(3)]
    attn_mine = swap(after(attn_sums, ff_all, *late))

    up_all = ff_all[:, :32].reshape(16, 2, 16, 1024)
    up_pieces = [pick(up_all, hi, 1)]
    for d in (3, 2, 1):
        up_pieces.append(send(pick(up_all, ((x + d) % 4) // 2, 1), RING[d]))
    attn_mine = jnp.sum(attn_mine.astype(F32), 0).astype(BF16)
    spread = jnp.concatenate([attn_mine, vectors], 0)
    attn_all = swap(jnp.broadcast_to(spread[None], (16, 40, 1024)))

    down_own = after(ff_all[:, 32:], attn_mine, *up_pieces)
    down_beside = send(down_own, NEXT)
    output, grad_in = own_tokens(
        at, inputs[0], grad_out[0], e_own, merged_own, feed_own, *late, *feeds, dense_all, vec
    )
    grad_up = all_columns(at, [p.reshape(256, 1024) for p in up_pieces], 1)
    attn_all = after(attn_all, down_beside, output, grad_up)
    down_given = send(jnp.where(core == lo, down_beside, down_own), CORE)
    down_kept = jnp.where(core == lo, down_own, down_beside)
    grad_down = call(down_kernel, at, (down_kept, down_given), (struct((1024, D), F32),), 0.1)[0]

    def by_columns(sums, width, rows=None):
        sums = sums.reshape(16, 2, 16, width).transpose(1, 0, 2, 3).reshape(2, 256, width)
        extra = [] if rows is None else [rows]
        pieces = [jnp.concatenate([pick(sums, hi), *extra], 0)]
        for d in (3, 2, 1):
            value = jnp.concatenate([pick(sums, ((x + d) % 4) // 2), *extra], 0)
            pieces.append(send(value, RING[d]))
        return pieces

    def by_rows(half):
        beside = send(half, NEXT)
        kept = jnp.where(core == lo, half, beside)
        given = send(jnp.where(core == lo, beside, half), CORE)
        return jnp.where(
            core == 0, jnp.concatenate([kept, given], 0), jnp.concatenate([given, kept], 0)
        ).astype(F32)

    rest = jnp.sum(attn_all[:, 32:].astype(F32), 0).reshape(-1)
    rest = rest + send(rest.astype(BF16), CORE).astype(F32)
    rest = jnp.pad(rest.astype(BF16), (0, 4096)).reshape(16, 768)
    pieces = by_columns(attn_all[:, :32, :768], 768, rest)
    pieces[1] = after(pieces[1], grad_down)
    grad_mix = all_columns(at, [p[:256] for p in pieces], 3)
    dense_half = attn_all[:, :32, 768:].reshape(4, 4, 32, 256).transpose(0, 2, 1, 3)
    grad_dense = by_rows(dense_half.reshape(128, 1024))
    rest = jnp.stack([p[256:] for p in pieces]).reshape(4, 12288)[:, :8192].astype(F32)
    whole = pick(jnp.sum(rest[:, :5120], 0).reshape(5, 4, 256), wa, 1)
    rest = lax.dynamic_slice_in_dim(jnp.concatenate([rest, rest]), (4 - x) % 4, 4, 0)
    rest_mix = rest[:, 5120:5888].reshape(4, 3, 256).transpose(1, 0, 2).reshape(4, 768)
    rest_up = rest[:, 6144:7168]
    return (
        output[None],
        grad_in[None],
        whole[0],
        whole[1],
        whole[2],
        whole[3],
        grad_mix,
        pick(rest_mix, wa),
        grad_dense,
        whole[4],
        grad_up,
        pick(rest_up, wa),
        grad_down,
        whole[4],
    )


def solution(mesh):
    rows, vec, tokens = P("wa", None), P("wa"), P("wa", "ctx", None)
    return jax.shard_map(
        shards,
        mesh=mesh,
        in_specs=(tokens, vec, vec, vec, vec, rows, vec, rows, vec, rows, vec, rows, vec, tokens),
        out_specs=(
            tokens,
            tokens,
            vec,
            vec,
            vec,
            vec,
            rows,
            vec,
            rows,
            vec,
            rows,
            vec,
            rows,
            vec,
        ),
        check_vma=False,
    )
```

```python
import functools
import math

import jax
import jax.numpy as jnp
from jax import lax
from jax.experimental import pallas as pl
from jax.experimental.pallas import tpu as pltpu
from jax.sharding import PartitionSpec as P

D = 1024
HEADS = 16
HDIM = 64
ROT = 16
FF = 4096
BLK = 192
HALF = 96
EPS = 1e-05
F32 = jnp.float32
BF16 = jnp.bfloat16


def attention_kernel(
    par_ref, x_ref, out_ref, kv, kvt, qd, s_buf, p_buf, dkv, oq, *, blocks, tq, kc
):
    n_keys, n_queries = blocks * BLK, blocks * HALF
    par = par_ref[0]

    def token(row):
        return (row // HALF) * BLK + par * HALF + row % HALF

    def fill(b, carry):
        kv[pl.ds(b * BLK, BLK), :] = x_ref[b, 0:BLK, :]
        qd[pl.ds(b * HALF, HALF), :] = x_ref[b, BLK : BLK + HALF, :]
        return carry

    lax.fori_loop(0, blocks, fill, 0)

    def turn(c, carry):
        kvt[:, pl.ds(pl.multiple_of(c * kc, kc), kc)] = kv[pl.ds(c * kc, kc), :].T
        dkv[pl.ds(c * kc, kc), :] = jnp.zeros((kc, 128), F32)
        return carry

    lax.fori_loop(0, n_keys // kc, turn, 0)
    row = lax.broadcasted_iota(jnp.int32, (128, tq), 0)
    lane = lax.broadcasted_iota(jnp.int32, (tq, 128), 1)
    q_col = lax.broadcasted_iota(jnp.int32, (kc, tq), 1)
    k_row = lax.broadcasted_iota(jnp.int32, (kc, tq), 0)
    zero = jnp.zeros((), F32)

    def group(t, carry):
        first = t * tq
        n_all = (token(first + tq - 1) + kc) // kc
        n_full = (token(first) + 1) // kc
        qd_rows = qd[pl.ds(pl.multiple_of(first, tq), tq), :]
        qd_t = qd_rows.astype(F32).T
        q_t = jnp.where(row < HDIM, qd_t * 0.125, zero).astype(BF16)
        q_idx = first + q_col
        q_tok = (q_idx // HALF) * BLK + par * HALF + q_idx % HALF

        def scores(c, top, masked):
            o = pl.multiple_of(c * kc, kc)
            s = jnp.dot(kv[pl.ds(o, kc), :], q_t, preferred_element_type=F32)
            if masked:
                s = jnp.where(c * kc + k_row <= q_tok, s, -1e30)
            s_buf[pl.ds(o, kc), :] = s
            return jnp.maximum(top, jnp.max(s.reshape(kc // 8, 8, tq), 0))

        top = jnp.full((8, tq), -1e30, F32)
        top = lax.fori_loop(0, n_full, lambda c, m: scores(c, m, False), top)
        top = lax.fori_loop(n_full, n_all, lambda c, m: scores(c, m, True), top)
        top = jnp.max(top, 0, keepdims=True)

        def weigh(c, state):
            total, out_t = state
            o = pl.multiple_of(c * kc, kc)
            p = jnp.exp(s_buf[pl.ds(o, kc), :] - top)
            total = total + jnp.sum(p.reshape(kc // 8, 8, tq), 0)
            p_low = p.astype(BF16)
            p_buf[pl.ds(o, kc), :] = p_low
            out_t = out_t + jnp.dot(kvt[HDIM:, pl.ds(o, kc)], p_low, preferred_element_type=F32)
            return total, out_t

        total, out_t = lax.fori_loop(
            0, n_all, weigh, (jnp.zeros((8, tq), F32), jnp.zeros((HDIM, tq), F32))
        )
        inv = 1.0 / jnp.sum(total, 0, keepdims=True)
        out_t = out_t * inv
        do_t = (qd_t[HDIM:] * inv).astype(BF16)
        delta = jnp.sum(do_t.astype(F32) * out_t, 0, keepdims=True)
        do_full = jnp.concatenate([jnp.zeros((HDIM, tq), BF16), do_t], 0)
        do_rows = do_full.astype(F32).T.astype(BF16)
        q_rows = jnp.where(lane < HDIM, qd_rows.astype(F32) * 0.125, zero).astype(BF16)

        def back(c, dq_t):
            o = pl.multiple_of(c * kc, kc)
            dp = jnp.dot(kv[pl.ds(o, kc), :], do_full, preferred_element_type=F32)
            p_low = p_buf[pl.ds(o, kc), :]
            ds = (p_low.astype(F32) * (dp - delta)).astype(BF16)
            dkv[pl.ds(o, kc), :] += jnp.dot(
                p_low, do_rows, preferred_element_type=F32
            ) + jnp.dot(ds, q_rows, preferred_element_type=F32)
            return dq_t + jnp.dot(kvt[:HDIM, pl.ds(o, kc)], ds, preferred_element_type=F32)

        dq_t = lax.fori_loop(0, n_all, back, jnp.zeros((HDIM, tq), F32)) * 0.125
        oq[pl.ds(pl.multiple_of(first, tq), tq), :] = (
            jnp.concatenate([dq_t, out_t], 0).T.astype(BF16)
        )
        return carry

    lax.fori_loop(0, n_queries // tq, group, 0)

    def drain(b, carry):
        out_ref[b, 0:BLK, :] = dkv[pl.ds(b * BLK, BLK), :].astype(BF16)
        out_ref[b, BLK : BLK + HALF, :] = oq[pl.ds(b * HALF, HALF), :]
        return carry

    lax.fori_loop(0, blocks, drain, 0)


def attention(par, x, tq=768, kc=1536):
    blocks = x.shape[0]
    n_keys, n_queries = blocks * BLK, blocks * HALF
    whole = pl.BlockSpec(x.shape, lambda i: (0, 0, 0), pipeline_mode=pl.Buffered(1))
    return pl.pallas_call(
        functools.partial(attention_kernel, blocks=blocks, tq=tq, kc=kc),
        grid=(1,),
        out_shape=jax.ShapeDtypeStruct(x.shape, BF16),
        in_specs=[pl.BlockSpec(memory_space=pltpu.SMEM), whole],
        out_specs=whole,
        scratch_shapes=[
            pltpu.VMEM((n_keys, 128), BF16),
            pltpu.VMEM((128, n_keys), BF16),
            pltpu.VMEM((n_queries, 128), BF16),
            pltpu.VMEM((n_keys, tq), F32),
            pltpu.VMEM((n_keys, tq), BF16),
            pltpu.VMEM((n_keys, 128), F32),
            pltpu.VMEM((n_queries, 128), BF16),
        ],
        compiler_params=pltpu.CompilerParams(vmem_limit_bytes=63 * 2**20),
        cost_estimate=cost(46),
    )(par, x)


def cost(micros):
    return pl.CostEstimate(flops=int(micros * 1.1e9), bytes_accessed=10**5, transcendentals=0)


def normalize(values):
    centred = values - jnp.mean(values, -1, keepdims=True)
    spread = jnp.mean(centred * centred, -1, keepdims=True)
    inv = lax.rsqrt(spread + EPS)
    return centred * inv, inv


def norm_back(normal, inv, e):
    return inv * (
        e
        - jnp.mean(e, -1, keepdims=True)
        - normal * jnp.mean(e * normal, -1, keepdims=True)
    )


def dot(a, b):
    return jnp.dot(a, b, preferred_element_type=F32)


def dot_t(a, b):
    return lax.dot_general(a, b, (((1,), (1,)), ((), ())), preferred_element_type=F32)


def t_dot(a, b):
    return lax.dot_general(a, b, (((0,), (0,)), ((), ())), preferred_element_type=F32)


AX = ("ctx", "wa")
YZ = [[2 * i + lo for i in range(16)] for lo in range(2)]
SMEM = pl.BlockSpec(memory_space=pltpu.SMEM)


def route(move):
    pairs = []
    for ctx in range(32):
        for wa in range(4):
            to_x, y, z, core = move(wa // 2 * 2 + ctx % 2, ctx // 8, ctx // 2 % 4, wa % 2)
            to_ctx, to_wa = y * 8 + z * 2 + to_x % 2, to_x // 2 * 2 + core
            pairs.append((ctx * 4 + wa, to_ctx * 4 + to_wa))
    return pairs


CORE = route(lambda x, y, z, c: (x, y, z, 1 - c))
CROSS = route(lambda x, y, z, c: (3 - x, y, z, c))
FAR = route(lambda x, y, z, c: (x ^ 2, y, z, c))
NEXT = route(lambda x, y, z, c: (x ^ 1, y, z, c))
ASIDE = route(lambda x, y, z, c: (x ^ 1, y, z, 1 - c))
TREE = (0, 1, 3, 2)


def send(value, pairs):
    return lax.ppermute(value, AX, pairs)


def pick(array, index, axis=0):
    return lax.dynamic_index_in_dim(array, index, axis, keepdims=False)


def after(value, *first):
    return lax.optimization_barrier((value, *first))[0]


def swap(pieces):
    return lax.all_to_all(pieces, "ctx", 0, 0, axis_index_groups=YZ, tiled=True)


def call(kernel, at, operands, outs, micros, scratch=()):
    def whole(a):
        return pl.BlockSpec(a.shape, lambda i: (0,) * len(a.shape), pipeline_mode=pl.Buffered(1))

    return pl.pallas_call(
        kernel,
        grid=(1,),
        out_shape=tuple(outs),
        in_specs=[SMEM] + [whole(a) for a in operands],
        out_specs=tuple(whole(a) for a in outs),
        scratch_shapes=list(scratch),
        compiler_params=pltpu.CompilerParams(vmem_limit_bytes=63 * 2**20),
        cost_estimate=cost(micros),
    )(at, *operands)


def struct(shape, dtype=BF16):
    return jax.ShapeDtypeStruct(shape, dtype)


def pack_kernel(at_ref, mix_ref, up_ref, dense_ref, small_ref, own, mix_cross, up_cross):
    for k, (mix_out, up_out) in enumerate(((own.at[0:256], own.at[256:512]), (mix_cross, up_cross))):
        q = at_ref[0] if k == 0 else 3 - at_ref[0]
        for j in range(3):
            cols = pl.ds(pl.multiple_of(q * 256 + j * 1024, 256), 256)
            mix_out[0:256, 256 * j : 256 * j + 256] = mix_ref[:, cols]
        if k == 0:
            mix_out[0:16, 768:1024] = small_ref[...]
            mix_out[16:256, 768:1024] = jnp.zeros((240, 256), BF16)
        else:
            mix_out[256:272, 0:256] = small_ref[...]
            mix_out[256:272, 256:768] = jnp.zeros((16, 512), BF16)
        up_out[...] = up_ref[:, pl.ds(pl.multiple_of(q * 1024, 1024), 1024)]
    own[512:768, :] = dense_ref[...]


def tables_kernel(at_ref, tables):
    shape = (BLK, 128)
    feature = lax.broadcasted_iota(jnp.int32, shape, 1) % HDIM
    exponent = (feature % 8).astype(F32) * (2.0 / ROT)
    inverse = jnp.exp(exponent * -math.log(10000.0))
    for block in range(2):
        spot = at_ref[4] * (2 * BLK) + block * BLK + lax.broadcasted_iota(jnp.int32, shape, 0)
        angle = spot.astype(F32) * inverse
        sine = jnp.sin(angle)
        tables[0, block] = jnp.where(feature < ROT, jnp.cos(angle), 1.0)
        tables[1, block] = jnp.where(feature < ROT // 2, -sine, 0.0)
        tables[2, block] = jnp.where((feature >= ROT // 2) & (feature < ROT), sine, 0.0)


def turn_lanes(pair, cos, sin_up, sin_down):
    return pair * cos + pltpu.roll(pair, 120, 1) * sin_up + pltpu.roll(pair, 8, 1) * sin_down


def project_kernel(at_ref, *refs):
    tokens, mixes = refs[0:4], refs[4:8]
    tables = refs[8]
    sent, mix_out, dense_out, vec_out = refs[9:13]
    x, core = at_ref[0], at_ref[1]
    hi, lo = x // 2, x % 2
    quarters = (2 * hi + core, 2 * (1 - hi) + core, 2 * hi + 1 - core, 2 * (1 - hi) + 1 - core)
    for w, piece in zip(quarters, mixes):
        cols = pl.ds(pl.multiple_of(w * 256, 256), 256)
        mix_out[cols, :] = piece[0:256, 0:768]
        if piece.shape[0] == 272:
            vec_out[0:16, cols] = piece[256:272, 0:256].astype(F32)
        else:
            vec_out[0:16, cols] = piece[0:16, 768:1024].astype(F32)

    @pl.when(core == lo)
    def _():
        dense_out[...] = mixes[0][512:768, :]

    @pl.when(core != lo)
    def _():
        dense_out[...] = mixes[2][512:768, :]

    for j in range(3):
        n = 4 * j + x
        row = vec_out[6:9, pl.ds(pl.multiple_of((n // 3) * 256, 256), 256)]
        keep = lax.broadcasted_iota(jnp.int32, (3, 256), 0) == n % 3
        vec_out[16:17, 256 * j : 256 * j + 256] = jnp.sum(
            jnp.where(keep, row, 0.0), 0, keepdims=True
        )
    for j in range(4):
        vec_out[17:18, 256 * j : 256 * j + 256] = vec_out[
            9 + j : 10 + j, pl.ds(pl.multiple_of(x * 256, 256), 256)
        ]
    gain1, shift1 = vec_out[0:1, :], vec_out[1:2, :]
    bias = vec_out[16:17, 0:768]
    lane = lax.broadcasted_iota(jnp.int32, (BLK, 128), 1)
    left = lane < HDIM
    for j in range(4):
        chip = lax.bitwise_xor(x, TREE[j])
        to_hi, to_lo = chip // 2, chip % 2
        normal, _ = normalize(tokens[j][0:BLK, :].astype(F32))
        low1 = (normal * gain1 + shift1).astype(BF16)
        grad = tokens[j][BLK : 2 * BLK, :]
        mixed = dot(low1, mix_out[...]) + bias
        d_merged = dot_t(grad, dense_out[...])
        cos, sin_up, sin_down = tables[0, to_lo], tables[1, to_lo], tables[2, to_lo]
        for h in range(2):
            at = slice(128 * h, 128 * h + 128)
            q = turn_lanes(mixed[:, 0:256][:, at], cos, sin_up, sin_down)
            k = turn_lanes(mixed[:, 256:512][:, at], cos, sin_up, sin_down)
            v = mixed[:, 512:768][:, at]
            dm = d_merged[:, at]
            for side in range(2):
                if side == 0:
                    kv = jnp.where(left, k, pltpu.roll(v, 64, 1)).astype(BF16)
                    qd = jnp.where(left, q, pltpu.roll(dm, 64, 1)).astype(BF16)
                else:
                    kv = jnp.where(left, pltpu.roll(k, 64, 1), v).astype(BF16)
                    qd = jnp.where(left, pltpu.roll(q, 64, 1), dm).astype(BF16)
                i = 2 * h + side
                for half in range(2):
                    sent[i, to_hi, half, to_lo, 0:BLK, :] = kv
                    sent[i, to_hi, half, to_lo, BLK : BLK + HALF, :] = qd[
                        HALF * half : HALF * half + HALF
                    ]


def project(at, tokens, mixes, tables):
    outs = (
        struct((4, 2, 2, 2, BLK + HALF, 128)),
        struct((D, 768)),
        struct((256, D)),
        struct((24, D), F32),
    )
    return call(project_kernel, at, (*tokens, *mixes, tables), outs, 0.1)


def mlp_kernel(at_ref, *refs):
    tokens, vec, ups, downs = refs[0:4], refs[4], refs[5:9], refs[9:11]
    normal_out, norm1_t, g_out, d_norm2, given, kept = refs[11:17]
    feed_sent, feed_own, sums = refs[17:20], *refs[20:22]
    norm1, norm2, norm2_t, hidden, hidden_t, d_pre, up, down = refs[22:30]
    x, core = at_ref[0], at_ref[1]
    hi, lo = x // 2, x % 2
    quarters = (2 * hi + core, 2 * (1 - hi) + core, 2 * hi + 1 - core, 2 * (1 - hi) + 1 - core)
    for w, piece in zip(quarters, ups):
        rows = slice(256, 512) if piece.shape[0] > 256 else slice(0, 256)
        up[pl.ds(pl.multiple_of(w * 256, 256), 256), :] = piece[rows, :]

    @pl.when(core == lo)
    def _():
        down[...] = downs[0][...]

    @pl.when(core != lo)
    def _():
        down[...] = downs[1][...]

    for j in range(4):
        rows = slice(BLK * j, BLK * j + BLK)
        normal, _ = normalize(tokens[j][0:BLK, :].astype(F32))
        normal_out[rows, :] = normal.astype(BF16)
        norm1[rows, :] = (normal * vec[0:1, :] + vec[1:2, :]).astype(BF16)
        norm2[rows, :] = (normal * vec[2:3, :] + vec[3:4, :]).astype(BF16)
        g_out[rows, :] = tokens[j][BLK : 2 * BLK, :]
    for k in range(4):
        cols = slice(256 * k, 256 * k + 256)
        pre = dot(norm2[...], up[:, cols]) + vec[17:18, cols]
        below = 0.5 + 0.5 * lax.erf(pre * 0.5**0.5)
        hidden[:, cols] = (pre * below).astype(BF16)
        bell = jnp.exp(-0.5 * pre * pre) * (0.5 / math.pi) ** 0.5
        dp = (dot_t(g_out[...], down[cols, :]) * (below + pre * bell)).astype(BF16)
        d_pre[:, cols] = dp
        sums[:, cols] = jnp.sum(dp.astype(F32), 0, keepdims=True)
    d_norm2[...] = dot_t(d_pre[...], up[...]).astype(BF16)
    for j in range(4):
        feed = dot(hidden[BLK * j : BLK * j + BLK, :], down[...])
        if j == 0:
            feed_own[...] = feed
        else:
            feed_sent[j - 1][...] = feed.astype(BF16)
    for k in range(8):
        at = slice(128 * k, 128 * k + 128)
        norm1_t[at, :] = norm1[:, at].T
        norm2_t[at, :] = norm2[:, at].T
        hidden_t[at, :] = hidden[:, at].T
    for c, out in ((1 - core, given), (core, kept)):
        for w in range(2):
            rows = pl.ds(pl.multiple_of(512 * w + 256 * c, 256), 256)
            part = dot(norm2_t[rows, :], d_pre[...])
            out[:, 16 * w : 16 * w + 16, :] = part.reshape(16, 16, 1024).astype(out.dtype)
        part = dot(hidden_t[pl.ds(pl.multiple_of(512 * c, 512), 512), :], g_out[...])
        out[:, 32:64, :] = part.reshape(16, 32, 1024).astype(out.dtype)


def feed_forward(at, *operands):
    outs = (
        struct((768, D)),
        struct((D, 768)),
        struct((768, D)),
        struct((768, D)),
        struct((16, 64, 1024)),
        struct((16, 64, 1024)),
        struct((BLK, D)),
        struct((BLK, D)),
        struct((BLK, D)),
        struct((BLK, D), F32),
        struct((1, 1024), F32),
    )
    rows, columns = pltpu.VMEM((768, D), BF16), pltpu.VMEM((D, 768), BF16)
    square = pltpu.VMEM((D, 1024), BF16)
    scratch = (rows, rows, columns, rows, columns, rows, square, square)
    return call(mlp_kernel, at, operands, outs, 0.1, scratch)


def add_kernel(at_ref, a, b, out):
    out[...] = (a[...].astype(F32) + b[...].astype(F32)).astype(out.dtype)


def add(at, a, b):
    return call(add_kernel, at, (a, b), (struct(a.shape),), 0.1)[0]


def unpack_kernel(at_ref, back, tables, norm1_t, g_ref, d_mixed, merged, given, kept):
    core = at_ref[1]
    lane = lax.broadcasted_iota(jnp.int32, (BLK, 128), 1)
    left = lane < HDIM
    for j in range(4):
        if True:
            chip = lax.bitwise_xor(at_ref[0], TREE[j])
            hi, lo = chip // 2, chip % 2
            cos, sin_up, sin_down = tables[0, lo], tables[1, lo], tables[2, lo]
            rows = slice(j * BLK, j * BLK + BLK)
            for h in range(2):
                kv, qo = [], []
                for i in (2 * h, 2 * h + 1):
                    kv.append(
                        back[i, hi, 0, lo, 0:BLK, :].astype(F32)
                        + back[i, hi, 1, lo, 0:BLK, :].astype(F32)
                    )
                    qo.append(
                        jnp.concatenate(
                            [back[i, hi, s, lo, BLK : BLK + HALF, :] for s in range(2)], 0
                        ).astype(F32)
                    )
                dq = jnp.where(left, qo[0], pltpu.roll(qo[1], 64, 1))
                out = jnp.where(left, pltpu.roll(qo[0], 64, 1), qo[1])
                dk = jnp.where(left, kv[0], pltpu.roll(kv[1], 64, 1))
                dv = jnp.where(left, pltpu.roll(kv[0], 64, 1), kv[1])
                dq = turn_lanes(dq, cos, -sin_up, -sin_down)
                dk = turn_lanes(dk, cos, -sin_up, -sin_down)
                for k, value in enumerate((dq, dk, dv)):
                    at = 256 * k + 128 * h
                    d_mixed[rows, at : at + 128] = value.astype(BF16)
                merged[rows, 128 * h : 128 * h + 128] = out.astype(BF16)
    merged_t = merged[...].astype(F32).T.astype(BF16)
    dense = dot(merged_t, g_ref[...])
    for c, out in ((1 - core, given), (core, kept)):
        for hi in range(2):
            rows = pl.ds(pl.multiple_of(512 * hi + 256 * c, 256), 256)
            part = dot(norm1_t[rows, :], d_mixed[...])
            out[:, 16 * hi : 16 * hi + 16, 0:768] = part.reshape(16, 16, 768).astype(out.dtype)
        half = jnp.where(c == 0, dense[0:128], dense[128:256]).astype(out.dtype)
        for i in range(4):
            for j in range(4):
                out[4 * i + j, :, 768:1024] = half[32 * i : 32 * i + 32, 256 * j : 256 * j + 256]


def unpack(at, *operands):
    outs = (
        struct((768, 768)),
        struct((768, 256)),
        struct((16, 32, 1024)),
        struct((16, 32, 1024)),
    )
    return call(unpack_kernel, at, operands, outs, 100)


def finish_kernel(
    at_ref, d_mixed, merged, mix, d_norm2, normal, g_own, up_sum, vec, *refs
):
    parts, e_own, merged_own, sums = refs[0:3], *refs[3:6]
    gain1, gain2 = vec[0:1, :], vec[2:3, :]
    totals = [jnp.zeros((1, D), F32) for _ in range(4)]
    for j in range(4):
        rows = slice(j * BLK, j * BLK + BLK)
        d1 = dot_t(d_mixed[rows, :], mix[...])
        d2 = d_norm2[rows, :].astype(F32)
        n = normal[rows, :].astype(F32)
        e = gain1 * d1 + gain2 * d2
        if j == 0:
            e_own[...] = e
            merged_own[...] = merged[rows, :]
        else:
            parts[j - 1][0:BLK, :] = e.astype(BF16)
            heads = merged[rows, :]
            for k in range(4):
                cols = slice(256 * k, 256 * k + 256)
                parts[j - 1][BLK : BLK + 48, cols] = heads[48 * k : 48 * k + 48]
        for k, value in enumerate((d1 * n, d1, d2 * n, d2)):
            totals[k] = totals[k] + jnp.sum(value, 0, keepdims=True)
    for k in range(4):
        sums[k : k + 1, :] = totals[k].astype(BF16)
    sums[4:5, :] = jnp.sum(g_own[...].astype(F32), 0, keepdims=True).astype(BF16)
    sums[5:6, :] = jnp.zeros((1, D), BF16)
    sums[5:6, 0:768] = jnp.sum(d_mixed[...].astype(F32), 0, keepdims=True).astype(BF16)
    sums[6:7, :] = up_sum[...].astype(BF16)
    sums[7:8, :] = jnp.zeros((1, D), BF16)


def finish(at, *operands):
    outs = (
        struct((BLK + 48, D)),
        struct((BLK + 48, D)),
        struct((BLK + 48, D)),
        struct((BLK, D), F32),
        struct((BLK, 256)),
        struct((8, D)),
    )
    return call(finish_kernel, at, operands, outs, 0.1)


def tokens_kernel(at_ref, x_ref, g_ref, *refs):
    e_own, merged_own, feed_own = refs[0:3]
    late, feeds = refs[3:6], refs[6:9]
    dense, vec, out, grad_in = refs[9:13]
    x = at_ref[0]
    tokens = x_ref[...].astype(F32)
    total = tokens + vec[4:5, :] + vec[5:6, :] + feed_own[...]
    total = total + dot(merged_own[...], dense[x])
    e = e_own[...]
    for j in range(3):
        total = total + feeds[j][...].astype(F32)
        heads = jnp.concatenate(
            [late[j][BLK : BLK + 48, 256 * k : 256 * k + 256] for k in range(4)], 0
        )
        total = total + dot(heads, dense[lax.bitwise_xor(x, TREE[j + 1])])
        e = e + late[j][0:BLK, :].astype(F32)
    out[...] = total.astype(BF16)
    normal, inv = normalize(tokens)
    grad_in[...] = (g_ref[...].astype(F32) + norm_back(normal, inv, e)).astype(BF16)


def own_tokens(at, *operands):
    return call(tokens_kernel, at, operands, (struct((BLK, D)),) * 2, 0.1)


def join_kernel(at_ref, own, beside, across, far, sibling, aside, out):
    hi, lo, core = at_ref[0] // 2, at_ref[0] % 2, at_ref[1]
    rows = pl.ds(pl.multiple_of(hi * 16, 16), 16)
    ring = (own, beside, across, far)
    ff = own.shape[0] == 64
    if ff:
        box, places = (slice(32, 64), slice(0, 1024)), ((64, 0), (96, 0))
        width = 1024
    else:
        box, places = (slice(0, 32), slice(768, 1024)), ((0, 768), (32, 768))
        width = 768
    for j in range(4):
        value = ring[j][rows, 0:width]
        for i in range(16):
            if i < out.shape[0]:
                out[i, 16 * j : 16 * j + 16, 0:width] = value
    for (row, column), near, off in zip(places, (own, sibling), (beside, aside)):
        value = jnp.where(core == lo, near[box], off[box])
        for i in range(out.shape[0]):
            out[i, row : row + 32, column : column + value.shape[1]] = value
    if not ff:
        chips = [r[32:40, :].astype(F32) for r in ring]
        vec = jnp.concatenate(
            [sum(c[0:5] for c in chips)]
            + [c[5:6] for c in chips]
            + [c[6:7] for c in chips]
            + [jnp.zeros((3, 1024), F32)],
            0,
        ).astype(BF16)
        for i in range(16):
            out[i, 64:80, :] = vec


def join(at, own, count):
    parts = [send(own, p) for p in (NEXT, CROSS, FAR, CORE, ASIDE)]
    rows = 128 if own.shape[0] == 64 else 80
    return call(join_kernel, at, (own, *parts), (struct((count, rows, 1024)),), 0.1)[0]


def place_ff_kernel(at_ref, sums, up_out, down_out):
    x, core = at_ref[0], at_ref[1]
    for j in range(4):
        cols = pl.ds(pl.multiple_of(lax.bitwise_xor(x, TREE[j]) * 1024, 1024), 1024)
        up_out[:, cols] = sums[:, 16 * j : 16 * j + 16, :].reshape(256, 1024).astype(F32)
    for side, at in ((core, 64), (1 - core, 96)):
        rows = pl.ds(pl.multiple_of(side * 512, 512), 512)
        down_out[rows, :] = sums[:, at : at + 32, :].reshape(512, 1024).astype(F32)


def place_attn_kernel(at_ref, sums, mix_out, dense_out, *vec_outs):
    x, core = at_ref[0], at_ref[1]
    for j in range(4):
        chip = lax.bitwise_xor(x, TREE[j])
        for k in range(3):
            cols = pl.ds(pl.multiple_of(k * 1024 + chip * 256, 256), 256)
            part = sums[:, 16 * j : 16 * j + 16, 256 * k : 256 * k + 256]
            mix_out[:, cols] = part.reshape(256, 256).astype(F32)
    for side, at in ((core, 0), (1 - core, 32)):
        for i in range(4):
            rows = pl.ds(pl.multiple_of(side * 128 + i * 32, 32), 32)
            for j in range(4):
                part = sums[4 * i + j, at : at + 32, 768:1024]
                dense_out[rows, 256 * j : 256 * j + 256] = part.astype(F32)
    total = jnp.zeros((16, 1024), F32)
    for i in range(16):
        total = total + sums[i, 64:80, :].astype(F32)
    quarter = 2 * (x // 2) + core
    scratch, vec_outs = vec_outs[-1], vec_outs[:-1]
    scratch[0:16, :] = total
    cols = pl.ds(pl.multiple_of(quarter * 256, 256), 256)
    for k in range(5):
        vec_outs[k][...] = scratch[k : k + 1, cols]
    for j in range(4):
        chip = lax.bitwise_xor(x, TREE[j])
        scratch[pl.ds(16 + chip, 1), :] = scratch[5 + j : 6 + j, :]
        scratch[pl.ds(20 + chip, 1), :] = scratch[9 + j : 10 + j, :]
    for k in range(3):
        n = 3 * quarter + k
        row = scratch[pl.ds(16 + n % 4, 1), pl.ds(pl.multiple_of(n // 4 * 256, 256), 256)]
        vec_outs[5][:, 256 * k : 256 * k + 256] = row
    vec_outs[6][...] = scratch[pl.ds(20 + quarter, 1), :]


def shards(
    inputs,
    first_gain,
    first_bias,
    second_gain,
    second_bias,
    mix_weight,
    mix_bias,
    dense_weight,
    dense_bias,
    up_weight,
    up_bias,
    down_weight,
    down_bias,
    grad_out,
):
    ctx, wa = lax.axis_index("ctx"), lax.axis_index("wa")
    lo, yz, hi, core = ctx % 2, ctx // 2, wa // 2, wa % 2
    x = 2 * hi + lo
    at = jnp.stack([x, core, yz // 4, yz % 4, yz])

    both = jnp.concatenate([inputs[0], grad_out[0]], 0)
    beside, across = send(both, NEXT), send(both, CROSS)
    tokens = (both, beside, across, send(after(across, beside), NEXT))
    small, filled = 0, 0
    for v in (
        first_gain,
        first_bias,
        second_gain,
        second_bias,
        dense_bias,
        down_bias,
        mix_bias,
        up_bias,
    ):
        rows = v.shape[0] // 256
        small = small + jnp.pad(v.reshape(rows, 256), ((filled, 16 - filled - rows), (0, 0)))
        filled += rows
    own, mix_cross, up_cross = call(
        pack_kernel,
        at,
        (mix_weight, up_weight, dense_weight, small),
        (struct((768, 1024)), struct((272, 768)), struct((256, 1024))),
        0.1,
    )
    tables = call(tables_kernel, at, (), (struct((3, 2, BLK, 128), F32),), 0.1)[0]
    mix_got = send(after(mix_cross, beside, across), CROSS)
    other = send(own, CORE)
    mix_other_got = send(mix_got, CORE)
    up_got = send(after(up_cross, across, mix_got), CROSS)
    up_other_got = send(up_got, CORE)
    down_other = send(after(down_weight, across), CORE)

    sent, mix, dense, vec = project(at, tokens, (own, mix_got, other, mix_other_got), tables)
    held = swap(sent.reshape(16, 2 * 288, 128)).reshape(32, 288, 128)

    up_other_got = send(after(up_got, sent), CORE)
    normal, norm1_t, token_g, d_norm2, given, kept, *feed_sent, feed_own, up_sum = feed_forward(
        at, *tokens, vec, own, up_got, other, up_other_got, down_weight, down_other
    )
    ff_sums = add(at, kept, send(given, CORE))
    ff_mine = swap(after(ff_sums, held))
    back = attention((yz % 2).reshape(1), after(held, ff_sums)).reshape(16, 2 * 288, 128)
    ff_mine = jnp.sum(after(ff_mine, back).astype(F32), 0).astype(BF16)
    ff_all = join(at, ff_mine, 1)[0]
    ff_all = lax.all_gather(ff_all, "ctx", axis=0, axis_index_groups=YZ, tiled=False)

    feeds = [send(feed_sent[j], (NEXT, CROSS, FAR)[j]) for j in range(3)]
    dense_got = send(after(dense_weight, up_got), CROSS)
    back = swap(after(back, dense_got, *feeds))
    dense_other_got = send(after(dense_got, ff_mine), CORE)
    near = jnp.where(
        core == 0, jnp.stack([dense_weight, other[512:]]), jnp.stack([other[512:], dense_weight])
    )
    away = jnp.where(
        core == 0,
        jnp.stack([dense_got, dense_other_got]),
        jnp.stack([dense_other_got, dense_got]),
    )
    dense_all = jnp.where(hi == 0, jnp.concatenate([near, away]), jnp.concatenate([away, near]))
    back = after(back, dense_all)

    d_mixed, merged, given, kept = unpack(
        at, back.reshape(4, 2, 2, 2, 288, 128), tables, norm1_t, token_g
    )
    attn_sums = add(at, kept, send(given, CORE))
    attn_mine = swap(attn_sums)
    *parts, e_own, merged_own, vectors = finish(
        at, after(d_mixed, attn_sums), merged, mix, d_norm2, normal, grad_out[0], up_sum, vec
    )
    vectors = add(at, vectors, send(vectors, CORE))
    late = [send(parts[j], (NEXT, CROSS, FAR)[j]) for j in range(3)]
    attn_mine = jnp.sum(attn_mine.astype(F32), 0).astype(BF16)
    gathered = join(at, jnp.concatenate([attn_mine, vectors], 0), 16)
    gathered = swap(gathered)
    grad_up, grad_down = call(
        place_ff_kernel, at, (ff_all,), (struct((256, FF), F32), struct((1024, D), F32)), 0.1
    )
    output, grad_in = own_tokens(
        at, inputs[0], grad_out[0], e_own, merged_own, feed_own, *late, *feeds, dense_all, vec
    )
    gathered = after(gathered, output, grad_up)
    row = struct((1, 256), F32)
    grad_mix, grad_dense, *rest = call(
        place_attn_kernel,
        at,
        (gathered,),
        (struct((256, 3 * D), F32), struct((256, D), F32))
        + (row,) * 5
        + (struct((1, 768), F32), struct((1, 1024), F32)),
        0.1,
        [pltpu.VMEM((24, 1024), F32)],
    )
    rest = [r.reshape(-1) for r in rest]
    return (
        output[None],
        grad_in[None],
        rest[0],
        rest[1],
        rest[2],
        rest[3],
        grad_mix,
        rest[5],
        grad_dense,
        rest[4],
        grad_up,
        rest[6],
        grad_down,
        rest[4],
    )


def solution(mesh):
    rows, vec, tokens = P("wa", None), P("wa"), P("wa", "ctx", None)
    return jax.shard_map(
        shards,
        mesh=mesh,
        in_specs=(tokens, vec, vec, vec, vec, rows, vec, rows, vec, rows, vec, rows, vec, tokens),
        out_specs=(
            tokens,
            tokens,
            vec,
            vec,
            vec,
            vec,
            rows,
            vec,
            rows,
            vec,
            rows,
            vec,
            rows,
            vec,
        ),
        check_vma=False,
    )
```

```python
import functools
import math

import jax
import jax.numpy as jnp
from jax import lax
from jax.experimental import pallas as pl
from jax.experimental.pallas import tpu as pltpu
from jax.sharding import PartitionSpec as P

D = 1024
HEADS = 16
HDIM = 64
ROT = 16
FF = 4096
BLK = 192
HALF = 96
EPS = 1e-05
F32 = jnp.float32
BF16 = jnp.bfloat16


def attention_kernel(par_ref, x_ref, out_ref, kvt, s_buf, p_buf, dkv, *, tq):
    kc = 2 * tq
    pairs = x_ref.shape[0]
    step = kc // (2 * BLK)
    groups = pairs // step
    par = par_ref[0]

    def keys(c, first=0, count=step):
        return x_ref[pl.ds(c * step + first, count), 0 : 2 * BLK, :].reshape(count * 2 * BLK, 128)

    def turn(c, carry):
        kvt[:, pl.ds(pl.multiple_of(c * kc, kc), kc)] = keys(c).T
        dkv[pl.ds(c * kc, kc), :] = jnp.zeros((kc, 128), F32)
        return carry

    lax.fori_loop(0, groups, turn, 0)
    row = lax.broadcasted_iota(jnp.int32, (128, tq), 0)
    lane = lax.broadcasted_iota(jnp.int32, (tq, 128), 1)
    q_idx = lax.broadcasted_iota(jnp.int32, (1, tq), 1)
    q_tok = (q_idx // HALF) * BLK + par * HALF + q_idx % HALF
    zero = jnp.zeros((), F32)
    own = ((0, tq, 0), (tq, tq, tq // 2))

    def widen(old, new, qs):
        return new if qs == 0 else jnp.concatenate([old[:, :qs], new], 1)

    def group(t, carry):
        qd_rows = x_ref[pl.ds(t * step, step), 2 * BLK : 3 * BLK, :].reshape(tq, 128)
        qd_t = qd_rows.astype(F32).T
        q_t = jnp.where(row < HDIM, qd_t * 0.125, zero).astype(BF16)

        def block(c, first, count):
            return pl.ds(pl.multiple_of(c * kc + first, count), count)

        def scores(c, part, top):
            first, count, qs = part or (0, kc, 0)
            at = block(c, first, count)
            kv = keys(c, first // (2 * BLK), count // (2 * BLK))
            s = jnp.dot(kv, q_t[:, qs:], preferred_element_type=F32)
            if part:
                k_tok = first + lax.broadcasted_iota(jnp.int32, (count, 1), 0)
                s = jnp.where(k_tok <= q_tok[:, qs:], s, -1e30)
            s_buf[at, qs:] = s
            high = jnp.max(s.reshape(count // 8, 8, tq - qs), 0)
            return widen(top, jnp.maximum(top[:, qs:], high), qs)

        top = jnp.full((8, tq), -1e30, F32)
        top = lax.fori_loop(0, t, lambda c, m: scores(c, None, m), top)
        for part in own:
            top = scores(t, part, top)
        top = jnp.max(top, 0, keepdims=True)

        def weigh(c, part, state):
            first, count, qs = part or (0, kc, 0)
            at = block(c, first, count)
            total, out_t = state
            p = jnp.exp(s_buf[at, qs:] - top[:, qs:])
            new_total = total[:, qs:] + jnp.sum(p.reshape(count // 8, 8, tq - qs), 0)
            p_low = p.astype(BF16)
            p_buf[at, qs:] = p_low
            new_out = out_t[:, qs:] + jnp.dot(kvt[HDIM:, at], p_low, preferred_element_type=F32)
            return widen(total, new_total, qs), widen(out_t, new_out, qs)

        state = (jnp.zeros((8, tq), F32), jnp.zeros((HDIM, tq), F32))
        state = lax.fori_loop(0, t, lambda c, s: weigh(c, None, s), state)
        for part in own:
            state = weigh(t, part, state)
        total, out_t = state
        inv = 1.0 / jnp.sum(total, 0, keepdims=True)
        out_t = out_t * inv
        do_t = (qd_t[HDIM:] * inv).astype(BF16)
        delta = jnp.sum(do_t.astype(F32) * out_t, 0, keepdims=True)
        do_full = jnp.concatenate([jnp.zeros((HDIM, tq), BF16), do_t], 0)
        do_rows = do_full.astype(F32).T.astype(BF16)
        q_rows = jnp.where(lane < HDIM, qd_rows.astype(F32) * 0.125, zero).astype(BF16)

        def back(c, part, dq_t):
            first, count, qs = part or (0, kc, 0)
            at = block(c, first, count)
            kv = keys(c, first // (2 * BLK), count // (2 * BLK))
            dp = jnp.dot(kv, do_full[:, qs:], preferred_element_type=F32)
            p_low = p_buf[at, qs:]
            ds = (p_low.astype(F32) * (dp - delta[:, qs:])).astype(BF16)
            dkv[at, :] += jnp.dot(p_low, do_rows[qs:], preferred_element_type=F32) + jnp.dot(
                ds, q_rows[qs:], preferred_element_type=F32
            )
            new = dq_t[:, qs:] + jnp.dot(kvt[:HDIM, at], ds, preferred_element_type=F32)
            return widen(dq_t, new, qs)

        dq_t = lax.fori_loop(0, t, lambda c, d: back(c, None, d), jnp.zeros((HDIM, tq), F32))
        for part in own:
            dq_t = back(t, part, dq_t)
        out = jnp.concatenate([dq_t * 0.125, out_t], 0).T.astype(BF16)
        out_ref[pl.ds(t * step, step), 2 * BLK : 3 * BLK, :] = out.reshape(step, BLK, 128)
        return carry

    lax.fori_loop(0, groups, group, 0)

    def drain(c, carry):
        rows = dkv[pl.ds(c * kc, kc), :].astype(BF16)
        out_ref[pl.ds(c * step, step), 0 : 2 * BLK, :] = rows.reshape(step, 2 * BLK, 128)
        return carry

    lax.fori_loop(0, groups, drain, 0)


def attention(par, x, tq=768):
    n_keys = x.shape[0] * 2 * BLK
    whole = pl.BlockSpec(x.shape, lambda i: (0, 0, 0), pipeline_mode=pl.Buffered(1))
    return pl.pallas_call(
        functools.partial(attention_kernel, tq=tq),
        grid=(1,),
        out_shape=jax.ShapeDtypeStruct(x.shape, BF16),
        in_specs=[pl.BlockSpec(memory_space=pltpu.SMEM), whole],
        out_specs=whole,
        scratch_shapes=[
            pltpu.VMEM((128, n_keys), BF16),
            pltpu.VMEM((n_keys, tq), F32),
            pltpu.VMEM((n_keys, tq), BF16),
            pltpu.VMEM((n_keys, 128), F32),
        ],
        compiler_params=pltpu.CompilerParams(vmem_limit_bytes=63 * 2**20),
        cost_estimate=cost(46),
    )(par, x)


def cost(micros):
    return pl.CostEstimate(flops=int(micros * 1.1e9), bytes_accessed=10**5, transcendentals=0)


def normalize(values):
    centred = values - jnp.mean(values, -1, keepdims=True)
    spread = jnp.mean(centred * centred, -1, keepdims=True)
    inv = lax.rsqrt(spread + EPS)
    return centred * inv, inv


def norm_back(normal, inv, e):
    return inv * (
        e
        - jnp.mean(e, -1, keepdims=True)
        - normal * jnp.mean(e * normal, -1, keepdims=True)
    )


def dot(a, b):
    return jnp.dot(a, b, preferred_element_type=F32)


def dot_t(a, b):
    return lax.dot_general(a, b, (((1,), (1,)), ((), ())), preferred_element_type=F32)


def t_dot(a, b):
    return lax.dot_general(a, b, (((0,), (0,)), ((), ())), preferred_element_type=F32)


AX = ("ctx", "wa")
YZ = [[2 * i + lo for i in range(16)] for lo in range(2)]
SMEM = pl.BlockSpec(memory_space=pltpu.SMEM)


def route(move):
    pairs = []
    for ctx in range(32):
        for wa in range(4):
            to_x, y, z, core = move(wa // 2 * 2 + ctx % 2, ctx // 8, ctx // 2 % 4, wa % 2)
            to_ctx, to_wa = y * 8 + z * 2 + to_x % 2, to_x // 2 * 2 + core
            pairs.append((ctx * 4 + wa, to_ctx * 4 + to_wa))
    return pairs


CORE = route(lambda x, y, z, c: (x, y, z, 1 - c))
CROSS = route(lambda x, y, z, c: (3 - x, y, z, c))
FAR = route(lambda x, y, z, c: (x ^ 2, y, z, c))
NEXT = route(lambda x, y, z, c: (x ^ 1, y, z, c))
ASIDE = route(lambda x, y, z, c: (x ^ 1, y, z, 1 - c))
TREE = (0, 1, 3, 2)


def send(value, pairs):
    return lax.ppermute(value, AX, pairs)


def pick(array, index, axis=0):
    return lax.dynamic_index_in_dim(array, index, axis, keepdims=False)


def after(value, *first):
    return lax.optimization_barrier((value, *first))[0]


def swap(pieces):
    return lax.all_to_all(pieces, "ctx", 0, 0, axis_index_groups=YZ, tiled=True)


def call(kernel, at, operands, outs, micros, scratch=()):
    def whole(a):
        return pl.BlockSpec(a.shape, lambda i: (0,) * len(a.shape), pipeline_mode=pl.Buffered(1))

    return pl.pallas_call(
        kernel,
        grid=(1,),
        out_shape=tuple(outs),
        in_specs=[SMEM] + [whole(a) for a in operands],
        out_specs=tuple(whole(a) for a in outs),
        scratch_shapes=list(scratch),
        compiler_params=pltpu.CompilerParams(vmem_limit_bytes=63 * 2**20),
        cost_estimate=cost(micros),
    )(at, *operands)


def struct(shape, dtype=BF16):
    return jax.ShapeDtypeStruct(shape, dtype)


def pack_kernel(at_ref, mix_ref, up_ref, dense_ref, small_ref, own, mix_cross, up_cross):
    for k, (mix_out, up_out) in enumerate(((own.at[0:256], own.at[256:512]), (mix_cross, up_cross))):
        q = at_ref[0] if k == 0 else 3 - at_ref[0]
        for j in range(3):
            cols = pl.ds(pl.multiple_of(q * 256 + j * 1024, 256), 256)
            mix_out[0:256, 256 * j : 256 * j + 256] = mix_ref[:, cols]
        if k == 0:
            mix_out[0:16, 768:1024] = small_ref[...]
            mix_out[16:256, 768:1024] = jnp.zeros((240, 256), BF16)
        else:
            mix_out[256:272, 0:256] = small_ref[...]
            mix_out[256:272, 256:768] = jnp.zeros((16, 512), BF16)
        up_out[...] = up_ref[:, pl.ds(pl.multiple_of(q * 1024, 1024), 1024)]
    own[512:768, :] = dense_ref[...]


def tables_kernel(at_ref, tables):
    shape = (BLK, 128)
    feature = lax.broadcasted_iota(jnp.int32, shape, 1) % HDIM
    exponent = (feature % 8).astype(F32) * (2.0 / ROT)
    inverse = jnp.exp(exponent * -math.log(10000.0))
    for block in range(2):
        spot = at_ref[4] * (2 * BLK) + block * BLK + lax.broadcasted_iota(jnp.int32, shape, 0)
        angle = spot.astype(F32) * inverse
        sine = jnp.sin(angle)
        tables[0, block] = jnp.where(feature < ROT, jnp.cos(angle), 1.0)
        tables[1, block] = jnp.where(feature < ROT // 2, -sine, 0.0)
        tables[2, block] = jnp.where((feature >= ROT // 2) & (feature < ROT), sine, 0.0)


def turn_lanes(pair, cos, sin_up, sin_down):
    return pair * cos + pltpu.roll(pair, 120, 1) * sin_up + pltpu.roll(pair, 8, 1) * sin_down


def project_kernel(at_ref, *refs):
    tokens, mixes = refs[0:4], refs[4:8]
    tables = refs[8]
    sent, vec_out, mix_out, dense_out = refs[9:13]
    x, core = at_ref[0], at_ref[1]
    hi, lo = x // 2, x % 2
    quarters = (2 * hi + core, 2 * (1 - hi) + core, 2 * hi + 1 - core, 2 * (1 - hi) + 1 - core)
    for w, piece in zip(quarters, mixes):
        cols = pl.ds(pl.multiple_of(w * 256, 256), 256)
        mix_out[cols, :] = piece[0:256, 0:768]
        if piece.shape[0] == 272:
            vec_out[0:16, cols] = piece[256:272, 0:256].astype(F32)
        else:
            vec_out[0:16, cols] = piece[0:16, 768:1024].astype(F32)

    @pl.when(core == lo)
    def _():
        dense_out[...] = mixes[0][512:768, :]

    @pl.when(core != lo)
    def _():
        dense_out[...] = mixes[2][512:768, :]

    for j in range(3):
        n = 4 * j + x
        row = vec_out[6:9, pl.ds(pl.multiple_of((n // 3) * 256, 256), 256)]
        keep = lax.broadcasted_iota(jnp.int32, (3, 256), 0) == n % 3
        vec_out[16:17, 256 * j : 256 * j + 256] = jnp.sum(
            jnp.where(keep, row, 0.0), 0, keepdims=True
        )
    for j in range(4):
        vec_out[17:18, 256 * j : 256 * j + 256] = vec_out[
            9 + j : 10 + j, pl.ds(pl.multiple_of(x * 256, 256), 256)
        ]
    gain1, shift1 = vec_out[0:1, :], vec_out[1:2, :]
    bias = vec_out[16:17, 0:768]
    lane = lax.broadcasted_iota(jnp.int32, (BLK, 128), 1)
    left = lane < HDIM
    for j in range(4):
        chip = lax.bitwise_xor(x, TREE[j])
        to_hi, to_lo = chip // 2, chip % 2
        normal, _ = normalize(tokens[j][0:BLK, :].astype(F32))
        low1 = (normal * gain1 + shift1).astype(BF16)
        grad = tokens[j][BLK : 2 * BLK, :]
        mixed = dot(low1, mix_out[...]) + bias
        d_merged = dot_t(grad, dense_out[...])
        cos, sin_up, sin_down = tables[0, to_lo], tables[1, to_lo], tables[2, to_lo]
        for h in range(2):
            cols = slice(128 * h, 128 * h + 128)
            q = turn_lanes(mixed[:, 0:256][:, cols], cos, sin_up, sin_down)
            k = turn_lanes(mixed[:, 256:512][:, cols], cos, sin_up, sin_down)
            v = mixed[:, 512:768][:, cols]
            dm = d_merged[:, cols]
            for side in range(2):
                if side == 0:
                    kv = jnp.where(left, k, pltpu.roll(v, 64, 1)).astype(BF16)
                    qd = jnp.where(left, q, pltpu.roll(dm, 64, 1)).astype(BF16)
                else:
                    kv = jnp.where(left, pltpu.roll(k, 64, 1), v).astype(BF16)
                    qd = jnp.where(left, pltpu.roll(q, 64, 1), dm).astype(BF16)
                i = 2 * h + side
                for half in range(2):
                    at = pl.ds(pl.multiple_of(to_lo * BLK, BLK), BLK)
                    sent[i, to_hi, half, at, :] = kv
                    at = pl.ds(pl.multiple_of(2 * BLK + to_lo * HALF, HALF), HALF)
                    sent[i, to_hi, half, at, :] = qd[HALF * half : HALF * half + HALF]


def project(at, tokens, mixes, tables):
    outs = (struct((4, 2, 2, 3 * BLK, 128)), struct((24, D), F32))
    scratch = [pltpu.VMEM((D, 768), BF16), pltpu.VMEM((256, D), BF16)]
    return call(project_kernel, at, (*tokens, *mixes, tables), outs, 0.1, scratch)


def mlp_kernel(at_ref, *refs):
    tokens, vec, ups, downs, mixes = refs[0:4], refs[4], refs[5:9], refs[9:11], refs[11:13]
    normal_out, norm1_t, g_out, d_norm2, given, kept = refs[13:19]
    feed_sent, feed_own, sums, mix = refs[19:22], *refs[22:25]
    norm1, norm2, norm2_t, hidden, hidden_t, d_pre, up, down = refs[25:33]
    x, core = at_ref[0], at_ref[1]
    hi, lo = x // 2, x % 2
    quarters = (2 * hi + core, 2 * (1 - hi) + core, 2 * hi + 1 - core, 2 * (1 - hi) + 1 - core)
    for w, piece in zip(quarters, ups):
        rows = slice(256, 512) if piece.shape[0] > 256 else slice(0, 256)
        at = pl.ds(pl.multiple_of(w * 256, 256), 256)
        up[at, :] = piece[rows, :]
        if piece.shape[0] > 256:
            mix[at, :] = piece[0:256, 0:768]
    for w, piece in zip((quarters[1], quarters[3]), mixes):
        mix[pl.ds(pl.multiple_of(w * 256, 256), 256), :] = piece[0:256, :]

    @pl.when(core == lo)
    def _():
        down[...] = downs[0][...]

    @pl.when(core != lo)
    def _():
        down[...] = downs[1][...]

    for j in range(4):
        rows = slice(BLK * j, BLK * j + BLK)
        normal, _ = normalize(tokens[j][0:BLK, :].astype(F32))
        normal_out[rows, :] = normal.astype(BF16)
        norm1[rows, :] = (normal * vec[0:1, :] + vec[1:2, :]).astype(BF16)
        norm2[rows, :] = (normal * vec[2:3, :] + vec[3:4, :]).astype(BF16)
        g_out[rows, :] = tokens[j][BLK : 2 * BLK, :]
    for k in range(4):
        cols = slice(256 * k, 256 * k + 256)
        pre = dot(norm2[...], up[:, cols]) + vec[17:18, cols]
        below = 0.5 + 0.5 * lax.erf(pre * 0.5**0.5)
        hidden[:, cols] = (pre * below).astype(BF16)
        bell = jnp.exp(-0.5 * pre * pre) * (0.5 / math.pi) ** 0.5
        dp = (dot_t(g_out[...], down[cols, :]) * (below + pre * bell)).astype(BF16)
        d_pre[:, cols] = dp
        sums[:, cols] = jnp.sum(dp.astype(F32), 0, keepdims=True)
    d_norm2[...] = dot_t(d_pre[...], up[...]).astype(BF16)
    for j in range(4):
        feed = dot(hidden[BLK * j : BLK * j + BLK, :], down[...])
        if j == 0:
            feed_own[...] = feed
        else:
            feed_sent[j - 1][...] = feed.astype(BF16)
    for k in range(8):
        at = slice(128 * k, 128 * k + 128)
        norm1_t[at, :] = norm1[:, at].T
        norm2_t[at, :] = norm2[:, at].T
        hidden_t[at, :] = hidden[:, at].T
    for c, out in ((1 - core, given), (core, kept)):
        for w in range(2):
            rows = pl.ds(pl.multiple_of(512 * w + 256 * c, 256), 256)
            part = dot(norm2_t[rows, :], d_pre[...])
            out[:, 16 * w : 16 * w + 16, :] = part.reshape(16, 16, 1024).astype(out.dtype)
        part = dot(hidden_t[pl.ds(pl.multiple_of(512 * c, 512), 512), :], g_out[...])
        out[:, 32:64, :] = part.reshape(16, 32, 1024).astype(out.dtype)


def feed_forward(at, *operands):
    outs = (
        struct((768, D)),
        struct((D, 768)),
        struct((768, D)),
        struct((768, D)),
        struct((16, 64, 1024)),
        struct((16, 64, 1024)),
        struct((BLK, D)),
        struct((BLK, D)),
        struct((BLK, D)),
        struct((BLK, D), F32),
        struct((1, 1024), F32),
        struct((D, 768)),
    )
    rows, columns = pltpu.VMEM((768, D), BF16), pltpu.VMEM((D, 768), BF16)
    square = pltpu.VMEM((D, 1024), BF16)
    scratch = (rows, rows, columns, rows, columns, rows, square, square)
    return call(mlp_kernel, at, operands, outs, 0.1, scratch)


def add_kernel(at_ref, a, b, out):
    out[...] = (a[...].astype(F32) + b[...].astype(F32)).astype(out.dtype)


def add(at, a, b):
    return call(add_kernel, at, (a, b), (struct(a.shape),), 0.1)[0]


def unpack_kernel(at_ref, back, tables, norm1_t, g_ref, d_mixed, merged, given, kept):
    core = at_ref[1]
    lane = lax.broadcasted_iota(jnp.int32, (BLK, 128), 1)
    left = lane < HDIM
    for j in range(4):
        if True:
            chip = lax.bitwise_xor(at_ref[0], TREE[j])
            hi, lo = chip // 2, chip % 2
            cos, sin_up, sin_down = tables[0, lo], tables[1, lo], tables[2, lo]
            rows = slice(j * BLK, j * BLK + BLK)
            for h in range(2):
                kv, qo = [], []
                for i in (2 * h, 2 * h + 1):
                    at = pl.ds(pl.multiple_of(lo * BLK, BLK), BLK)
                    kv.append(back[i, hi, 0, at, :].astype(F32) + back[i, hi, 1, at, :].astype(F32))
                    at = pl.ds(pl.multiple_of(2 * BLK + lo * HALF, HALF), HALF)
                    halves = [back[i, hi, s, at, :] for s in range(2)]
                    qo.append(jnp.concatenate(halves, 0).astype(F32))
                dq = jnp.where(left, qo[0], pltpu.roll(qo[1], 64, 1))
                out = jnp.where(left, pltpu.roll(qo[0], 64, 1), qo[1])
                dk = jnp.where(left, kv[0], pltpu.roll(kv[1], 64, 1))
                dv = jnp.where(left, pltpu.roll(kv[0], 64, 1), kv[1])
                dq = turn_lanes(dq, cos, -sin_up, -sin_down)
                dk = turn_lanes(dk, cos, -sin_up, -sin_down)
                for k, value in enumerate((dq, dk, dv)):
                    at = 256 * k + 128 * h
                    d_mixed[rows, at : at + 128] = value.astype(BF16)
                merged[rows, 128 * h : 128 * h + 128] = out.astype(BF16)
    merged_t = merged[...].astype(F32).T.astype(BF16)
    dense = dot(merged_t, g_ref[...])
    for c, out in ((1 - core, given), (core, kept)):
        for hi in range(2):
            rows = pl.ds(pl.multiple_of(512 * hi + 256 * c, 256), 256)
            part = dot(norm1_t[rows, :], d_mixed[...])
            out[:, 16 * hi : 16 * hi + 16, 0:768] = part.reshape(16, 16, 768).astype(out.dtype)
        half = jnp.where(c == 0, dense[0:128], dense[128:256]).astype(out.dtype)
        for i in range(4):
            for j in range(4):
                out[4 * i + j, :, 768:1024] = half[32 * i : 32 * i + 32, 256 * j : 256 * j + 256]


def unpack(at, *operands):
    outs = (
        struct((768, 768)),
        struct((768, 256)),
        struct((16, 32, 1024)),
        struct((16, 32, 1024)),
    )
    return call(unpack_kernel, at, operands, outs, 100)


def finish_kernel(
    at_ref, d_mixed, merged, mix, d_norm2, normal, g_own, up_sum, vec, *refs
):
    parts, e_own, merged_own, sums = refs[0:3], *refs[3:6]
    gain1, gain2 = vec[0:1, :], vec[2:3, :]
    totals = [jnp.zeros((1, D), F32) for _ in range(4)]
    for j in range(4):
        rows = slice(j * BLK, j * BLK + BLK)
        d1 = dot_t(d_mixed[rows, :], mix[...])
        d2 = d_norm2[rows, :].astype(F32)
        n = normal[rows, :].astype(F32)
        e = gain1 * d1 + gain2 * d2
        if j == 0:
            e_own[...] = e
            merged_own[...] = merged[rows, :]
        else:
            parts[j - 1][0:BLK, :] = e.astype(BF16)
            heads = merged[rows, :]
            for k in range(4):
                cols = slice(256 * k, 256 * k + 256)
                parts[j - 1][BLK : BLK + 48, cols] = heads[48 * k : 48 * k + 48]
        for k, value in enumerate((d1 * n, d1, d2 * n, d2)):
            totals[k] = totals[k] + jnp.sum(value, 0, keepdims=True)
    for k in range(4):
        sums[k : k + 1, :] = totals[k].astype(BF16)
    sums[4:5, :] = jnp.sum(g_own[...].astype(F32), 0, keepdims=True).astype(BF16)
    sums[5:6, :] = jnp.zeros((1, D), BF16)
    sums[5:6, 0:768] = jnp.sum(d_mixed[...].astype(F32), 0, keepdims=True).astype(BF16)
    sums[6:7, :] = up_sum[...].astype(BF16)
    sums[7:8, :] = jnp.zeros((1, D), BF16)


def finish(at, *operands):
    outs = (
        struct((BLK + 48, D)),
        struct((BLK + 48, D)),
        struct((BLK + 48, D)),
        struct((BLK, D), F32),
        struct((BLK, 256)),
        struct((8, D)),
    )
    return call(finish_kernel, at, operands, outs, 0.1)


def tokens_kernel(at_ref, x_ref, g_ref, *refs):
    e_own, merged_own, feed_own = refs[0:3]
    late, feeds = refs[3:6], refs[6:9]
    dense, vec, out, grad_in = refs[9:13]
    x = at_ref[0]
    tokens = x_ref[...].astype(F32)
    total = tokens + vec[4:5, :] + vec[5:6, :] + feed_own[...]
    total = total + dot(merged_own[...], dense[x])
    e = e_own[...]
    for j in range(3):
        total = total + feeds[j][...].astype(F32)
        heads = jnp.concatenate(
            [late[j][BLK : BLK + 48, 256 * k : 256 * k + 256] for k in range(4)], 0
        )
        total = total + dot(heads, dense[lax.bitwise_xor(x, TREE[j + 1])])
        e = e + late[j][0:BLK, :].astype(F32)
    out[...] = total.astype(BF16)
    normal, inv = normalize(tokens)
    grad_in[...] = (g_ref[...].astype(F32) + norm_back(normal, inv, e)).astype(BF16)


def own_tokens(at, *operands):
    return call(tokens_kernel, at, operands, (struct((BLK, D)),) * 2, 0.1)


def join_kernel(at_ref, own, beside, across, far, sibling, aside, out, scratch):
    hi, lo, core = at_ref[0] // 2, at_ref[0] % 2, at_ref[1]
    rows = pl.ds(pl.multiple_of(hi * 16, 16), 16)
    ring = (own, beside, across, far)
    ff = own.shape[0] == 64
    if ff:
        box, places = (slice(32, 64), slice(0, 1024)), ((64, 0), (96, 0))
        width = 1024
    else:
        box, places = (slice(0, 32), slice(768, 1024)), ((0, 768), (32, 768))
        width = 768
    for j in range(4):
        value = ring[j][rows, 0:width]
        for i in range(16):
            if i < out.shape[0]:
                out[i, 16 * j : 16 * j + 16, 0:width] = value
    for (row, column), near, off in zip(places, (own, sibling), (beside, aside)):
        value = jnp.where(core == lo, near[box], off[box])
        for i in range(out.shape[0]):
            out[i, row : row + 32, column : column + value.shape[1]] = value
    if not ff:
        quarter = 2 * hi + core
        chips = [r[32:40, :].astype(F32) for r in ring]
        scratch[0:5, :] = sum(c[0:5] for c in chips)
        for j in range(4):
            chip = lax.bitwise_xor(at_ref[0], TREE[j])
            scratch[pl.ds(8 + chip, 1), :] = chips[j][5:6]
            scratch[pl.ds(12 + chip, 1), :] = chips[j][6:7]
        cols = pl.ds(pl.multiple_of(quarter * 256, 256), 256)
        parts = [scratch[k : k + 1, cols] for k in range(5)]
        for k in range(3):
            n = 3 * quarter + k
            cols = pl.ds(pl.multiple_of(n // 4 * 256, 256), 256)
            parts.append(scratch[pl.ds(8 + n % 4, 1), cols])
        vec = [jnp.concatenate(parts[0:4], 1), jnp.concatenate(parts[4:8], 1)]
        vec += [scratch[pl.ds(12 + quarter, 1), :], jnp.zeros((5, 1024), F32)]
        vec = jnp.concatenate(vec, 0).astype(BF16)
        for i in range(16):
            out[i, 64:72, :] = vec


def join(at, own, count):
    parts = [send(own, p) for p in (NEXT, CROSS, FAR, CORE, ASIDE)]
    rows = 128 if own.shape[0] == 64 else 72
    scratch = [pltpu.VMEM((16, 1024), F32)]
    return call(join_kernel, at, (own, *parts), (struct((count, rows, 1024)),), 0.1, scratch)[0]


def place_ff_kernel(at_ref, sums, up_out, down_out):
    x, core = at_ref[0], at_ref[1]
    for j in range(4):
        cols = pl.ds(pl.multiple_of(lax.bitwise_xor(x, TREE[j]) * 1024, 1024), 1024)
        up_out[:, cols] = sums[:, 16 * j : 16 * j + 16, :].reshape(256, 1024).astype(F32)
    for side, at in ((core, 64), (1 - core, 96)):
        rows = pl.ds(pl.multiple_of(side * 512, 512), 512)
        down_out[rows, :] = sums[:, at : at + 32, :].reshape(512, 1024).astype(F32)


def place_attn_kernel(at_ref, sums, mix_out, dense_out, *vec_outs):
    x, core = at_ref[0], at_ref[1]
    for j in range(4):
        chip = lax.bitwise_xor(x, TREE[j])
        for k in range(3):
            cols = pl.ds(pl.multiple_of(k * 1024 + chip * 256, 256), 256)
            part = sums[:, 16 * j : 16 * j + 16, 256 * k : 256 * k + 256]
            mix_out[:, cols] = part.reshape(256, 256).astype(F32)
    for side, at in ((core, 0), (1 - core, 32)):
        for i in range(4):
            rows = pl.ds(pl.multiple_of(side * 128 + i * 32, 32), 32)
            for j in range(4):
                part = sums[4 * i + j, at : at + 32, 768:1024]
                dense_out[rows, 256 * j : 256 * j + 256] = part.astype(F32)
    total = jnp.zeros((8, 1024), F32)
    for i in range(16):
        total = total + sums[i, 64:72, :].astype(F32)
    for k in range(5):
        vec_outs[k][...] = total[k // 4, 256 * (k % 4) : 256 * (k % 4) + 256]
    vec_outs[5][...] = total[1, 0:256]
    vec_outs[6][...] = total[1, 256:1024]
    vec_outs[7][...] = total[2, :]


def shards(
    inputs,
    first_gain,
    first_bias,
    second_gain,
    second_bias,
    mix_weight,
    mix_bias,
    dense_weight,
    dense_bias,
    up_weight,
    up_bias,
    down_weight,
    down_bias,
    grad_out,
):
    ctx, wa = lax.axis_index("ctx"), lax.axis_index("wa")
    lo, yz, hi, core = ctx % 2, ctx // 2, wa // 2, wa % 2
    x = 2 * hi + lo
    at = jnp.stack([x, core, yz // 4, yz % 4, yz])

    both = jnp.concatenate([inputs[0], grad_out[0]], 0)
    beside, across = send(both, NEXT), send(both, CROSS)
    tokens = (both, beside, across, send(after(across, beside), NEXT))
    small, filled = 0, 0
    for v in (
        first_gain,
        first_bias,
        second_gain,
        second_bias,
        dense_bias,
        down_bias,
        mix_bias,
        up_bias,
    ):
        rows = v.shape[0] // 256
        small = small + jnp.pad(v.reshape(rows, 256), ((filled, 16 - filled - rows), (0, 0)))
        filled += rows
    own, mix_cross, up_cross = call(
        pack_kernel,
        at,
        (mix_weight, up_weight, dense_weight, small),
        (struct((768, 1024)), struct((272, 768)), struct((256, 1024))),
        0.1,
    )
    tables = call(tables_kernel, at, (), (struct((3, 2, BLK, 128), F32),), 0.1)[0]
    mix_got = send(after(mix_cross, beside, across), CROSS)
    other = send(own, CORE)
    mix_other_got = send(mix_got, CORE)
    up_got = send(after(up_cross, across, mix_got), CROSS)
    up_other_got = send(up_got, CORE)
    down_other = send(after(down_weight, across), CORE)

    sent, vec = project(at, tokens, (own, mix_got, other, mix_other_got), tables)
    held = swap(sent.reshape(16, 3 * BLK, 128))

    up_other_got = send(after(up_got, sent), CORE)
    normal, norm1_t, token_g, d_norm2, given, kept, *feed_sent, feed_own, up_sum, mix = feed_forward(
        at,
        *tokens,
        vec,
        own,
        up_got,
        other,
        up_other_got,
        down_weight,
        down_other,
        mix_got,
        mix_other_got,
    )
    ff_sums = add(at, kept, send(given, CORE))
    ff_mine = swap(after(ff_sums, held))
    back = attention((yz % 2).reshape(1), after(held, ff_sums))
    ff_mine = jnp.sum(after(ff_mine, back).astype(F32), 0).astype(BF16)
    ff_all = join(at, ff_mine, 1)[0]
    ff_all = lax.all_gather(ff_all, "ctx", axis=0, axis_index_groups=YZ, tiled=False)

    feeds = [send(feed_sent[j], (NEXT, CROSS, FAR)[j]) for j in range(3)]
    dense_got = send(after(dense_weight, up_got), CROSS)
    back = swap(after(back, dense_got, *feeds))
    dense_other_got = send(after(dense_got, ff_mine), CORE)
    near = jnp.where(
        core == 0, jnp.stack([dense_weight, other[512:]]), jnp.stack([other[512:], dense_weight])
    )
    away = jnp.where(
        core == 0,
        jnp.stack([dense_got, dense_other_got]),
        jnp.stack([dense_other_got, dense_got]),
    )
    dense_all = jnp.where(hi == 0, jnp.concatenate([near, away]), jnp.concatenate([away, near]))
    back = after(back, dense_all)

    d_mixed, merged, given, kept = unpack(
        at, back.reshape(4, 2, 2, 3 * BLK, 128), tables, norm1_t, token_g
    )
    attn_sums = add(at, kept, send(given, CORE))
    attn_mine = swap(attn_sums)
    *parts, e_own, merged_own, vectors = finish(
        at, after(d_mixed, attn_sums), merged, mix, d_norm2, normal, grad_out[0], up_sum, vec
    )
    vectors = add(at, vectors, send(vectors, CORE))
    late = [send(parts[j], (NEXT, CROSS, FAR)[j]) for j in range(3)]
    attn_mine = jnp.sum(attn_mine.astype(F32), 0).astype(BF16)
    gathered = join(at, jnp.concatenate([attn_mine, vectors], 0), 16)
    gathered = swap(gathered)
    grad_up, grad_down = call(
        place_ff_kernel, at, (ff_all,), (struct((256, FF), F32), struct((1024, D), F32)), 0.1
    )
    output, grad_in = own_tokens(
        at, after(inputs[0], grad_up), grad_out[0], e_own, merged_own, feed_own, *late, *feeds, dense_all, vec
    )
    gathered = after(gathered, output, grad_up)
    row = struct((256,), F32)
    grad_mix, grad_dense, *rest = call(
        place_attn_kernel,
        at,
        (gathered,),
        (struct((256, 3 * D), F32), struct((256, D), F32))
        + (row,) * 6
        + (struct((768,), F32), struct((1024,), F32)),
        0.1,
    )
    return (
        output[None],
        grad_in[None],
        rest[0],
        rest[1],
        rest[2],
        rest[3],
        grad_mix,
        rest[6],
        grad_dense,
        rest[4],
        grad_up,
        rest[7],
        grad_down,
        rest[5],
    )


def solution(mesh):
    rows, vec, tokens = P("wa", None), P("wa"), P("wa", "ctx", None)
    return jax.shard_map(
        shards,
        mesh=mesh,
        in_specs=(tokens, vec, vec, vec, vec, rows, vec, rows, vec, rows, vec, rows, vec, tokens),
        out_specs=(
            tokens,
            tokens,
            vec,
            vec,
            vec,
            vec,
            rows,
            vec,
            rows,
            vec,
            rows,
            vec,
            rows,
            vec,
        ),
        check_vma=False,
    )
```

```python
import functools
import math

import jax
import jax.numpy as jnp
from jax import lax
from jax.experimental import pallas as pl
from jax.experimental.pallas import tpu as pltpu
from jax.sharding import PartitionSpec as P

D = 1024
HEADS = 16
HDIM = 64
ROT = 16
FF = 4096
BLK = 192
HALF = 96
EPS = 1e-05
F32 = jnp.float32
BF16 = jnp.bfloat16


def attention_kernel(par_ref, x_ref, out_ref, kvt, s_buf, p_even, p_odd, dkv, *, tq):
    width = 2 * BLK
    step = 2 * tq // width
    groups = x_ref.shape[0] // step
    par = par_ref[0]
    p_bufs = (p_even, p_odd)

    def rows_of(pair, count):
        return pl.ds(pl.multiple_of(pair * width, width), count * width)

    def keys(pair, count):
        return x_ref[pl.ds(pair, count), 0:width, :].reshape(count * width, 128)

    def turn(c, carry):
        kvt[:, rows_of(c * step, step)] = keys(c * step, step).T
        return carry

    lax.fori_loop(0, groups, turn, 0)
    row = lax.broadcasted_iota(jnp.int32, (128, tq), 0)
    lane = lax.broadcasted_iota(jnp.int32, (tq, 128), 1)
    q_idx = lax.broadcasted_iota(jnp.int32, (1, tq), 1)
    q_tok = (q_idx // HALF) * BLK + par * HALF + q_idx % HALF
    zero = jnp.zeros((), F32)

    def own(t):
        half = step // 2
        return ((t * step, half, 0, 0), (t * step + half, half, tq // 2, tq))

    def widen(old, new, qs):
        return new if qs == 0 else jnp.concatenate([old[:, :qs], new], 1)

    def operands(t):
        qd_rows = x_ref[t * step : t * step + step, width : width + BLK, :].reshape(tq, 128)
        return qd_rows, qd_rows.astype(F32).T

    def scores(q_t, top, pair, count, qs=0, first=None):
        s = jnp.dot(keys(pair, count), q_t[:, qs:], preferred_element_type=F32)
        if first is not None:
            k_tok = first + lax.broadcasted_iota(jnp.int32, (count * width, 1), 0)
            s = jnp.where(k_tok <= q_tok[:, qs:], s, -1e30)
        s_buf[rows_of(pair, count), qs:] = s
        high = jnp.max(s.reshape(count * width // 8, 8, tq - qs), 0)
        return widen(top, jnp.maximum(top[:, qs:], high), qs)

    def all_scores(t, qd_t):
        q_t = jnp.where(row < HDIM, qd_t * 0.125, zero).astype(BF16)
        top = jnp.full((8, tq), -1e30, F32)
        if t:
            top = lax.fori_loop(0, t, lambda c, m: scores(q_t, m, c * step, step), top)
        for part in own(t):
            top = scores(q_t, top, *part)
        return jnp.max(top, 0, keepdims=True)

    def weigh(t, top, state, pair, count, qs=0, first=None):
        at = rows_of(pair, count)
        total, out_t = state
        p = jnp.exp(s_buf[at, qs:] - top[:, qs:])
        p_sum = jnp.sum(p.reshape(count * width // 8, 8, tq - qs), 0)
        p_low = p.astype(BF16)
        p_bufs[t % 2][at, qs:] = p_low
        term = jnp.dot(kvt[HDIM:, at], p_low, preferred_element_type=F32)
        return widen(total, total[:, qs:] + p_sum, qs), widen(out_t, out_t[:, qs:] + term, qs)

    def ready(qd_rows, qd_t, state):
        total, out_t = state
        inv = 1.0 / jnp.sum(total, 0, keepdims=True)
        out_t = out_t * inv
        do_t = (qd_t[HDIM:] * inv).astype(BF16)
        delta = jnp.sum(do_t.astype(F32) * out_t, 0, keepdims=True)
        do_full = jnp.concatenate([jnp.zeros((HDIM, tq), BF16), do_t], 0)
        do_rows = do_full.astype(F32).T.astype(BF16)
        q_rows = jnp.where(lane < HDIM, qd_rows.astype(F32) * 0.125, zero).astype(BF16)
        return do_full, do_rows, q_rows, delta, out_t

    def back(t, given, dq_t, pair, count, qs=0, first=None):
        do_full, do_rows, q_rows, delta, _ = given
        at = rows_of(pair, count)
        dp = jnp.dot(keys(pair, count), do_full[:, qs:], preferred_element_type=F32)
        p_low = p_bufs[t % 2][at, qs:]
        ds = (p_low.astype(F32) * (dp - delta[:, qs:])).astype(BF16)
        term = jnp.dot(p_low, do_rows[qs:], preferred_element_type=F32) + jnp.dot(
            ds, q_rows[qs:], preferred_element_type=F32
        )
        if t == groups - 1:
            dkv[at, :] = term
        else:
            dkv[at, :] += term
        dq = jnp.dot(kvt[:HDIM, at], ds, preferred_element_type=F32)
        return widen(dq_t, dq_t[:, qs:] + dq, qs)

    def finish_group(t, given, dq_t):
        out = jnp.concatenate([dq_t * 0.125, given[4]], 0).T.astype(BF16)
        out_ref[t * step : t * step + step, width : width + BLK, :] = out.reshape(step, BLK, 128)

    half = step // 2
    given = None
    for t in reversed(range(groups)):
        rows_t = operands(t)
        top = all_scores(t, rows_t[1])
        state = (jnp.zeros((8, tq), F32), jnp.zeros((HDIM, tq), F32))
        dq_t = jnp.zeros((HDIM, tq), F32)
        if given is None:
            if t:
                state = lax.fori_loop(
                    0, t, lambda c, s, t=t, top=top: weigh(t, top, s, c * step, step), state
                )
            for part in own(t):
                state = weigh(t, top, state, *part)
        else:

            def both(c, carry, t=t, top=top, given=given):
                state, dq_t = carry
                state = weigh(t, top, state, c * half, half)
                return state, back(t + 1, given, dq_t, c * half, half)

            if t:
                state, dq_t = lax.fori_loop(0, 2 * t, both, (state, dq_t))
            for u in range(2):
                dq_t = back(t + 1, given, dq_t, t * step + u * half, half)
            for part in own(t):
                state = weigh(t, top, state, *part)
            for part in own(t + 1):
                dq_t = back(t + 1, given, dq_t, *part)
            finish_group(t + 1, given, dq_t)
        given = ready(*rows_t, state)
    dq_t = jnp.zeros((HDIM, tq), F32)
    for part in own(0):
        dq_t = back(0, given, dq_t, *part)
    finish_group(0, given, dq_t)

    def drain(c, carry):
        rows = dkv[rows_of(c * step, step), :].astype(BF16)
        out_ref[pl.ds(c * step, step), 0:width, :] = rows.reshape(step, width, 128)
        return carry

    lax.fori_loop(0, groups, drain, 0)


def attention(par, x, tq=768):
    n_keys = x.shape[0] * 2 * BLK
    whole = pl.BlockSpec(x.shape, lambda i: (0, 0, 0), pipeline_mode=pl.Buffered(1))
    return pl.pallas_call(
        functools.partial(attention_kernel, tq=tq),
        grid=(1,),
        out_shape=jax.ShapeDtypeStruct(x.shape, BF16),
        in_specs=[pl.BlockSpec(memory_space=pltpu.SMEM), whole],
        out_specs=whole,
        scratch_shapes=[
            pltpu.VMEM((128, n_keys), BF16),
            pltpu.VMEM((n_keys, tq), F32),
            pltpu.VMEM((n_keys - 2 * tq, tq), BF16),
            pltpu.VMEM((n_keys, tq), BF16),
            pltpu.VMEM((n_keys, 128), F32),
        ],
        compiler_params=pltpu.CompilerParams(vmem_limit_bytes=63 * 2**20),
        cost_estimate=cost(46),
    )(par, x)


def cost(micros):
    return pl.CostEstimate(flops=int(micros * 1.1e9), bytes_accessed=10**5, transcendentals=0)


def normalize(values):
    centred = values - jnp.mean(values, -1, keepdims=True)
    spread = jnp.mean(centred * centred, -1, keepdims=True)
    inv = lax.rsqrt(spread + EPS)
    return centred * inv, inv


def norm_back(normal, inv, e):
    return inv * (
        e
        - jnp.mean(e, -1, keepdims=True)
        - normal * jnp.mean(e * normal, -1, keepdims=True)
    )


def dot(a, b):
    return jnp.dot(a, b, preferred_element_type=F32)


def dot_t(a, b):
    return lax.dot_general(a, b, (((1,), (1,)), ((), ())), preferred_element_type=F32)


def t_dot(a, b):
    return lax.dot_general(a, b, (((0,), (0,)), ((), ())), preferred_element_type=F32)


AX = ("ctx", "wa")
YZ = [[2 * i + lo for i in range(16)] for lo in range(2)]
SMEM = pl.BlockSpec(memory_space=pltpu.SMEM)


def route(move):
    pairs = []
    for ctx in range(32):
        for wa in range(4):
            to_x, y, z, core = move(wa // 2 * 2 + ctx % 2, ctx // 8, ctx // 2 % 4, wa % 2)
            to_ctx, to_wa = y * 8 + z * 2 + to_x % 2, to_x // 2 * 2 + core
            pairs.append((ctx * 4 + wa, to_ctx * 4 + to_wa))
    return pairs


CORE = route(lambda x, y, z, c: (x, y, z, 1 - c))
CROSS = route(lambda x, y, z, c: (3 - x, y, z, c))
FAR = route(lambda x, y, z, c: (x ^ 2, y, z, c))
NEXT = route(lambda x, y, z, c: (x ^ 1, y, z, c))
ASIDE = route(lambda x, y, z, c: (x ^ 1, y, z, 1 - c))
TREE = (0, 1, 3, 2)


def send(value, pairs):
    return lax.ppermute(value, AX, pairs)


def pick(array, index, axis=0):
    return lax.dynamic_index_in_dim(array, index, axis, keepdims=False)


def after(value, *first):
    return lax.optimization_barrier((value, *first))[0]


def swap(pieces):
    return lax.all_to_all(pieces, "ctx", 0, 0, axis_index_groups=YZ, tiled=True)


def call(kernel, at, operands, outs, micros, scratch=()):
    def whole(a):
        return pl.BlockSpec(a.shape, lambda i: (0,) * len(a.shape), pipeline_mode=pl.Buffered(1))

    return pl.pallas_call(
        kernel,
        grid=(1,),
        out_shape=tuple(outs),
        in_specs=[SMEM] + [whole(a) for a in operands],
        out_specs=tuple(whole(a) for a in outs),
        scratch_shapes=list(scratch),
        compiler_params=pltpu.CompilerParams(vmem_limit_bytes=63 * 2**20),
        cost_estimate=cost(micros),
    )(at, *operands)


def struct(shape, dtype=BF16):
    return jax.ShapeDtypeStruct(shape, dtype)


def pack_kernel(at_ref, mix_ref, up_ref, dense_ref, small_ref, own, mix_cross, up_cross):
    for k, (mix_out, up_out) in enumerate(((own.at[0:256], own.at[256:512]), (mix_cross, up_cross))):
        q = at_ref[0] if k == 0 else 3 - at_ref[0]
        for j in range(3):
            cols = pl.ds(pl.multiple_of(q * 256 + j * 1024, 256), 256)
            mix_out[0:256, 256 * j : 256 * j + 256] = mix_ref[:, cols]
        if k == 0:
            mix_out[0:16, 768:1024] = small_ref[...]
            mix_out[16:256, 768:1024] = jnp.zeros((240, 256), BF16)
        else:
            mix_out[256:272, 0:256] = small_ref[...]
            mix_out[256:272, 256:768] = jnp.zeros((16, 512), BF16)
        up_out[...] = up_ref[:, pl.ds(pl.multiple_of(q * 1024, 1024), 1024)]
    own[512:768, :] = dense_ref[...]


def tables_kernel(at_ref, tables):
    shape = (BLK, 128)
    feature = lax.broadcasted_iota(jnp.int32, shape, 1) % HDIM
    exponent = (feature % 8).astype(F32) * (2.0 / ROT)
    inverse = jnp.exp(exponent * -math.log(10000.0))
    for block in range(2):
        spot = at_ref[4] * (2 * BLK) + block * BLK + lax.broadcasted_iota(jnp.int32, shape, 0)
        angle = spot.astype(F32) * inverse
        sine = jnp.sin(angle)
        tables[0, block] = jnp.where(feature < ROT, jnp.cos(angle), 1.0)
        tables[1, block] = jnp.where(feature < ROT // 2, -sine, 0.0)
        tables[2, block] = jnp.where((feature >= ROT // 2) & (feature < ROT), sine, 0.0)


def turn_lanes(pair, cos, sin_up, sin_down):
    return pair * cos + pltpu.roll(pair, 120, 1) * sin_up + pltpu.roll(pair, 8, 1) * sin_down


def project_kernel(at_ref, *refs):
    tokens, mixes = refs[0:4], refs[4:8]
    tables = refs[8]
    sent, vec_out, mix_out, dense_out = refs[9:13]
    x, core = at_ref[0], at_ref[1]
    hi, lo = x // 2, x % 2
    quarters = (2 * hi + core, 2 * (1 - hi) + core, 2 * hi + 1 - core, 2 * (1 - hi) + 1 - core)
    for w, piece in zip(quarters, mixes):
        cols = pl.ds(pl.multiple_of(w * 256, 256), 256)
        mix_out[cols, :] = piece[0:256, 0:768]
        if piece.shape[0] == 272:
            vec_out[0:16, cols] = piece[256:272, 0:256].astype(F32)
        else:
            vec_out[0:16, cols] = piece[0:16, 768:1024].astype(F32)

    @pl.when(core == lo)
    def _():
        dense_out[...] = mixes[0][512:768, :]

    @pl.when(core != lo)
    def _():
        dense_out[...] = mixes[2][512:768, :]

    for j in range(3):
        n = 4 * j + x
        row = vec_out[6:9, pl.ds(pl.multiple_of((n // 3) * 256, 256), 256)]
        keep = lax.broadcasted_iota(jnp.int32, (3, 256), 0) == n % 3
        vec_out[16:17, 256 * j : 256 * j + 256] = jnp.sum(
            jnp.where(keep, row, 0.0), 0, keepdims=True
        )
    for j in range(4):
        vec_out[17:18, 256 * j : 256 * j + 256] = vec_out[
            9 + j : 10 + j, pl.ds(pl.multiple_of(x * 256, 256), 256)
        ]
    gain1, shift1 = vec_out[0:1, :], vec_out[1:2, :]
    bias = vec_out[16:17, 0:768]
    lane = lax.broadcasted_iota(jnp.int32, (BLK, 128), 1)
    left = lane < HDIM
    for j in range(4):
        chip = lax.bitwise_xor(x, TREE[j])
        to_hi, to_lo = chip // 2, chip % 2
        normal, _ = normalize(tokens[j][0:BLK, :].astype(F32))
        low1 = (normal * gain1 + shift1).astype(BF16)
        grad = tokens[j][BLK : 2 * BLK, :]
        mixed = dot(low1, mix_out[...]) + bias
        d_merged = dot_t(grad, dense_out[...])
        cos, sin_up, sin_down = tables[0, to_lo], tables[1, to_lo], tables[2, to_lo]
        for h in range(2):
            cols = slice(128 * h, 128 * h + 128)
            q = turn_lanes(mixed[:, 0:256][:, cols], cos, sin_up, sin_down)
            k = turn_lanes(mixed[:, 256:512][:, cols], cos, sin_up, sin_down)
            v = mixed[:, 512:768][:, cols]
            dm = d_merged[:, cols]
            for side in range(2):
                if side == 0:
                    kv = jnp.where(left, k, pltpu.roll(v, 64, 1)).astype(BF16)
                    qd = jnp.where(left, q, pltpu.roll(dm, 64, 1)).astype(BF16)
                else:
                    kv = jnp.where(left, pltpu.roll(k, 64, 1), v).astype(BF16)
                    qd = jnp.where(left, pltpu.roll(q, 64, 1), dm).astype(BF16)
                i = 2 * h + side
                for half in range(2):
                    at = pl.ds(pl.multiple_of(to_lo * BLK, BLK), BLK)
                    sent[i, to_hi, half, at, :] = kv
                    at = pl.ds(pl.multiple_of(2 * BLK + to_lo * HALF, HALF), HALF)
                    sent[i, to_hi, half, at, :] = qd[HALF * half : HALF * half + HALF]


def project(at, tokens, mixes, tables):
    outs = (struct((4, 2, 2, 3 * BLK, 128)), struct((24, D), F32))
    scratch = [pltpu.VMEM((D, 768), BF16), pltpu.VMEM((256, D), BF16)]
    return call(project_kernel, at, (*tokens, *mixes, tables), outs, 0.1, scratch)


def mlp_kernel(at_ref, *refs):
    tokens, vec, ups, downs, mixes = refs[0:4], refs[4], refs[5:9], refs[9:11], refs[11:13]
    normal_out, norm1_t, g_out, d_norm2, given, kept = refs[13:19]
    feed_sent, feed_own, sums, mix = refs[19:22], *refs[22:25]
    norm1, norm2, norm2_t, hidden, hidden_t, d_pre, up, down = refs[25:33]
    x, core = at_ref[0], at_ref[1]
    hi, lo = x // 2, x % 2
    quarters = (2 * hi + core, 2 * (1 - hi) + core, 2 * hi + 1 - core, 2 * (1 - hi) + 1 - core)
    for w, piece in zip(quarters, ups):
        rows = slice(256, 512) if piece.shape[0] > 256 else slice(0, 256)
        at = pl.ds(pl.multiple_of(w * 256, 256), 256)
        up[at, :] = piece[rows, :]
        if piece.shape[0] > 256:
            mix[at, :] = piece[0:256, 0:768]
    for w, piece in zip((quarters[1], quarters[3]), mixes):
        mix[pl.ds(pl.multiple_of(w * 256, 256), 256), :] = piece[0:256, :]

    @pl.when(core == lo)
    def _():
        down[...] = downs[0][...]

    @pl.when(core != lo)
    def _():
        down[...] = downs[1][...]

    for j in range(4):
        rows = slice(BLK * j, BLK * j + BLK)
        normal, _ = normalize(tokens[j][0:BLK, :].astype(F32))
        normal_out[rows, :] = normal.astype(BF16)
        norm1[rows, :] = (normal * vec[0:1, :] + vec[1:2, :]).astype(BF16)
        norm2[rows, :] = (normal * vec[2:3, :] + vec[3:4, :]).astype(BF16)
        g_out[rows, :] = tokens[j][BLK : 2 * BLK, :]
    for k in range(4):
        cols = slice(256 * k, 256 * k + 256)
        pre = dot(norm2[...], up[:, cols]) + vec[17:18, cols]
        below = 0.5 + 0.5 * lax.erf(pre * 0.5**0.5)
        hidden[:, cols] = (pre * below).astype(BF16)
        bell = jnp.exp(-0.5 * pre * pre) * (0.5 / math.pi) ** 0.5
        dp = (dot_t(g_out[...], down[cols, :]) * (below + pre * bell)).astype(BF16)
        d_pre[:, cols] = dp
        sums[:, cols] = jnp.sum(dp.astype(F32), 0, keepdims=True)
    d_norm2[...] = dot_t(d_pre[...], up[...]).astype(BF16)
    for j in range(4):
        feed = dot(hidden[BLK * j : BLK * j + BLK, :], down[...])
        if j == 0:
            feed_own[...] = feed
        else:
            feed_sent[j - 1][...] = feed.astype(BF16)
    for k in range(8):
        at = slice(128 * k, 128 * k + 128)
        norm1_t[at, :] = norm1[:, at].T
        norm2_t[at, :] = norm2[:, at].T
        hidden_t[at, :] = hidden[:, at].T
    for c, out in ((1 - core, given), (core, kept)):
        for w in range(2):
            rows = pl.ds(pl.multiple_of(512 * w + 256 * c, 256), 256)
            part = dot(norm2_t[rows, :], d_pre[...])
            out[:, 16 * w : 16 * w + 16, :] = part.reshape(16, 16, 1024).astype(out.dtype)
        part = dot(hidden_t[pl.ds(pl.multiple_of(512 * c, 512), 512), :], g_out[...])
        out[:, 32:64, :] = part.reshape(16, 32, 1024).astype(out.dtype)


def feed_forward(at, *operands):
    outs = (
        struct((768, D)),
        struct((D, 768)),
        struct((768, D)),
        struct((768, D)),
        struct((16, 64, 1024)),
        struct((16, 64, 1024)),
        struct((BLK, D)),
        struct((BLK, D)),
        struct((BLK, D)),
        struct((BLK, D), F32),
        struct((1, 1024), F32),
        struct((D, 768)),
    )
    rows, columns = pltpu.VMEM((768, D), BF16), pltpu.VMEM((D, 768), BF16)
    square = pltpu.VMEM((D, 1024), BF16)
    scratch = (rows, rows, columns, rows, columns, rows, square, square)
    return call(mlp_kernel, at, operands, outs, 0.1, scratch)


def add_kernel(at_ref, a, b, out):
    out[...] = (a[...].astype(F32) + b[...].astype(F32)).astype(out.dtype)


def add(at, a, b):
    return call(add_kernel, at, (a, b), (struct(a.shape),), 0.1)[0]


def unpack_kernel(at_ref, back, tables, norm1_t, g_ref, d_mixed, merged, given, kept):
    core = at_ref[1]
    lane = lax.broadcasted_iota(jnp.int32, (BLK, 128), 1)
    left = lane < HDIM
    for j in range(4):
        if True:
            chip = lax.bitwise_xor(at_ref[0], TREE[j])
            hi, lo = chip // 2, chip % 2
            cos, sin_up, sin_down = tables[0, lo], tables[1, lo], tables[2, lo]
            rows = slice(j * BLK, j * BLK + BLK)
            for h in range(2):
                kv, qo = [], []
                for i in (2 * h, 2 * h + 1):
                    at = pl.ds(pl.multiple_of(lo * BLK, BLK), BLK)
                    kv.append(back[i, hi, 0, at, :].astype(F32) + back[i, hi, 1, at, :].astype(F32))
                    at = pl.ds(pl.multiple_of(2 * BLK + lo * HALF, HALF), HALF)
                    halves = [back[i, hi, s, at, :] for s in range(2)]
                    qo.append(jnp.concatenate(halves, 0).astype(F32))
                dq = jnp.where(left, qo[0], pltpu.roll(qo[1], 64, 1))
                out = jnp.where(left, pltpu.roll(qo[0], 64, 1), qo[1])
                dk = jnp.where(left, kv[0], pltpu.roll(kv[1], 64, 1))
                dv = jnp.where(left, pltpu.roll(kv[0], 64, 1), kv[1])
                dq = turn_lanes(dq, cos, -sin_up, -sin_down)
                dk = turn_lanes(dk, cos, -sin_up, -sin_down)
                for k, value in enumerate((dq, dk, dv)):
                    at = 256 * k + 128 * h
                    d_mixed[rows, at : at + 128] = value.astype(BF16)
                merged[rows, 128 * h : 128 * h + 128] = out.astype(BF16)
    merged_t = merged[...].astype(F32).T.astype(BF16)
    dense = dot(merged_t, g_ref[...])
    for c, out in ((1 - core, given), (core, kept)):
        for hi in range(2):
            rows = pl.ds(pl.multiple_of(512 * hi + 256 * c, 256), 256)
            part = dot(norm1_t[rows, :], d_mixed[...])
            out[:, 16 * hi : 16 * hi + 16, 0:768] = part.reshape(16, 16, 768).astype(out.dtype)
        half = jnp.where(c == 0, dense[0:128], dense[128:256]).astype(out.dtype)
        for i in range(4):
            for j in range(4):
                out[4 * i + j, :, 768:1024] = half[32 * i : 32 * i + 32, 256 * j : 256 * j + 256]


def unpack(at, *operands):
    outs = (
        struct((768, 768)),
        struct((768, 256)),
        struct((16, 32, 1024)),
        struct((16, 32, 1024)),
    )
    return call(unpack_kernel, at, operands, outs, 100)


def finish_kernel(
    at_ref, d_mixed, merged, mix, d_norm2, normal, g_own, up_sum, vec, *refs
):
    parts, e_own, merged_own, sums = refs[0:3], *refs[3:6]
    gain1, gain2 = vec[0:1, :], vec[2:3, :]
    totals = [jnp.zeros((1, D), F32) for _ in range(4)]
    for j in range(4):
        rows = slice(j * BLK, j * BLK + BLK)
        d1 = dot_t(d_mixed[rows, :], mix[...])
        d2 = d_norm2[rows, :].astype(F32)
        n = normal[rows, :].astype(F32)
        e = gain1 * d1 + gain2 * d2
        if j == 0:
            e_own[...] = e
            merged_own[...] = merged[rows, :]
        else:
            parts[j - 1][0:BLK, :] = e.astype(BF16)
            heads = merged[rows, :]
            for k in range(4):
                cols = slice(256 * k, 256 * k + 256)
                parts[j - 1][BLK : BLK + 48, cols] = heads[48 * k : 48 * k + 48]
        for k, value in enumerate((d1 * n, d1, d2 * n, d2)):
            totals[k] = totals[k] + jnp.sum(value, 0, keepdims=True)
    for k in range(4):
        sums[k : k + 1, :] = totals[k].astype(BF16)
    sums[4:5, :] = jnp.sum(g_own[...].astype(F32), 0, keepdims=True).astype(BF16)
    sums[5:6, :] = jnp.zeros((1, D), BF16)
    sums[5:6, 0:768] = jnp.sum(d_mixed[...].astype(F32), 0, keepdims=True).astype(BF16)
    sums[6:7, :] = up_sum[...].astype(BF16)
    sums[7:8, :] = jnp.zeros((1, D), BF16)


def finish(at, *operands):
    outs = (
        struct((BLK + 48, D)),
        struct((BLK + 48, D)),
        struct((BLK + 48, D)),
        struct((BLK, D), F32),
        struct((BLK, 256)),
        struct((8, D)),
    )
    return call(finish_kernel, at, operands, outs, 0.1)


def tokens_kernel(at_ref, x_ref, g_ref, *refs):
    e_own, merged_own, feed_own = refs[0:3]
    late, feeds = refs[3:6], refs[6:9]
    dense, vec, out, grad_in = refs[9:13]
    x = at_ref[0]
    tokens = x_ref[...].astype(F32)
    total = tokens + vec[4:5, :] + vec[5:6, :] + feed_own[...]
    total = total + dot(merged_own[...], dense[x])
    e = e_own[...]
    for j in range(3):
        total = total + feeds[j][...].astype(F32)
        heads = jnp.concatenate(
            [late[j][BLK : BLK + 48, 256 * k : 256 * k + 256] for k in range(4)], 0
        )
        total = total + dot(heads, dense[lax.bitwise_xor(x, TREE[j + 1])])
        e = e + late[j][0:BLK, :].astype(F32)
    out[...] = total.astype(BF16)
    normal, inv = normalize(tokens)
    grad_in[...] = (g_ref[...].astype(F32) + norm_back(normal, inv, e)).astype(BF16)


def own_tokens(at, *operands):
    return call(tokens_kernel, at, operands, (struct((BLK, D)),) * 2, 0.1)


def join_kernel(at_ref, own, beside, across, far, sibling, aside, out, scratch):
    hi, lo, core = at_ref[0] // 2, at_ref[0] % 2, at_ref[1]
    rows = pl.ds(pl.multiple_of(hi * 16, 16), 16)
    ring = (own, beside, across, far)
    ff = own.shape[0] == 64
    if ff:
        box, places = (slice(32, 64), slice(0, 1024)), ((64, 0), (96, 0))
        width = 1024
    else:
        box, places = (slice(0, 32), slice(768, 1024)), ((0, 768), (32, 768))
        width = 768
    for j in range(4):
        value = ring[j][rows, 0:width]
        for i in range(16):
            if i < out.shape[0]:
                out[i, 16 * j : 16 * j + 16, 0:width] = value
    for (row, column), near, off in zip(places, (own, sibling), (beside, aside)):
        value = jnp.where(core == lo, near[box], off[box])
        for i in range(out.shape[0]):
            out[i, row : row + 32, column : column + value.shape[1]] = value
    if not ff:
        quarter = 2 * hi + core
        chips = [r[32:40, :].astype(F32) for r in ring]
        scratch[0:5, :] = sum(c[0:5] for c in chips)
        for j in range(4):
            chip = lax.bitwise_xor(at_ref[0], TREE[j])
            scratch[pl.ds(8 + chip, 1), :] = chips[j][5:6]
            scratch[pl.ds(12 + chip, 1), :] = chips[j][6:7]
        cols = pl.ds(pl.multiple_of(quarter * 256, 256), 256)
        parts = [scratch[k : k + 1, cols] for k in range(5)]
        for k in range(3):
            n = 3 * quarter + k
            cols = pl.ds(pl.multiple_of(n // 4 * 256, 256), 256)
            parts.append(scratch[pl.ds(8 + n % 4, 1), cols])
        vec = [jnp.concatenate(parts[0:4], 1), jnp.concatenate(parts[4:8], 1)]
        vec += [scratch[pl.ds(12 + quarter, 1), :], jnp.zeros((5, 1024), F32)]
        vec = jnp.concatenate(vec, 0).astype(BF16)
        for i in range(16):
            out[i, 64:72, :] = vec


def join(at, own, count):
    parts = [send(own, p) for p in (NEXT, CROSS, FAR, CORE, ASIDE)]
    rows = 128 if own.shape[0] == 64 else 72
    scratch = [pltpu.VMEM((16, 1024), F32)]
    return call(join_kernel, at, (own, *parts), (struct((count, rows, 1024)),), 0.1, scratch)[0]


def place_ff_kernel(at_ref, sums, up_out, down_out):
    x, core = at_ref[0], at_ref[1]
    for j in range(4):
        cols = pl.ds(pl.multiple_of(lax.bitwise_xor(x, TREE[j]) * 1024, 1024), 1024)
        up_out[:, cols] = sums[:, 16 * j : 16 * j + 16, :].reshape(256, 1024).astype(F32)
    for side, at in ((core, 64), (1 - core, 96)):
        rows = pl.ds(pl.multiple_of(side * 512, 512), 512)
        down_out[rows, :] = sums[:, at : at + 32, :].reshape(512, 1024).astype(F32)


def place_attn_kernel(at_ref, sums, mix_out, dense_out, *vec_outs):
    x, core = at_ref[0], at_ref[1]
    for j in range(4):
        chip = lax.bitwise_xor(x, TREE[j])
        for k in range(3):
            cols = pl.ds(pl.multiple_of(k * 1024 + chip * 256, 256), 256)
            part = sums[:, 16 * j : 16 * j + 16, 256 * k : 256 * k + 256]
            mix_out[:, cols] = part.reshape(256, 256).astype(F32)
    for side, at in ((core, 0), (1 - core, 32)):
        for i in range(4):
            rows = pl.ds(pl.multiple_of(side * 128 + i * 32, 32), 32)
            for j in range(4):
                part = sums[4 * i + j, at : at + 32, 768:1024]
                dense_out[rows, 256 * j : 256 * j + 256] = part.astype(F32)
    total = jnp.zeros((8, 1024), F32)
    for i in range(16):
        total = total + sums[i, 64:72, :].astype(F32)
    for k in range(5):
        vec_outs[k][...] = total[k // 4, 256 * (k % 4) : 256 * (k % 4) + 256]
    vec_outs[5][...] = total[1, 0:256]
    vec_outs[6][...] = total[1, 256:1024]
    vec_outs[7][...] = total[2, :]


def shards(
    inputs,
    first_gain,
    first_bias,
    second_gain,
    second_bias,
    mix_weight,
    mix_bias,
    dense_weight,
    dense_bias,
    up_weight,
    up_bias,
    down_weight,
    down_bias,
    grad_out,
):
    ctx, wa = lax.axis_index("ctx"), lax.axis_index("wa")
    lo, yz, hi, core = ctx % 2, ctx // 2, wa // 2, wa % 2
    x = 2 * hi + lo
    at = jnp.stack([x, core, yz // 4, yz % 4, yz])

    both = jnp.concatenate([inputs[0], grad_out[0]], 0)
    beside, across = send(both, NEXT), send(both, CROSS)
    tokens = (both, beside, across, send(after(across, beside), NEXT))
    small, filled = 0, 0
    for v in (
        first_gain,
        first_bias,
        second_gain,
        second_bias,
        dense_bias,
        down_bias,
        mix_bias,
        up_bias,
    ):
        rows = v.shape[0] // 256
        small = small + jnp.pad(v.reshape(rows, 256), ((filled, 16 - filled - rows), (0, 0)))
        filled += rows
    own, mix_cross, up_cross = call(
        pack_kernel,
        at,
        (mix_weight, up_weight, dense_weight, small),
        (struct((768, 1024)), struct((272, 768)), struct((256, 1024))),
        0.1,
    )
    tables = call(tables_kernel, at, (), (struct((3, 2, BLK, 128), F32),), 0.1)[0]
    mix_got = send(after(mix_cross, beside, across), CROSS)
    other = send(own, CORE)
    mix_other_got = send(mix_got, CORE)
    up_got = send(after(up_cross, across, mix_got), CROSS)
    up_other_got = send(up_got, CORE)
    down_other = send(after(down_weight, across), CORE)

    sent, vec = project(at, tokens, (own, mix_got, other, mix_other_got), tables)
    held = swap(sent.reshape(16, 3 * BLK, 128))

    up_other_got = send(after(up_got, sent), CORE)
    normal, norm1_t, token_g, d_norm2, given, kept, *feed_sent, feed_own, up_sum, mix = feed_forward(
        at,
        *tokens,
        vec,
        own,
        up_got,
        other,
        up_other_got,
        down_weight,
        down_other,
        mix_got,
        mix_other_got,
    )
    ff_sums = add(at, kept, send(given, CORE))
    ff_mine = swap(after(ff_sums, held))
    back = attention((yz % 2).reshape(1), after(held, ff_sums))
    ff_mine = jnp.sum(after(ff_mine, back).astype(F32), 0).astype(BF16)
    ff_all = join(at, ff_mine, 1)[0]
    ff_all = lax.all_gather(ff_all, "ctx", axis=0, axis_index_groups=YZ, tiled=False)

    feeds = [send(feed_sent[j], (NEXT, CROSS, FAR)[j]) for j in range(3)]
    dense_got = send(after(dense_weight, up_got), CROSS)
    back = swap(after(back, dense_got, *feeds))
    dense_other_got = send(after(dense_got, ff_mine), CORE)
    near = jnp.where(
        core == 0, jnp.stack([dense_weight, other[512:]]), jnp.stack([other[512:], dense_weight])
    )
    away = jnp.where(
        core == 0,
        jnp.stack([dense_got, dense_other_got]),
        jnp.stack([dense_other_got, dense_got]),
    )
    dense_all = jnp.where(hi == 0, jnp.concatenate([near, away]), jnp.concatenate([away, near]))
    back = after(back, dense_all)

    d_mixed, merged, given, kept = unpack(
        at, back.reshape(4, 2, 2, 3 * BLK, 128), tables, norm1_t, token_g
    )
    attn_sums = add(at, kept, send(given, CORE))
    attn_mine = swap(attn_sums)
    *parts, e_own, merged_own, vectors = finish(
        at, after(d_mixed, attn_sums), merged, mix, d_norm2, normal, grad_out[0], up_sum, vec
    )
    vectors = add(at, vectors, send(vectors, CORE))
    late = [send(parts[j], (NEXT, CROSS, FAR)[j]) for j in range(3)]
    attn_mine = jnp.sum(attn_mine.astype(F32), 0).astype(BF16)
    gathered = join(at, jnp.concatenate([attn_mine, vectors], 0), 16)
    gathered = swap(gathered)
    grad_up, grad_down = call(
        place_ff_kernel, at, (ff_all,), (struct((256, FF), F32), struct((1024, D), F32)), 0.1
    )
    output, grad_in = own_tokens(
        at, after(inputs[0], grad_up), grad_out[0], e_own, merged_own, feed_own, *late, *feeds, dense_all, vec
    )
    gathered = after(gathered, output, grad_up)
    row = struct((256,), F32)
    grad_mix, grad_dense, *rest = call(
        place_attn_kernel,
        at,
        (gathered,),
        (struct((256, 3 * D), F32), struct((256, D), F32))
        + (row,) * 6
        + (struct((768,), F32), struct((1024,), F32)),
        0.1,
    )
    return (
        output[None],
        grad_in[None],
        rest[0],
        rest[1],
        rest[2],
        rest[3],
        grad_mix,
        rest[6],
        grad_dense,
        rest[4],
        grad_up,
        rest[7],
        grad_down,
        rest[5],
    )


def solution(mesh):
    rows, vec, tokens = P("wa", None), P("wa"), P("wa", "ctx", None)
    return jax.shard_map(
        shards,
        mesh=mesh,
        in_specs=(tokens, vec, vec, vec, vec, rows, vec, rows, vec, rows, vec, rows, vec, tokens),
        out_specs=(
            tokens,
            tokens,
            vec,
            vec,
            vec,
            vec,
            rows,
            vec,
            rows,
            vec,
            rows,
            vec,
            rows,
            vec,
        ),
        check_vma=False,
    )
```

```python
import functools
import math

import jax
import jax.numpy as jnp
from jax import lax
from jax.experimental import pallas as pl
from jax.experimental.pallas import tpu as pltpu
from jax.sharding import PartitionSpec as P

D = 1024
HEADS = 16
HDIM = 64
ROT = 16
FF = 4096
BLK = 192
HALF = 96
EPS = 1e-05
F32 = jnp.float32
BF16 = jnp.bfloat16


def attention_kernel(par_ref, x_ref, out_ref, kvt, s_buf, p_even, p_odd, dkv, *, tq):
    width = 2 * BLK
    step = 2 * tq // width
    groups = x_ref.shape[0] // step
    par = par_ref[0]
    p_bufs = (p_even, p_odd)

    def rows_of(pair, count):
        return pl.ds(pl.multiple_of(pair * width, width), count * width)

    def keys(pair, count):
        return x_ref[pl.ds(pair, count), 0:width, :].reshape(count * width, 128)

    def turn(c, carry):
        kvt[:, rows_of(c * step, step)] = keys(c * step, step).T
        return carry

    lax.fori_loop(0, groups, turn, 0)
    row = lax.broadcasted_iota(jnp.int32, (128, tq), 0)
    lane = lax.broadcasted_iota(jnp.int32, (tq, 128), 1)
    q_idx = lax.broadcasted_iota(jnp.int32, (1, tq), 1)
    q_tok = (q_idx // HALF) * BLK + par * HALF + q_idx % HALF
    zero = jnp.zeros((), F32)

    def own(t):
        half = step // 2
        return ((t * step, half, 0, 0), (t * step + half, half, tq // 2, tq))

    def widen(old, new, qs):
        return new if qs == 0 else jnp.concatenate([old[:, :qs], new], 1)

    def operands(t):
        qd_rows = x_ref[t * step : t * step + step, width : width + BLK, :].reshape(tq, 128)
        return qd_rows, qd_rows.astype(F32).T

    def scores(q_t, top, pair, count, qs=0, first=None):
        s = jnp.dot(keys(pair, count), q_t[:, qs:], preferred_element_type=F32)
        if first is not None:
            k_tok = first + lax.broadcasted_iota(jnp.int32, (count * width, 1), 0)
            s = jnp.where(k_tok <= q_tok[:, qs:], s, -1e30)
        s_buf[rows_of(pair, count), qs:] = s
        high = jnp.max(s.reshape(count * width // 8, 8, tq - qs), 0)
        return widen(top, jnp.maximum(top[:, qs:], high), qs)

    def all_scores(t, qd_t):
        q_t = jnp.where(row < HDIM, qd_t * 0.125, zero).astype(BF16)
        top = jnp.full((8, tq), -1e30, F32)
        if t:
            top = lax.fori_loop(0, t, lambda c, m: scores(q_t, m, c * step, step), top)
        for part in own(t):
            top = scores(q_t, top, *part)
        return jnp.max(top, 0, keepdims=True)

    def weigh(t, top, state, pair, count, qs=0, first=None):
        at = rows_of(pair, count)
        total, out_t = state
        p = jnp.exp(s_buf[at, qs:] - top[:, qs:])
        p_sum = jnp.sum(p.reshape(count * width // 8, 8, tq - qs), 0)
        p_low = p.astype(BF16)
        p_bufs[t % 2][at, qs:] = p_low
        term = jnp.dot(kvt[HDIM:, at], p_low, preferred_element_type=F32)
        return widen(total, total[:, qs:] + p_sum, qs), widen(out_t, out_t[:, qs:] + term, qs)

    def ready(qd_rows, qd_t, state):
        total, out_t = state
        inv = 1.0 / jnp.sum(total, 0, keepdims=True)
        out_t = out_t * inv
        do_t = (qd_t[HDIM:] * inv).astype(BF16)
        delta = jnp.sum(do_t.astype(F32) * out_t, 0, keepdims=True)
        do_full = jnp.concatenate([jnp.zeros((HDIM, tq), BF16), do_t], 0)
        do_rows = do_full.astype(F32).T.astype(BF16)
        q_rows = jnp.where(lane < HDIM, qd_rows.astype(F32) * 0.125, zero).astype(BF16)
        return do_full, do_rows, q_rows, delta, out_t

    def back(t, given, dq_t, pair, count, qs=0, first=None):
        do_full, do_rows, q_rows, delta, _ = given
        at = rows_of(pair, count)
        dp = jnp.dot(keys(pair, count), do_full[:, qs:], preferred_element_type=F32)
        p_low = p_bufs[t % 2][at, qs:]
        ds = (p_low.astype(F32) * (dp - delta[:, qs:])).astype(BF16)
        term = jnp.dot(p_low, do_rows[qs:], preferred_element_type=F32) + jnp.dot(
            ds, q_rows[qs:], preferred_element_type=F32
        )
        if t == groups - 1:
            dkv[at, :] = term
        else:
            dkv[at, :] += term
        dq = jnp.dot(kvt[:HDIM, at], ds, preferred_element_type=F32)
        return widen(dq_t, dq_t[:, qs:] + dq, qs)

    def finish_group(t, given, dq_t):
        out = jnp.concatenate([dq_t * 0.125, given[4]], 0).T.astype(BF16)
        out_ref[t * step : t * step + step, width : width + BLK, :] = out.reshape(step, BLK, 128)

    half = step // 2
    given = None
    for t in reversed(range(groups)):
        rows_t = operands(t)
        top = all_scores(t, rows_t[1])
        state = (jnp.zeros((8, tq), F32), jnp.zeros((HDIM, tq), F32))
        dq_t = jnp.zeros((HDIM, tq), F32)
        if given is None:
            if t:
                state = lax.fori_loop(
                    0, t, lambda c, s, t=t, top=top: weigh(t, top, s, c * step, step), state
                )
            for part in own(t):
                state = weigh(t, top, state, *part)
        else:

            def both(c, carry, t=t, top=top, given=given):
                state, dq_t = carry
                state = weigh(t, top, state, c * half, half)
                return state, back(t + 1, given, dq_t, c * half, half)

            if t:
                state, dq_t = lax.fori_loop(0, 2 * t, both, (state, dq_t))
            for u in range(2):
                dq_t = back(t + 1, given, dq_t, t * step + u * half, half)
            for part in own(t):
                state = weigh(t, top, state, *part)
            for part in own(t + 1):
                dq_t = back(t + 1, given, dq_t, *part)
            finish_group(t + 1, given, dq_t)
        given = ready(*rows_t, state)
    dq_t = jnp.zeros((HDIM, tq), F32)
    for part in own(0):
        dq_t = back(0, given, dq_t, *part)
    finish_group(0, given, dq_t)

    def drain(c, carry):
        rows = dkv[rows_of(c * step, step), :].astype(BF16)
        out_ref[pl.ds(c * step, step), 0:width, :] = rows.reshape(step, width, 128)
        return carry

    lax.fori_loop(0, groups, drain, 0)


def attention(par, x, tq=768):
    n_keys = x.shape[0] * 2 * BLK
    whole = pl.BlockSpec(x.shape, lambda i: (0, 0, 0), pipeline_mode=pl.Buffered(1))
    return pl.pallas_call(
        functools.partial(attention_kernel, tq=tq),
        grid=(1,),
        out_shape=jax.ShapeDtypeStruct(x.shape, BF16),
        in_specs=[pl.BlockSpec(memory_space=pltpu.SMEM), whole],
        out_specs=whole,
        scratch_shapes=[
            pltpu.VMEM((128, n_keys), BF16),
            pltpu.VMEM((n_keys, tq), F32),
            pltpu.VMEM((n_keys - 2 * tq, tq), BF16),
            pltpu.VMEM((n_keys, tq), BF16),
            pltpu.VMEM((n_keys, 128), F32),
        ],
        compiler_params=pltpu.CompilerParams(vmem_limit_bytes=63 * 2**20),
        cost_estimate=cost(46),
    )(par, x)


def cost(micros):
    return pl.CostEstimate(flops=int(micros * 1.1e9), bytes_accessed=10**5, transcendentals=0)


def normalize(values):
    centred = values - jnp.mean(values, -1, keepdims=True)
    spread = jnp.mean(centred * centred, -1, keepdims=True)
    inv = lax.rsqrt(spread + EPS)
    return centred * inv, inv


def norm_back(normal, inv, e):
    return inv * (
        e
        - jnp.mean(e, -1, keepdims=True)
        - normal * jnp.mean(e * normal, -1, keepdims=True)
    )


def dot(a, b):
    return jnp.dot(a, b, preferred_element_type=F32)


def dot_t(a, b):
    return lax.dot_general(a, b, (((1,), (1,)), ((), ())), preferred_element_type=F32)


def t_dot(a, b):
    return lax.dot_general(a, b, (((0,), (0,)), ((), ())), preferred_element_type=F32)


AX = ("ctx", "wa")
YZ = [[2 * i + lo for i in range(16)] for lo in range(2)]
SMEM = pl.BlockSpec(memory_space=pltpu.SMEM)


def route(move):
    pairs = []
    for ctx in range(32):
        for wa in range(4):
            to_x, y, z, core = move(wa // 2 * 2 + ctx % 2, ctx // 8, ctx // 2 % 4, wa % 2)
            to_ctx, to_wa = y * 8 + z * 2 + to_x % 2, to_x // 2 * 2 + core
            pairs.append((ctx * 4 + wa, to_ctx * 4 + to_wa))
    return pairs


CORE = route(lambda x, y, z, c: (x, y, z, 1 - c))
CROSS = route(lambda x, y, z, c: (3 - x, y, z, c))
FAR = route(lambda x, y, z, c: (x ^ 2, y, z, c))
NEXT = route(lambda x, y, z, c: (x ^ 1, y, z, c))
ASIDE = route(lambda x, y, z, c: (x ^ 1, y, z, 1 - c))
TREE = (0, 1, 3, 2)


def send(value, pairs):
    return lax.ppermute(value, AX, pairs)


def pick(array, index, axis=0):
    return lax.dynamic_index_in_dim(array, index, axis, keepdims=False)


def after(value, *first):
    return lax.optimization_barrier((value, *first))[0]


def swap(pieces):
    return lax.all_to_all(pieces, "ctx", 0, 0, axis_index_groups=YZ, tiled=True)


def call(kernel, at, operands, outs, micros, scratch=()):
    def whole(a):
        return pl.BlockSpec(a.shape, lambda i: (0,) * len(a.shape), pipeline_mode=pl.Buffered(1))

    return pl.pallas_call(
        kernel,
        grid=(1,),
        out_shape=tuple(outs),
        in_specs=[SMEM] + [whole(a) for a in operands],
        out_specs=tuple(whole(a) for a in outs),
        scratch_shapes=list(scratch),
        compiler_params=pltpu.CompilerParams(vmem_limit_bytes=63 * 2**20),
        cost_estimate=cost(micros),
    )(at, *operands)


def struct(shape, dtype=BF16):
    return jax.ShapeDtypeStruct(shape, dtype)


def pack_kernel(at_ref, mix_ref, up_ref, dense_ref, small_ref, own, mix_cross, up_cross):
    for k, (mix_out, up_out) in enumerate(((own.at[0:256], own.at[256:512]), (mix_cross, up_cross))):
        q = at_ref[0] if k == 0 else 3 - at_ref[0]
        for j in range(3):
            cols = pl.ds(pl.multiple_of(q * 256 + j * 1024, 256), 256)
            mix_out[0:256, 256 * j : 256 * j + 256] = mix_ref[:, cols]
        if k == 0:
            mix_out[0:16, 768:1024] = small_ref[...]
            mix_out[16:256, 768:1024] = jnp.zeros((240, 256), BF16)
        else:
            mix_out[256:272, 0:256] = small_ref[...]
            mix_out[256:272, 256:768] = jnp.zeros((16, 512), BF16)
        up_out[...] = up_ref[:, pl.ds(pl.multiple_of(q * 1024, 1024), 1024)]
    own[512:768, :] = dense_ref[...]


def tables_kernel(at_ref, tables):
    shape = (BLK, 128)
    feature = lax.broadcasted_iota(jnp.int32, shape, 1) % HDIM
    exponent = (feature % 8).astype(F32) * (2.0 / ROT)
    inverse = jnp.exp(exponent * -math.log(10000.0))
    for block in range(2):
        spot = at_ref[4] * (2 * BLK) + block * BLK + lax.broadcasted_iota(jnp.int32, shape, 0)
        angle = spot.astype(F32) * inverse
        sine = jnp.sin(angle)
        tables[0, block] = jnp.where(feature < ROT, jnp.cos(angle), 1.0)
        tables[1, block] = jnp.where(feature < ROT // 2, -sine, 0.0)
        tables[2, block] = jnp.where((feature >= ROT // 2) & (feature < ROT), sine, 0.0)


def turn_lanes(pair, cos, sin_up, sin_down):
    return pair * cos + pltpu.roll(pair, 120, 1) * sin_up + pltpu.roll(pair, 8, 1) * sin_down


def project_kernel(at_ref, *refs):
    tokens, tail, mixes = refs[0:4], refs[4], refs[5:9]
    tables = refs[9]
    sent, vec_out, mix_out, dense_out = refs[10:14]
    x, core = at_ref[0], at_ref[1]
    hi, lo = x // 2, x % 2
    quarters = (2 * hi + core, 2 * (1 - hi) + core, 2 * hi + 1 - core, 2 * (1 - hi) + 1 - core)
    for w, piece in zip(quarters, mixes):
        cols = pl.ds(pl.multiple_of(w * 256, 256), 256)
        mix_out[cols, :] = piece[0:256, 0:768]
        if piece.shape[0] == 272:
            vec_out[0:16, cols] = piece[256:272, 0:256].astype(F32)
        else:
            vec_out[0:16, cols] = piece[0:16, 768:1024].astype(F32)

    @pl.when(core == lo)
    def _():
        dense_out[...] = mixes[0][512:768, :]

    @pl.when(core != lo)
    def _():
        dense_out[...] = mixes[2][512:768, :]

    for j in range(3):
        n = 4 * j + x
        row = vec_out[6:9, pl.ds(pl.multiple_of((n // 3) * 256, 256), 256)]
        keep = lax.broadcasted_iota(jnp.int32, (3, 256), 0) == n % 3
        vec_out[16:17, 256 * j : 256 * j + 256] = jnp.sum(
            jnp.where(keep, row, 0.0), 0, keepdims=True
        )
    for j in range(4):
        vec_out[17:18, 256 * j : 256 * j + 256] = vec_out[
            9 + j : 10 + j, pl.ds(pl.multiple_of(x * 256, 256), 256)
        ]
    gain1, shift1 = vec_out[0:1, :], vec_out[1:2, :]
    bias = vec_out[16:17, 0:768]
    lane = lax.broadcasted_iota(jnp.int32, (BLK, 128), 1)
    left = lane < HDIM
    for j in range(4):
        chip = lax.bitwise_xor(x, TREE[j])
        to_hi, to_lo = chip // 2, chip % 2
        normal, _ = normalize(tokens[j][0:BLK, :].astype(F32))
        low1 = (normal * gain1 + shift1).astype(BF16)
        grad = tokens[j][BLK : 2 * BLK, :]
        if j == 3:
            grad = jnp.concatenate([grad, tail[...]], 0)
        mixed = dot(low1, mix_out[...]) + bias
        d_merged = dot_t(grad, dense_out[...])
        cos, sin_up, sin_down = tables[0, to_lo], tables[1, to_lo], tables[2, to_lo]
        for h in range(2):
            cols = slice(128 * h, 128 * h + 128)
            q = turn_lanes(mixed[:, 0:256][:, cols], cos, sin_up, sin_down)
            k = turn_lanes(mixed[:, 256:512][:, cols], cos, sin_up, sin_down)
            v = mixed[:, 512:768][:, cols]
            dm = d_merged[:, cols]
            for side in range(2):
                if side == 0:
                    kv = jnp.where(left, k, pltpu.roll(v, 64, 1)).astype(BF16)
                    qd = jnp.where(left, q, pltpu.roll(dm, 64, 1)).astype(BF16)
                else:
                    kv = jnp.where(left, pltpu.roll(k, 64, 1), v).astype(BF16)
                    qd = jnp.where(left, pltpu.roll(q, 64, 1), dm).astype(BF16)
                i = 2 * h + side
                for half in range(2):
                    at = pl.ds(pl.multiple_of(to_lo * BLK, BLK), BLK)
                    sent[i, to_hi, half, at, :] = kv
                    at = pl.ds(pl.multiple_of(2 * BLK + to_lo * HALF, HALF), HALF)
                    sent[i, to_hi, half, at, :] = qd[HALF * half : HALF * half + HALF]


def project(at, tokens, mixes, tables):
    outs = (struct((4, 2, 2, 3 * BLK, 128)), struct((24, D), F32))
    scratch = [pltpu.VMEM((D, 768), BF16), pltpu.VMEM((256, D), BF16)]
    return call(project_kernel, at, (*tokens, *mixes, tables), outs, 0.1, scratch)


def mlp_kernel(at_ref, *refs):
    tokens, tail, refs = refs[0:4], refs[4], refs[1:]
    vec, ups, downs, mixes = refs[4], refs[5:9], refs[9:11], refs[11:13]
    normal_out, norm1_t, g_out, d_norm2, given, kept = refs[13:19]
    feed_sent, feed_own, sums, mix = refs[19:22], *refs[22:25]
    norm1, norm2, norm2_t, hidden, hidden_t, d_pre, up, down = refs[25:33]
    x, core = at_ref[0], at_ref[1]
    hi, lo = x // 2, x % 2
    quarters = (2 * hi + core, 2 * (1 - hi) + core, 2 * hi + 1 - core, 2 * (1 - hi) + 1 - core)
    for w, piece in zip(quarters, ups):
        rows = slice(256, 512) if piece.shape[0] > 256 else slice(0, 256)
        at = pl.ds(pl.multiple_of(w * 256, 256), 256)
        up[at, :] = piece[rows, :]
        if piece.shape[0] > 256:
            mix[at, :] = piece[0:256, 0:768]
    for w, piece in zip((quarters[1], quarters[3]), mixes):
        mix[pl.ds(pl.multiple_of(w * 256, 256), 256), :] = piece[0:256, :]

    @pl.when(core == lo)
    def _():
        down[...] = downs[0][...]

    @pl.when(core != lo)
    def _():
        down[...] = downs[1][...]

    for j in range(4):
        rows = slice(BLK * j, BLK * j + BLK)
        normal, _ = normalize(tokens[j][0:BLK, :].astype(F32))
        normal_out[rows, :] = normal.astype(BF16)
        norm1[rows, :] = (normal * vec[0:1, :] + vec[1:2, :]).astype(BF16)
        norm2[rows, :] = (normal * vec[2:3, :] + vec[3:4, :]).astype(BF16)
        grad = tokens[j][BLK : 2 * BLK, :]
        if j == 3:
            grad = jnp.concatenate([grad, tail[...]], 0)
        g_out[rows, :] = grad
    for k in range(4):
        cols = slice(256 * k, 256 * k + 256)
        pre = dot(norm2[...], up[:, cols]) + vec[17:18, cols]
        below = 0.5 + 0.5 * lax.erf(pre * 0.5**0.5)
        hidden[:, cols] = (pre * below).astype(BF16)
        bell = jnp.exp(-0.5 * pre * pre) * (0.5 / math.pi) ** 0.5
        dp = (dot_t(g_out[...], down[cols, :]) * (below + pre * bell)).astype(BF16)
        d_pre[:, cols] = dp
        sums[:, cols] = jnp.sum(dp.astype(F32), 0, keepdims=True)
    d_norm2[...] = dot_t(d_pre[...], up[...]).astype(BF16)
    for j in range(4):
        feed = dot(hidden[BLK * j : BLK * j + BLK, :], down[...])
        if j == 0:
            feed_own[...] = feed
        else:
            feed_sent[j - 1][...] = feed.astype(BF16)
    for k in range(8):
        at = slice(128 * k, 128 * k + 128)
        norm1_t[at, :] = norm1[:, at].T
        norm2_t[at, :] = norm2[:, at].T
        hidden_t[at, :] = hidden[:, at].T
    for c, out in ((1 - core, given), (core, kept)):
        for w in range(2):
            rows = pl.ds(pl.multiple_of(512 * w + 256 * c, 256), 256)
            part = dot(norm2_t[rows, :], d_pre[...])
            out[:, 16 * w : 16 * w + 16, :] = part.reshape(16, 16, 1024).astype(out.dtype)
        part = dot(hidden_t[pl.ds(pl.multiple_of(512 * c, 512), 512), :], g_out[...])
        out[:, 32:64, :] = part.reshape(16, 32, 1024).astype(out.dtype)


def feed_forward(at, *operands):
    outs = (
        struct((768, D)),
        struct((D, 768)),
        struct((768, D)),
        struct((768, D)),
        struct((16, 64, 1024)),
        struct((16, 64, 1024)),
        struct((BLK, D)),
        struct((BLK, D)),
        struct((BLK, D)),
        struct((BLK, D), F32),
        struct((1, 1024), F32),
        struct((D, 768)),
    )
    rows, columns = pltpu.VMEM((768, D), BF16), pltpu.VMEM((D, 768), BF16)
    square = pltpu.VMEM((D, 1024), BF16)
    scratch = (rows, rows, columns, rows, columns, rows, square, square)
    return call(mlp_kernel, at, operands, outs, 0.1, scratch)


def add_kernel(at_ref, a, b, out):
    out[...] = (a[...].astype(F32) + b[...].astype(F32)).astype(out.dtype)


def add(at, a, b):
    return call(add_kernel, at, (a, b), (struct(a.shape),), 0.1)[0]


def unpack_kernel(at_ref, back, tables, norm1_t, g_ref, d_mixed, merged, given, kept):
    core = at_ref[1]
    lane = lax.broadcasted_iota(jnp.int32, (BLK, 128), 1)
    left = lane < HDIM
    for j in range(4):
        if True:
            chip = lax.bitwise_xor(at_ref[0], TREE[j])
            hi, lo = chip // 2, chip % 2
            cos, sin_up, sin_down = tables[0, lo], tables[1, lo], tables[2, lo]
            rows = slice(j * BLK, j * BLK + BLK)
            for h in range(2):
                kv, qo = [], []
                for i in (2 * h, 2 * h + 1):
                    at = pl.ds(pl.multiple_of(lo * BLK, BLK), BLK)
                    kv.append(back[i, hi, 0, at, :].astype(F32) + back[i, hi, 1, at, :].astype(F32))
                    at = pl.ds(pl.multiple_of(2 * BLK + lo * HALF, HALF), HALF)
                    halves = [back[i, hi, s, at, :] for s in range(2)]
                    qo.append(jnp.concatenate(halves, 0).astype(F32))
                dq = jnp.where(left, qo[0], pltpu.roll(qo[1], 64, 1))
                out = jnp.where(left, pltpu.roll(qo[0], 64, 1), qo[1])
                dk = jnp.where(left, kv[0], pltpu.roll(kv[1], 64, 1))
                dv = jnp.where(left, pltpu.roll(kv[0], 64, 1), kv[1])
                dq = turn_lanes(dq, cos, -sin_up, -sin_down)
                dk = turn_lanes(dk, cos, -sin_up, -sin_down)
                for k, value in enumerate((dq, dk, dv)):
                    at = 256 * k + 128 * h
                    d_mixed[rows, at : at + 128] = value.astype(BF16)
                merged[rows, 128 * h : 128 * h + 128] = out.astype(BF16)
    merged_t = merged[...].astype(F32).T.astype(BF16)
    dense = dot(merged_t, g_ref[...])
    for c, out in ((1 - core, given), (core, kept)):
        for hi in range(2):
            rows = pl.ds(pl.multiple_of(512 * hi + 256 * c, 256), 256)
            part = dot(norm1_t[rows, :], d_mixed[...])
            out[:, 16 * hi : 16 * hi + 16, 0:768] = part.reshape(16, 16, 768).astype(out.dtype)
        half = jnp.where(c == 0, dense[0:128], dense[128:256]).astype(out.dtype)
        for i in range(4):
            for j in range(4):
                out[4 * i + j, :, 768:1024] = half[32 * i : 32 * i + 32, 256 * j : 256 * j + 256]


def unpack(at, *operands):
    outs = (
        struct((768, 768)),
        struct((768, 256)),
        struct((16, 32, 1024)),
        struct((16, 32, 1024)),
    )
    return call(unpack_kernel, at, operands, outs, 100)


def finish_kernel(
    at_ref, d_mixed, merged, mix, d_norm2, normal, g_own, up_sum, vec, *refs
):
    parts, e_own, merged_own, sums = refs[0:3], *refs[3:6]
    gain1, gain2 = vec[0:1, :], vec[2:3, :]
    totals = [jnp.zeros((1, D), F32) for _ in range(4)]
    for j in range(4):
        rows = slice(j * BLK, j * BLK + BLK)
        d1 = dot_t(d_mixed[rows, :], mix[...])
        d2 = d_norm2[rows, :].astype(F32)
        n = normal[rows, :].astype(F32)
        e = gain1 * d1 + gain2 * d2
        if j == 0:
            e_own[...] = e
            merged_own[...] = merged[rows, :]
        else:
            parts[j - 1][0:BLK, :] = e.astype(BF16)
            heads = merged[rows, :]
            for k in range(4):
                cols = slice(256 * k, 256 * k + 256)
                parts[j - 1][BLK : BLK + 48, cols] = heads[48 * k : 48 * k + 48]
        for k, value in enumerate((d1 * n, d1, d2 * n, d2)):
            totals[k] = totals[k] + jnp.sum(value, 0, keepdims=True)
    for k in range(4):
        sums[k : k + 1, :] = totals[k].astype(BF16)
    sums[4:5, :] = jnp.sum(g_own[...].astype(F32), 0, keepdims=True).astype(BF16)
    sums[5:6, :] = jnp.zeros((1, D), BF16)
    sums[5:6, 0:768] = jnp.sum(d_mixed[...].astype(F32), 0, keepdims=True).astype(BF16)
    sums[6:7, :] = up_sum[...].astype(BF16)
    sums[7:8, :] = jnp.zeros((1, D), BF16)


def finish(at, *operands):
    outs = (
        struct((BLK + 48, D)),
        struct((BLK + 48, D)),
        struct((BLK + 48, D)),
        struct((BLK, D), F32),
        struct((BLK, 256)),
        struct((8, D)),
    )
    return call(finish_kernel, at, operands, outs, 0.1)


def tokens_kernel(at_ref, x_ref, g_ref, *refs):
    e_own, merged_own, feed_own = refs[0:3]
    late, feeds = refs[3:6], refs[6:9]
    dense, vec, out, grad_in = refs[9:13]
    x = at_ref[0]
    tokens = x_ref[...].astype(F32)
    total = tokens + vec[4:5, :] + vec[5:6, :] + feed_own[...]
    total = total + dot(merged_own[...], dense[x])
    e = e_own[...]
    for j in range(3):
        total = total + feeds[j][...].astype(F32)
        heads = jnp.concatenate(
            [late[j][BLK : BLK + 48, 256 * k : 256 * k + 256] for k in range(4)], 0
        )
        total = total + dot(heads, dense[lax.bitwise_xor(x, TREE[j + 1])])
        e = e + late[j][0:BLK, :].astype(F32)
    out[...] = total.astype(BF16)
    normal, inv = normalize(tokens)
    grad_in[...] = (g_ref[...].astype(F32) + norm_back(normal, inv, e)).astype(BF16)


def own_tokens(at, *operands):
    return call(tokens_kernel, at, operands, (struct((BLK, D)),) * 2, 0.1)


def join_kernel(at_ref, own, beside, across, far, sibling, aside, out, scratch):
    hi, lo, core = at_ref[0] // 2, at_ref[0] % 2, at_ref[1]
    rows = pl.ds(pl.multiple_of(hi * 16, 16), 16)
    ring = (own, beside, across, far)
    ff = own.shape[0] == 64
    if ff:
        box, places = (slice(32, 64), slice(0, 1024)), ((64, 0), (96, 0))
        width = 1024
    else:
        box, places = (slice(0, 32), slice(768, 1024)), ((0, 768), (32, 768))
        width = 768
    for j in range(4):
        value = ring[j][rows, 0:width]
        for i in range(16):
            if i < out.shape[0]:
                out[i, 16 * j : 16 * j + 16, 0:width] = value
    for (row, column), near, off in zip(places, (own, sibling), (beside, aside)):
        value = jnp.where(core == lo, near[box], off[box])
        for i in range(out.shape[0]):
            out[i, row : row + 32, column : column + value.shape[1]] = value
    if not ff:
        quarter = 2 * hi + core
        chips = [r[32:40, :].astype(F32) for r in ring]
        scratch[0:5, :] = sum(c[0:5] for c in chips)
        for j in range(4):
            chip = lax.bitwise_xor(at_ref[0], TREE[j])
            scratch[pl.ds(8 + chip, 1), :] = chips[j][5:6]
            scratch[pl.ds(12 + chip, 1), :] = chips[j][6:7]
        cols = pl.ds(pl.multiple_of(quarter * 256, 256), 256)
        parts = [scratch[k : k + 1, cols] for k in range(5)]
        for k in range(3):
            n = 3 * quarter + k
            cols = pl.ds(pl.multiple_of(n // 4 * 256, 256), 256)
            parts.append(scratch[pl.ds(8 + n % 4, 1), cols])
        vec = [jnp.concatenate(parts[0:4], 1), jnp.concatenate(parts[4:8], 1)]
        vec += [scratch[pl.ds(12 + quarter, 1), :], jnp.zeros((5, 1024), F32)]
        vec = jnp.concatenate(vec, 0).astype(BF16)
        for i in range(16):
            out[i, 64:72, :] = vec


def join(at, own, count):
    parts = [send(own, p) for p in (NEXT, CROSS, FAR, CORE, ASIDE)]
    rows = 128 if own.shape[0] == 64 else 72
    scratch = [pltpu.VMEM((16, 1024), F32)]
    return call(join_kernel, at, (own, *parts), (struct((count, rows, 1024)),), 0.1, scratch)[0]


def place_ff_kernel(at_ref, sums, up_out, down_out):
    x, core = at_ref[0], at_ref[1]
    for j in range(4):
        cols = pl.ds(pl.multiple_of(lax.bitwise_xor(x, TREE[j]) * 1024, 1024), 1024)
        up_out[:, cols] = sums[:, 16 * j : 16 * j + 16, :].reshape(256, 1024).astype(F32)
    for side, at in ((core, 64), (1 - core, 96)):
        rows = pl.ds(pl.multiple_of(side * 512, 512), 512)
        down_out[rows, :] = sums[:, at : at + 32, :].reshape(512, 1024).astype(F32)


def place_attn_kernel(at_ref, sums, mix_out, dense_out, *vec_outs):
    x, core = at_ref[0], at_ref[1]
    for j in range(4):
        chip = lax.bitwise_xor(x, TREE[j])
        for k in range(3):
            cols = pl.ds(pl.multiple_of(k * 1024 + chip * 256, 256), 256)
            part = sums[:, 16 * j : 16 * j + 16, 256 * k : 256 * k + 256]
            mix_out[:, cols] = part.reshape(256, 256).astype(F32)
    for side, at in ((core, 0), (1 - core, 32)):
        for i in range(4):
            rows = pl.ds(pl.multiple_of(side * 128 + i * 32, 32), 32)
            for j in range(4):
                part = sums[4 * i + j, at : at + 32, 768:1024]
                dense_out[rows, 256 * j : 256 * j + 256] = part.astype(F32)
    total = jnp.zeros((8, 1024), F32)
    for i in range(16):
        total = total + sums[i, 64:72, :].astype(F32)
    for k in range(5):
        vec_outs[k][...] = total[k // 4, 256 * (k % 4) : 256 * (k % 4) + 256]
    vec_outs[5][...] = total[1, 0:256]
    vec_outs[6][...] = total[1, 256:1024]
    vec_outs[7][...] = total[2, :]


def shards(
    inputs,
    first_gain,
    first_bias,
    second_gain,
    second_bias,
    mix_weight,
    mix_bias,
    dense_weight,
    dense_bias,
    up_weight,
    up_bias,
    down_weight,
    down_bias,
    grad_out,
):
    ctx, wa = lax.axis_index("ctx"), lax.axis_index("wa")
    lo, yz, hi, core = ctx % 2, ctx // 2, wa // 2, wa % 2
    x = 2 * hi + lo
    at = jnp.stack([x, core, yz // 4, yz % 4, yz])

    both = jnp.concatenate([inputs[0], grad_out[0]], 0)
    beside, across = send(both, NEXT), send(both, CROSS)
    far = send(after(across[:256], beside), NEXT)
    tail = send(after(beside[256:], across), CROSS)
    tokens = (both, beside, across, far, tail)
    small, filled = 0, 0
    for v in (
        first_gain,
        first_bias,
        second_gain,
        second_bias,
        dense_bias,
        down_bias,
        mix_bias,
        up_bias,
    ):
        rows = v.shape[0] // 256
        small = small + jnp.pad(v.reshape(rows, 256), ((filled, 16 - filled - rows), (0, 0)))
        filled += rows
    tables = call(tables_kernel, at, (), (struct((3, 2, BLK, 128), F32),), 0.1)[0]
    own, mix_cross, up_cross = call(
        pack_kernel,
        at,
        (mix_weight, up_weight, dense_weight, after(small, tables)),
        (struct((768, 1024)), struct((272, 768)), struct((256, 1024))),
        0.1,
    )
    mix_got = send(after(mix_cross, beside, across), CROSS)
    other = send(own, CORE)
    mix_other_got = send(mix_got, CORE)
    up_got = send(after(up_cross, across, mix_got, tail), CROSS)
    up_other_got = send(up_got, CORE)
    down_other = send(after(down_weight, across), CORE)

    sent, vec = project(at, tokens, (own, mix_got, other, mix_other_got), tables)
    held = swap(sent.reshape(16, 3 * BLK, 128))

    up_other_got = send(after(up_got, sent), CORE)
    normal, norm1_t, token_g, d_norm2, given, kept, *feed_sent, feed_own, up_sum, mix = feed_forward(
        at,
        *tokens,
        vec,
        own,
        up_got,
        other,
        up_other_got,
        down_weight,
        down_other,
        mix_got,
        mix_other_got,
    )
    ff_sums = add(at, kept, send(given, CORE))
    ff_mine = swap(after(ff_sums, held))
    back = attention((yz % 2).reshape(1), after(held, ff_sums))
    ff_mine = jnp.sum(after(ff_mine, back).astype(F32), 0).astype(BF16)
    ff_all = join(at, ff_mine, 1)[0]
    ff_all = lax.all_gather(ff_all, "ctx", axis=0, axis_index_groups=YZ, tiled=False)

    feeds = [send(feed_sent[j], (NEXT, CROSS, FAR)[j]) for j in range(3)]
    dense_got = send(after(dense_weight, up_got), CROSS)
    back = swap(after(back, dense_got, *feeds))
    dense_other_got = send(after(dense_got, ff_mine), CORE)
    near = jnp.where(
        core == 0, jnp.stack([dense_weight, other[512:]]), jnp.stack([other[512:], dense_weight])
    )
    away = jnp.where(
        core == 0,
        jnp.stack([dense_got, dense_other_got]),
        jnp.stack([dense_other_got, dense_got]),
    )
    dense_all = jnp.where(hi == 0, jnp.concatenate([near, away]), jnp.concatenate([away, near]))
    back = after(back, dense_all)

    d_mixed, merged, given, kept = unpack(
        at, back.reshape(4, 2, 2, 3 * BLK, 128), tables, norm1_t, token_g
    )
    attn_sums = add(at, kept, send(given, CORE))
    attn_mine = swap(attn_sums)
    *parts, e_own, merged_own, vectors = finish(
        at, after(d_mixed, attn_sums), merged, mix, d_norm2, normal, grad_out[0], up_sum, vec
    )
    vectors = add(at, vectors, send(vectors, CORE))
    late = [send(parts[j], (NEXT, CROSS, FAR)[j]) for j in range(3)]
    attn_mine = jnp.sum(attn_mine.astype(F32), 0).astype(BF16)
    gathered = join(at, jnp.concatenate([attn_mine, vectors], 0), 16)
    gathered = swap(gathered)
    grad_up, grad_down = call(
        place_ff_kernel, at, (ff_all,), (struct((256, FF), F32), struct((1024, D), F32)), 0.1
    )
    output, grad_in = own_tokens(
        at, after(inputs[0], grad_up), grad_out[0], e_own, merged_own, feed_own, *late, *feeds, dense_all, vec
    )
    gathered = after(gathered, output, grad_up)
    row = struct((256,), F32)
    grad_mix, grad_dense, *rest = call(
        place_attn_kernel,
        at,
        (gathered,),
        (struct((256, 3 * D), F32), struct((256, D), F32))
        + (row,) * 6
        + (struct((768,), F32), struct((1024,), F32)),
        0.1,
    )
    return (
        output[None],
        grad_in[None],
        rest[0],
        rest[1],
        rest[2],
        rest[3],
        grad_mix,
        rest[6],
        grad_dense,
        rest[4],
        grad_up,
        rest[7],
        grad_down,
        rest[5],
    )


def solution(mesh):
    rows, vec, tokens = P("wa", None), P("wa"), P("wa", "ctx", None)
    return jax.shard_map(
        shards,
        mesh=mesh,
        in_specs=(tokens, vec, vec, vec, vec, rows, vec, rows, vec, rows, vec, rows, vec, tokens),
        out_specs=(
            tokens,
            tokens,
            vec,
            vec,
            vec,
            vec,
            rows,
            vec,
            rows,
            vec,
            rows,
            vec,
            rows,
            vec,
        ),
        check_vma=False,
    )
```

```python
import functools
import math

import jax
import jax.numpy as jnp
from jax import lax
from jax.experimental import pallas as pl
from jax.experimental.pallas import tpu as pltpu
from jax.sharding import PartitionSpec as P

D = 1024
HEADS = 16
HDIM = 64
ROT = 16
FF = 4096
BLK = 192
HALF = 96
EPS = 1e-05
F32 = jnp.float32
BF16 = jnp.bfloat16


def attention_kernel(par_ref, x_ref, out_ref, kvt, s_buf, p_even, p_odd, dkv, *, tq):
    width = 2 * BLK
    step = 2 * tq // width
    groups = x_ref.shape[0] // step
    par = par_ref[0]
    p_bufs = (p_even, p_odd)

    def rows_of(pair, count):
        return pl.ds(pl.multiple_of(pair * width, width), count * width)

    def keys(pair, count):
        return x_ref[pl.ds(pair, count), 0:width, :].reshape(count * width, 128)

    def turn(c, carry):
        kvt[:, rows_of(c * step, step)] = keys(c * step, step).T
        return carry

    lax.fori_loop(0, groups, turn, 0)
    row = lax.broadcasted_iota(jnp.int32, (128, tq), 0)
    lane = lax.broadcasted_iota(jnp.int32, (tq, 128), 1)
    q_idx = lax.broadcasted_iota(jnp.int32, (1, tq), 1)
    q_tok = (q_idx // HALF) * BLK + par * HALF + q_idx % HALF
    zero = jnp.zeros((), F32)

    def own(t):
        half = step // 2
        return ((t * step, half, 0, 0), (t * step + half, half, tq // 2, tq))

    def widen(old, new, qs):
        return new if qs == 0 else jnp.concatenate([old[:, :qs], new], 1)

    def operands(t):
        qd_rows = x_ref[t * step : t * step + step, width : width + BLK, :].reshape(tq, 128)
        return qd_rows, qd_rows.astype(F32).T

    def scores(q_t, top, pair, count, qs=0, first=None):
        s = jnp.dot(keys(pair, count), q_t[:, qs:], preferred_element_type=F32)
        if first is not None:
            k_tok = first + lax.broadcasted_iota(jnp.int32, (count * width, 1), 0)
            s = jnp.where(k_tok <= q_tok[:, qs:], s, -1e30)
        s_buf[rows_of(pair, count), qs:] = s
        high = jnp.max(s.reshape(count * width // 8, 8, tq - qs), 0)
        return widen(top, jnp.maximum(top[:, qs:], high), qs)

    def all_scores(t, qd_t):
        q_t = jnp.where(row < HDIM, qd_t * 0.125, zero).astype(BF16)
        top = jnp.full((8, tq), -1e30, F32)
        if t:
            top = lax.fori_loop(0, t, lambda c, m: scores(q_t, m, c * step, step), top)
        for part in own(t):
            top = scores(q_t, top, *part)
        return jnp.max(top, 0, keepdims=True)

    def weigh(t, top, state, pair, count, qs=0, first=None):
        at = rows_of(pair, count)
        total, out_t = state
        p = jnp.exp(s_buf[at, qs:] - top[:, qs:])
        p_sum = jnp.sum(p.reshape(count * width // 8, 8, tq - qs), 0)
        p_low = p.astype(BF16)
        p_bufs[t % 2][at, qs:] = p_low
        term = jnp.dot(kvt[HDIM:, at], p_low, preferred_element_type=F32)
        return widen(total, total[:, qs:] + p_sum, qs), widen(out_t, out_t[:, qs:] + term, qs)

    def ready(qd_rows, qd_t, state):
        total, out_t = state
        inv = 1.0 / jnp.sum(total, 0, keepdims=True)
        out_t = out_t * inv
        do_t = (qd_t[HDIM:] * inv).astype(BF16)
        delta = jnp.sum(do_t.astype(F32) * out_t, 0, keepdims=True)
        do_full = jnp.concatenate([jnp.zeros((HDIM, tq), BF16), do_t], 0)
        do_rows = do_full.astype(F32).T.astype(BF16)
        q_rows = jnp.where(lane < HDIM, qd_rows.astype(F32) * 0.125, zero).astype(BF16)
        return do_full, do_rows, q_rows, delta, out_t

    def back(t, given, dq_t, pair, count, qs=0, first=None):
        do_full, do_rows, q_rows, delta, _ = given
        at = rows_of(pair, count)
        dp = jnp.dot(keys(pair, count), do_full[:, qs:], preferred_element_type=F32)
        p_low = p_bufs[t % 2][at, qs:]
        ds = (p_low.astype(F32) * (dp - delta[:, qs:])).astype(BF16)
        term = jnp.dot(p_low, do_rows[qs:], preferred_element_type=F32) + jnp.dot(
            ds, q_rows[qs:], preferred_element_type=F32
        )
        if t == groups - 1:
            dkv[at, :] = term
        else:
            dkv[at, :] += term
        dq = jnp.dot(kvt[:HDIM, at], ds, preferred_element_type=F32)
        return widen(dq_t, dq_t[:, qs:] + dq, qs)

    def finish_group(t, given, dq_t):
        out = jnp.concatenate([dq_t * 0.125, given[4]], 0).T.astype(BF16)
        out_ref[t * step : t * step + step, width : width + BLK, :] = out.reshape(step, BLK, 128)

    half = step // 2
    given = None
    for t in reversed(range(groups)):
        rows_t = operands(t)
        top = all_scores(t, rows_t[1])
        state = (jnp.zeros((8, tq), F32), jnp.zeros((HDIM, tq), F32))
        dq_t = jnp.zeros((HDIM, tq), F32)
        if given is None:
            if t:
                state = lax.fori_loop(
                    0, t, lambda c, s, t=t, top=top: weigh(t, top, s, c * step, step), state
                )
            for part in own(t):
                state = weigh(t, top, state, *part)
        else:

            def both(c, carry, t=t, top=top, given=given):
                state, dq_t = carry
                state = weigh(t, top, state, c * half, half)
                return state, back(t + 1, given, dq_t, c * half, half)

            if t:
                state, dq_t = lax.fori_loop(0, 2 * t, both, (state, dq_t))
            for u in range(2):
                dq_t = back(t + 1, given, dq_t, t * step + u * half, half)
            for part in own(t):
                state = weigh(t, top, state, *part)
            for part in own(t + 1):
                dq_t = back(t + 1, given, dq_t, *part)
            finish_group(t + 1, given, dq_t)
        given = ready(*rows_t, state)
    dq_t = jnp.zeros((HDIM, tq), F32)
    for part in own(0):
        dq_t = back(0, given, dq_t, *part)
    finish_group(0, given, dq_t)

    def drain(c, carry):
        rows = dkv[rows_of(c * step, step), :].astype(BF16)
        out_ref[pl.ds(c * step, step), 0:width, :] = rows.reshape(step, width, 128)
        return carry

    lax.fori_loop(0, groups, drain, 0)


def attention(par, x, tq=768):
    n_keys = x.shape[0] * 2 * BLK
    whole = pl.BlockSpec(x.shape, lambda i: (0, 0, 0), pipeline_mode=pl.Buffered(1))
    return pl.pallas_call(
        functools.partial(attention_kernel, tq=tq),
        grid=(1,),
        out_shape=jax.ShapeDtypeStruct(x.shape, BF16),
        in_specs=[pl.BlockSpec(memory_space=pltpu.SMEM), whole],
        out_specs=whole,
        scratch_shapes=[
            pltpu.VMEM((128, n_keys), BF16),
            pltpu.VMEM((n_keys, tq), F32),
            pltpu.VMEM((n_keys - 2 * tq, tq), BF16),
            pltpu.VMEM((n_keys, tq), BF16),
            pltpu.VMEM((n_keys, 128), F32),
        ],
        compiler_params=pltpu.CompilerParams(vmem_limit_bytes=63 * 2**20),
        cost_estimate=cost(46),
    )(par, x)


def cost(micros):
    return pl.CostEstimate(flops=int(micros * 1.1e9), bytes_accessed=10**5, transcendentals=0)


def normalize(values):
    centred = values - jnp.mean(values, -1, keepdims=True)
    spread = jnp.mean(centred * centred, -1, keepdims=True)
    inv = lax.rsqrt(spread + EPS)
    return centred * inv, inv


def norm_back(normal, inv, e):
    return inv * (
        e
        - jnp.mean(e, -1, keepdims=True)
        - normal * jnp.mean(e * normal, -1, keepdims=True)
    )


def dot(a, b):
    return jnp.dot(a, b, preferred_element_type=F32)


def dot_t(a, b):
    return lax.dot_general(a, b, (((1,), (1,)), ((), ())), preferred_element_type=F32)


def t_dot(a, b):
    return lax.dot_general(a, b, (((0,), (0,)), ((), ())), preferred_element_type=F32)


AX = ("ctx", "wa")
YZ = [[2 * i + lo for i in range(16)] for lo in range(2)]
SMEM = pl.BlockSpec(memory_space=pltpu.SMEM)


def route(move):
    pairs = []
    for ctx in range(32):
        for wa in range(4):
            to_x, y, z, core = move(wa // 2 * 2 + ctx % 2, ctx // 8, ctx // 2 % 4, wa % 2)
            to_ctx, to_wa = y * 8 + z * 2 + to_x % 2, to_x // 2 * 2 + core
            pairs.append((ctx * 4 + wa, to_ctx * 4 + to_wa))
    return pairs


CORE = route(lambda x, y, z, c: (x, y, z, 1 - c))
CROSS = route(lambda x, y, z, c: (3 - x, y, z, c))
FAR = route(lambda x, y, z, c: (x ^ 2, y, z, c))
NEXT = route(lambda x, y, z, c: (x ^ 1, y, z, c))
ASIDE = route(lambda x, y, z, c: (x ^ 1, y, z, 1 - c))
TREE = (0, 1, 3, 2)


def send(value, pairs):
    return lax.ppermute(value, AX, pairs)


def pick(array, index, axis=0):
    return lax.dynamic_index_in_dim(array, index, axis, keepdims=False)


def after(value, *first):
    return lax.optimization_barrier((value, *first))[0]


def swap(pieces):
    return lax.all_to_all(pieces, "ctx", 0, 0, axis_index_groups=YZ, tiled=True)


def call(kernel, at, operands, outs, micros, scratch=()):
    def whole(a):
        return pl.BlockSpec(a.shape, lambda i: (0,) * len(a.shape), pipeline_mode=pl.Buffered(1))

    return pl.pallas_call(
        kernel,
        grid=(1,),
        out_shape=tuple(outs),
        in_specs=[SMEM] + [whole(a) for a in operands],
        out_specs=tuple(whole(a) for a in outs),
        scratch_shapes=list(scratch),
        compiler_params=pltpu.CompilerParams(vmem_limit_bytes=63 * 2**20),
        cost_estimate=cost(micros),
    )(at, *operands)


def struct(shape, dtype=BF16):
    return jax.ShapeDtypeStruct(shape, dtype)


def pack_kernel(at_ref, mix_ref, up_ref, dense_ref, small_ref, own, mix_cross, up_cross):
    for k, (mix_out, up_out) in enumerate(((own.at[0:256], own.at[256:512]), (mix_cross, up_cross))):
        q = at_ref[0] if k == 0 else 3 - at_ref[0]
        for j in range(3):
            cols = pl.ds(pl.multiple_of(q * 256 + j * 1024, 256), 256)
            mix_out[0:256, 256 * j : 256 * j + 256] = mix_ref[:, cols]
        if k == 0:
            mix_out[0:16, 768:1024] = small_ref[...]
            mix_out[16:256, 768:1024] = jnp.zeros((240, 256), BF16)
        else:
            mix_out[256:272, 0:256] = small_ref[...]
            mix_out[256:272, 256:768] = jnp.zeros((16, 512), BF16)
        up_out[...] = up_ref[:, pl.ds(pl.multiple_of(q * 1024, 1024), 1024)]
    own[512:768, :] = dense_ref[...]


def tables_kernel(at_ref, tables):
    shape = (BLK, 128)
    feature = lax.broadcasted_iota(jnp.int32, shape, 1) % HDIM
    exponent = (feature % 8).astype(F32) * (2.0 / ROT)
    inverse = jnp.exp(exponent * -math.log(10000.0))
    for block in range(2):
        spot = at_ref[4] * (2 * BLK) + block * BLK + lax.broadcasted_iota(jnp.int32, shape, 0)
        angle = spot.astype(F32) * inverse
        sine = jnp.sin(angle)
        tables[0, block] = jnp.where(feature < ROT, jnp.cos(angle), 1.0)
        tables[1, block] = jnp.where(feature < ROT // 2, -sine, 0.0)
        tables[2, block] = jnp.where((feature >= ROT // 2) & (feature < ROT), sine, 0.0)


def turn_lanes(pair, cos, sin_up, sin_down):
    return pair * cos + pltpu.roll(pair, 120, 1) * sin_up + pltpu.roll(pair, 8, 1) * sin_down


def project_kernel(at_ref, *refs):
    tokens, tail, mixes = refs[0:4], refs[4], refs[5:9]
    tables = refs[9]
    sent, vec_out, mix_out, dense_out = refs[10:14]
    x, core = at_ref[0], at_ref[1]
    hi, lo = x // 2, x % 2
    quarters = (2 * hi + core, 2 * (1 - hi) + core, 2 * hi + 1 - core, 2 * (1 - hi) + 1 - core)
    for w, piece in zip(quarters, mixes):
        cols = pl.ds(pl.multiple_of(w * 256, 256), 256)
        mix_out[cols, :] = piece[0:256, 0:768]
        if piece.shape[0] == 272:
            vec_out[0:16, cols] = piece[256:272, 0:256].astype(F32)
        else:
            vec_out[0:16, cols] = piece[0:16, 768:1024].astype(F32)

    @pl.when(core == lo)
    def _():
        dense_out[...] = mixes[0][512:768, :]

    @pl.when(core != lo)
    def _():
        dense_out[...] = mixes[2][512:768, :]

    for j in range(3):
        n = 4 * j + x
        row = vec_out[6:9, pl.ds(pl.multiple_of((n // 3) * 256, 256), 256)]
        keep = lax.broadcasted_iota(jnp.int32, (3, 256), 0) == n % 3
        vec_out[16:17, 256 * j : 256 * j + 256] = jnp.sum(
            jnp.where(keep, row, 0.0), 0, keepdims=True
        )
    for j in range(4):
        vec_out[17:18, 256 * j : 256 * j + 256] = vec_out[
            9 + j : 10 + j, pl.ds(pl.multiple_of(x * 256, 256), 256)
        ]
    gain1, shift1 = vec_out[0:1, :], vec_out[1:2, :]
    bias = vec_out[16:17, 0:768]
    lane = lax.broadcasted_iota(jnp.int32, (BLK, 128), 1)
    left = lane < HDIM
    for j in range(4):
        chip = lax.bitwise_xor(x, TREE[j])
        to_hi, to_lo = chip // 2, chip % 2
        normal, _ = normalize(tokens[j][0:BLK, :].astype(F32))
        low1 = (normal * gain1 + shift1).astype(BF16)
        grad = tokens[j][BLK : 2 * BLK, :]
        if j == 3:
            grad = jnp.concatenate([grad, tail[...]], 0)
        mixed = dot(low1, mix_out[...]) + bias
        d_merged = dot_t(grad, dense_out[...])
        cos, sin_up, sin_down = tables[0, to_lo], tables[1, to_lo], tables[2, to_lo]
        for h in range(2):
            cols = slice(128 * h, 128 * h + 128)
            q = turn_lanes(mixed[:, 0:256][:, cols], cos, sin_up, sin_down)
            k = turn_lanes(mixed[:, 256:512][:, cols], cos, sin_up, sin_down)
            v = mixed[:, 512:768][:, cols]
            dm = d_merged[:, cols]
            for side in range(2):
                if side == 0:
                    kv = jnp.where(left, k, pltpu.roll(v, 64, 1)).astype(BF16)
                    qd = jnp.where(left, q, pltpu.roll(dm, 64, 1)).astype(BF16)
                else:
                    kv = jnp.where(left, pltpu.roll(k, 64, 1), v).astype(BF16)
                    qd = jnp.where(left, pltpu.roll(q, 64, 1), dm).astype(BF16)
                i = 2 * h + side
                for half in range(2):
                    at = pl.ds(pl.multiple_of(to_lo * BLK, BLK), BLK)
                    sent[i, to_hi, half, at, :] = kv
                    at = pl.ds(pl.multiple_of(2 * BLK + to_lo * HALF, HALF), HALF)
                    sent[i, to_hi, half, at, :] = qd[HALF * half : HALF * half + HALF]


def project(at, tokens, mixes, tables):
    outs = (struct((4, 2, 2, 3 * BLK, 128)), struct((24, D), F32))
    scratch = [pltpu.VMEM((D, 768), BF16), pltpu.VMEM((256, D), BF16)]
    return call(project_kernel, at, (*tokens, *mixes, tables), outs, 0.1, scratch)


def mlp_kernel(at_ref, *refs):
    tokens, tail, refs = refs[0:4], refs[4], refs[1:]
    vec, ups, downs, mixes = refs[4], refs[5:9], refs[9:11], refs[11:13]
    normal_out, norm1_t, g_out, d_norm2, given, kept = refs[13:19]
    feed_sent, feed_own, sums, mix = refs[19:22], *refs[22:25]
    norm1, norm2, norm2_t, hidden, hidden_t, d_pre, up, down = refs[25:33]
    x, core = at_ref[0], at_ref[1]
    hi, lo = x // 2, x % 2
    quarters = (2 * hi + core, 2 * (1 - hi) + core, 2 * hi + 1 - core, 2 * (1 - hi) + 1 - core)
    for w, piece in zip(quarters, ups):
        rows = slice(256, 512) if piece.shape[0] > 256 else slice(0, 256)
        at = pl.ds(pl.multiple_of(w * 256, 256), 256)
        up[at, :] = piece[rows, :]
        if piece.shape[0] > 256:
            mix[at, :] = piece[0:256, 0:768]
    for w, piece in zip((quarters[1], quarters[3]), mixes):
        mix[pl.ds(pl.multiple_of(w * 256, 256), 256), :] = piece[0:256, :]

    @pl.when(core == lo)
    def _():
        down[...] = downs[0][...]

    @pl.when(core != lo)
    def _():
        down[...] = downs[1][...]

    for j in range(4):
        rows = slice(BLK * j, BLK * j + BLK)
        normal, _ = normalize(tokens[j][0:BLK, :].astype(F32))
        normal_out[rows, :] = normal.astype(BF16)
        norm1[rows, :] = (normal * vec[0:1, :] + vec[1:2, :]).astype(BF16)
        norm2[rows, :] = (normal * vec[2:3, :] + vec[3:4, :]).astype(BF16)
        grad = tokens[j][BLK : 2 * BLK, :]
        if j == 3:
            grad = jnp.concatenate([grad, tail[...]], 0)
        g_out[rows, :] = grad
    for k in range(4):
        cols = slice(256 * k, 256 * k + 256)
        pre = dot(norm2[...], up[:, cols]) + vec[17:18, cols]
        below = 0.5 + 0.5 * lax.erf(pre * 0.5**0.5)
        hidden[:, cols] = (pre * below).astype(BF16)
        bell = jnp.exp(-0.5 * pre * pre) * (0.5 / math.pi) ** 0.5
        dp = (dot_t(g_out[...], down[cols, :]) * (below + pre * bell)).astype(BF16)
        d_pre[:, cols] = dp
        sums[:, cols] = jnp.sum(dp.astype(F32), 0, keepdims=True)
    d_norm2[...] = dot_t(d_pre[...], up[...]).astype(BF16)
    for j in range(4):
        feed = dot(hidden[BLK * j : BLK * j + BLK, :], down[...])
        if j == 0:
            feed_own[...] = feed
        else:
            feed_sent[j - 1][...] = feed.astype(BF16)
    for k in range(8):
        at = slice(128 * k, 128 * k + 128)
        norm1_t[at, :] = norm1[:, at].T
        norm2_t[at, :] = norm2[:, at].T
        hidden_t[at, :] = hidden[:, at].T
    for c, out in ((1 - core, given), (core, kept)):
        for w in range(2):
            rows = pl.ds(pl.multiple_of(512 * w + 256 * c, 256), 256)
            part = dot(norm2_t[rows, :], d_pre[...])
            out[:, 16 * w : 16 * w + 16, :] = part.reshape(16, 16, 1024).astype(out.dtype)
        part = dot(hidden_t[pl.ds(pl.multiple_of(512 * c, 512), 512), :], g_out[...])
        out[:, 32:64, :] = part.reshape(16, 32, 1024).astype(out.dtype)


def feed_forward(at, *operands):
    outs = (
        struct((768, D)),
        struct((D, 768)),
        struct((768, D)),
        struct((768, D)),
        struct((16, 64, 1024)),
        struct((16, 64, 1024)),
        struct((BLK, D)),
        struct((BLK, D)),
        struct((BLK, D)),
        struct((BLK, D), F32),
        struct((1, 1024), F32),
        struct((D, 768)),
    )
    rows, columns = pltpu.VMEM((768, D), BF16), pltpu.VMEM((D, 768), BF16)
    square = pltpu.VMEM((D, 1024), BF16)
    scratch = (rows, rows, columns, rows, columns, rows, square, square)
    return call(mlp_kernel, at, operands, outs, 0.1, scratch)


def add_kernel(at_ref, a, b, out):
    out[...] = (a[...].astype(F32) + b[...].astype(F32)).astype(out.dtype)


def add(at, a, b):
    return call(add_kernel, at, (a, b), (struct(a.shape),), 0.1)[0]


def unpack_kernel(at_ref, back, tables, norm1_t, g_ref, d_mixed, merged, given, kept):
    core = at_ref[1]
    lane = lax.broadcasted_iota(jnp.int32, (BLK, 128), 1)
    left = lane < HDIM
    for j in range(4):
        if True:
            chip = lax.bitwise_xor(at_ref[0], TREE[j])
            hi, lo = chip // 2, chip % 2
            cos, sin_up, sin_down = tables[0, lo], tables[1, lo], tables[2, lo]
            rows = slice(j * BLK, j * BLK + BLK)
            for h in range(2):
                kv, qo = [], []
                for i in (2 * h, 2 * h + 1):
                    at = pl.ds(pl.multiple_of(lo * BLK, BLK), BLK)
                    kv.append(back[i, hi, 0, at, :].astype(F32) + back[i, hi, 1, at, :].astype(F32))
                    at = pl.ds(pl.multiple_of(2 * BLK + lo * HALF, HALF), HALF)
                    halves = [back[i, hi, s, at, :] for s in range(2)]
                    qo.append(jnp.concatenate(halves, 0).astype(F32))
                dq = jnp.where(left, qo[0], pltpu.roll(qo[1], 64, 1))
                out = jnp.where(left, pltpu.roll(qo[0], 64, 1), qo[1])
                dk = jnp.where(left, kv[0], pltpu.roll(kv[1], 64, 1))
                dv = jnp.where(left, pltpu.roll(kv[0], 64, 1), kv[1])
                dq = turn_lanes(dq, cos, -sin_up, -sin_down)
                dk = turn_lanes(dk, cos, -sin_up, -sin_down)
                for k, value in enumerate((dq, dk, dv)):
                    at = 256 * k + 128 * h
                    d_mixed[rows, at : at + 128] = value.astype(BF16)
                merged[rows, 128 * h : 128 * h + 128] = out.astype(BF16)
    merged_t = merged[...].astype(F32).T.astype(BF16)
    dense = dot(merged_t, g_ref[...])
    for c, out in ((1 - core, given), (core, kept)):
        for hi in range(2):
            rows = pl.ds(pl.multiple_of(512 * hi + 256 * c, 256), 256)
            part = dot(norm1_t[rows, :], d_mixed[...])
            out[:, 16 * hi : 16 * hi + 16, 0:768] = part.reshape(16, 16, 768).astype(out.dtype)
        half = jnp.where(c == 0, dense[0:128], dense[128:256]).astype(out.dtype)
        for i in range(4):
            for j in range(4):
                out[4 * i + j, :, 768:1024] = half[32 * i : 32 * i + 32, 256 * j : 256 * j + 256]


def unpack(at, *operands):
    outs = (
        struct((768, 768)),
        struct((768, 256)),
        struct((16, 32, 1024)),
        struct((16, 32, 1024)),
    )
    return call(unpack_kernel, at, operands, outs, 100)


def finish_kernel(
    at_ref, d_mixed, merged, mix, d_norm2, normal, g_own, up_sum, vec, *refs
):
    parts, e_own, merged_own, sums = refs[0:3], *refs[3:6]
    gain1, gain2 = vec[0:1, :], vec[2:3, :]
    totals = [jnp.zeros((1, D), F32) for _ in range(4)]
    for j in range(4):
        rows = slice(j * BLK, j * BLK + BLK)
        d1 = dot_t(d_mixed[rows, :], mix[...])
        d2 = d_norm2[rows, :].astype(F32)
        n = normal[rows, :].astype(F32)
        e = gain1 * d1 + gain2 * d2
        if j == 0:
            e_own[...] = e
            merged_own[...] = merged[rows, :]
        else:
            parts[j - 1][0:BLK, :] = e.astype(BF16)
            heads = merged[rows, :]
            for k in range(4):
                cols = slice(256 * k, 256 * k + 256)
                parts[j - 1][BLK : BLK + 48, cols] = heads[48 * k : 48 * k + 48]
        for k, value in enumerate((d1 * n, d1, d2 * n, d2)):
            totals[k] = totals[k] + jnp.sum(value, 0, keepdims=True)
    for k in range(4):
        sums[k : k + 1, :] = totals[k].astype(BF16)
    sums[4:5, :] = jnp.sum(g_own[...].astype(F32), 0, keepdims=True).astype(BF16)
    sums[5:6, :] = jnp.zeros((1, D), BF16)
    sums[5:6, 0:768] = jnp.sum(d_mixed[...].astype(F32), 0, keepdims=True).astype(BF16)
    sums[6:7, :] = up_sum[...].astype(BF16)
    sums[7:8, :] = jnp.zeros((1, D), BF16)


def finish(at, *operands):
    outs = (
        struct((BLK + 48, D)),
        struct((BLK + 48, D)),
        struct((BLK + 48, D)),
        struct((BLK, D), F32),
        struct((BLK, 256)),
        struct((8, D)),
    )
    return call(finish_kernel, at, operands, outs, 0.1)


def tokens_kernel(at_ref, x_ref, g_ref, *refs):
    e_own, merged_own, feed_own = refs[0:3]
    late, feeds = refs[3:6], refs[6:9]
    dense, vec, out, grad_in = refs[9:13]
    x = at_ref[0]
    tokens = x_ref[...].astype(F32)
    total = tokens + vec[4:5, :] + vec[5:6, :] + feed_own[...]
    total = total + dot(merged_own[...], dense[x])
    e = e_own[...]
    for j in range(3):
        total = total + feeds[j][...].astype(F32)
        heads = jnp.concatenate(
            [late[j][BLK : BLK + 48, 256 * k : 256 * k + 256] for k in range(4)], 0
        )
        total = total + dot(heads, dense[lax.bitwise_xor(x, TREE[j + 1])])
        e = e + late[j][0:BLK, :].astype(F32)
    out[...] = total.astype(BF16)
    normal, inv = normalize(tokens)
    grad_in[...] = (g_ref[...].astype(F32) + norm_back(normal, inv, e)).astype(BF16)


def own_tokens(at, *operands):
    return call(tokens_kernel, at, operands, (struct((BLK, D)),) * 2, 0.1)


def join_kernel(at_ref, own, beside, across, far, sibling, aside, out, scratch):
    hi, lo, core = at_ref[0] // 2, at_ref[0] % 2, at_ref[1]
    rows = pl.ds(pl.multiple_of(hi * 16, 16), 16)
    ring = (own, beside, across, far)
    ff = own.shape[0] == 64
    if ff:
        box, places = (slice(32, 64), slice(0, 1024)), ((64, 0), (96, 0))
        width = 1024
    else:
        box, places = (slice(0, 32), slice(768, 1024)), ((0, 768), (32, 768))
        width = 768
    for j in range(4):
        value = ring[j][rows, 0:width]
        for i in range(16):
            if i < out.shape[0]:
                out[i, 16 * j : 16 * j + 16, 0:width] = value
    for (row, column), near, off in zip(places, (own, sibling), (beside, aside)):
        value = jnp.where(core == lo, near[box], off[box])
        for i in range(out.shape[0]):
            out[i, row : row + 32, column : column + value.shape[1]] = value
    if not ff:
        quarter = 2 * hi + core
        chips = [r[32:40, :].astype(F32) for r in ring]
        scratch[0:5, :] = sum(c[0:5] for c in chips)
        for j in range(4):
            chip = lax.bitwise_xor(at_ref[0], TREE[j])
            scratch[pl.ds(8 + chip, 1), :] = chips[j][5:6]
            scratch[pl.ds(12 + chip, 1), :] = chips[j][6:7]
        cols = pl.ds(pl.multiple_of(quarter * 256, 256), 256)
        parts = [scratch[k : k + 1, cols] for k in range(5)]
        for k in range(3):
            n = 3 * quarter + k
            cols = pl.ds(pl.multiple_of(n // 4 * 256, 256), 256)
            parts.append(scratch[pl.ds(8 + n % 4, 1), cols])
        vec = [jnp.concatenate(parts[0:4], 1), jnp.concatenate(parts[4:8], 1)]
        vec += [scratch[pl.ds(12 + quarter, 1), :], jnp.zeros((5, 1024), F32)]
        vec = jnp.concatenate(vec, 0).astype(BF16)
        for i in range(16):
            out[i, 64:72, :] = vec


def join(at, own, count):
    parts = [send(own, p) for p in (NEXT, CROSS, FAR, CORE, ASIDE)]
    rows = 128 if own.shape[0] == 64 else 72
    scratch = [pltpu.VMEM((16, 1024), F32)]
    return call(join_kernel, at, (own, *parts), (struct((count, rows, 1024)),), 0.1, scratch)[0]


def place_ff_kernel(at_ref, sums, up_out, down_out):
    x, core = at_ref[0], at_ref[1]
    for j in range(4):
        cols = pl.ds(pl.multiple_of(lax.bitwise_xor(x, TREE[j]) * 1024, 1024), 1024)
        up_out[:, cols] = sums[:, 16 * j : 16 * j + 16, :].reshape(256, 1024).astype(F32)
    for side, at in ((core, 64), (1 - core, 96)):
        rows = pl.ds(pl.multiple_of(side * 512, 512), 512)
        down_out[rows, :] = sums[:, at : at + 32, :].reshape(512, 1024).astype(F32)


def place_attn_kernel(at_ref, sums, mix_out, dense_out, *vec_outs):
    x, core = at_ref[0], at_ref[1]
    for j in range(4):
        chip = lax.bitwise_xor(x, TREE[j])
        for k in range(3):
            cols = pl.ds(pl.multiple_of(k * 1024 + chip * 256, 256), 256)
            part = sums[:, 16 * j : 16 * j + 16, 256 * k : 256 * k + 256]
            mix_out[:, cols] = part.reshape(256, 256).astype(F32)
    for side, at in ((core, 0), (1 - core, 32)):
        for i in range(4):
            rows = pl.ds(pl.multiple_of(side * 128 + i * 32, 32), 32)
            for j in range(4):
                part = sums[4 * i + j, at : at + 32, 768:1024]
                dense_out[rows, 256 * j : 256 * j + 256] = part.astype(F32)
    total = jnp.zeros((8, 1024), F32)
    for i in range(16):
        total = total + sums[i, 64:72, :].astype(F32)
    for k in range(5):
        vec_outs[k][...] = total[k // 4, 256 * (k % 4) : 256 * (k % 4) + 256]
    vec_outs[5][...] = total[1, 0:256]
    vec_outs[6][...] = total[1, 256:1024]
    vec_outs[7][...] = total[2, :]


def shards(
    inputs,
    first_gain,
    first_bias,
    second_gain,
    second_bias,
    mix_weight,
    mix_bias,
    dense_weight,
    dense_bias,
    up_weight,
    up_bias,
    down_weight,
    down_bias,
    grad_out,
):
    ctx, wa = lax.axis_index("ctx"), lax.axis_index("wa")
    lo, yz, hi, core = ctx % 2, ctx // 2, wa // 2, wa % 2
    x = 2 * hi + lo
    at = jnp.stack([x, core, yz // 4, yz % 4, yz])

    both = jnp.concatenate([inputs[0], grad_out[0]], 0)
    beside, across = send(both, NEXT), send(both, CROSS)
    far = send(after(across[:256], beside), NEXT)
    tail = send(after(beside[256:], across), CROSS)
    tokens = (both, beside, across, far, tail)
    small, filled = 0, 0
    for v in (
        first_gain,
        first_bias,
        second_gain,
        second_bias,
        dense_bias,
        down_bias,
        mix_bias,
        up_bias,
    ):
        rows = v.shape[0] // 256
        small = small + jnp.pad(v.reshape(rows, 256), ((filled, 16 - filled - rows), (0, 0)))
        filled += rows
    tables = call(tables_kernel, at, (), (struct((3, 2, BLK, 128), F32),), 0.1)[0]
    own, mix_cross, up_cross = call(
        pack_kernel,
        at,
        (mix_weight, up_weight, dense_weight, after(small, tables)),
        (struct((768, 1024)), struct((272, 768)), struct((256, 1024))),
        0.1,
    )
    mix_got = send(after(mix_cross, beside, across), CROSS)
    other = send(own, CORE)
    mix_other_got = send(mix_got, CORE)
    up_got = send(after(up_cross, across, mix_got), CROSS)
    up_other_got = send(up_got, CORE)
    down_other = send(after(down_weight, across), CORE)

    sent, vec = project(at, tokens, (own, mix_got, other, mix_other_got), tables)
    held = swap(sent.reshape(16, 3 * BLK, 128))

    up_other_got = send(after(up_got, sent), CORE)
    normal, norm1_t, token_g, d_norm2, given, kept, *feed_sent, feed_own, up_sum, mix = feed_forward(
        at,
        *tokens,
        vec,
        own,
        up_got,
        other,
        up_other_got,
        down_weight,
        down_other,
        mix_got,
        mix_other_got,
    )
    ff_sums = add(at, kept, send(given, CORE))
    ff_mine = swap(after(ff_sums, held))
    back = attention((yz % 2).reshape(1), after(held, ff_sums))
    ff_mine = jnp.sum(after(ff_mine, back).astype(F32), 0).astype(BF16)
    ff_all = join(at, ff_mine, 1)[0]
    ff_all = lax.all_gather(ff_all, "ctx", axis=0, axis_index_groups=YZ, tiled=False)

    feeds = [send(feed_sent[j], (NEXT, CROSS, FAR)[j]) for j in range(3)]
    dense_got = send(after(dense_weight, up_got), CROSS)
    back = swap(after(back, dense_got, *feeds))
    dense_other_got = send(after(dense_got, ff_mine), CORE)
    near = jnp.where(
        core == 0, jnp.stack([dense_weight, other[512:]]), jnp.stack([other[512:], dense_weight])
    )
    away = jnp.where(
        core == 0,
        jnp.stack([dense_got, dense_other_got]),
        jnp.stack([dense_other_got, dense_got]),
    )
    dense_all = jnp.where(hi == 0, jnp.concatenate([near, away]), jnp.concatenate([away, near]))
    back = after(back, dense_all)

    d_mixed, merged, given, kept = unpack(
        at, back.reshape(4, 2, 2, 3 * BLK, 128), tables, norm1_t, token_g
    )
    attn_sums = add(at, kept, send(given, CORE))
    attn_mine = swap(attn_sums)
    *parts, e_own, merged_own, vectors = finish(
        at, after(d_mixed, attn_sums), merged, mix, d_norm2, normal, grad_out[0], up_sum, vec
    )
    vectors = add(at, vectors, send(vectors, CORE))
    late = [send(parts[j], (NEXT, CROSS, FAR)[j]) for j in range(3)]
    attn_mine = jnp.sum(attn_mine.astype(F32), 0).astype(BF16)
    gathered = join(at, jnp.concatenate([attn_mine, vectors], 0), 16)
    gathered = swap(gathered)
    grad_up, grad_down = call(
        place_ff_kernel, at, (ff_all,), (struct((256, FF), F32), struct((1024, D), F32)), 0.1
    )
    output, grad_in = own_tokens(
        at, after(inputs[0], grad_up), grad_out[0], e_own, merged_own, feed_own, *late, *feeds, dense_all, vec
    )
    gathered = after(gathered, output, grad_up)
    row = struct((256,), F32)
    grad_mix, grad_dense, *rest = call(
        place_attn_kernel,
        at,
        (gathered,),
        (struct((256, 3 * D), F32), struct((256, D), F32))
        + (row,) * 6
        + (struct((768,), F32), struct((1024,), F32)),
        0.1,
    )
    return (
        output[None],
        grad_in[None],
        rest[0],
        rest[1],
        rest[2],
        rest[3],
        grad_mix,
        rest[6],
        grad_dense,
        rest[4],
        grad_up,
        rest[7],
        grad_down,
        rest[5],
    )


def solution(mesh):
    rows, vec, tokens = P("wa", None), P("wa"), P("wa", "ctx", None)
    return jax.shard_map(
        shards,
        mesh=mesh,
        in_specs=(tokens, vec, vec, vec, vec, rows, vec, rows, vec, rows, vec, rows, vec, tokens),
        out_specs=(
            tokens,
            tokens,
            vec,
            vec,
            vec,
            vec,
            rows,
            vec,
            rows,
            vec,
            rows,
            vec,
            rows,
            vec,
        ),
        check_vma=False,
    )
```
